32 devices in a mesh: seq: 8 (over y, x, core), lvl: 4 (over z).
Axes of the slice: x: 2, y: 2, z: 4, core: 2. Of those that a mesh axis runs over, the one named last changes fastest.
Arguments:
- queries: bfloat16 [16384, 1024], P(('seq', 'lvl')), may hold values from -24 to 24
- keys: bfloat16 [16384, 1024], P(('seq', 'lvl')), may hold values from -24 to 24
- values: bfloat16 [16384, 1024], P(('seq', 'lvl')), may hold values from -6 to 6
- grad_out: bfloat16 [16384, 1024], P(('seq', 'lvl')), may hold values from -6 to 6
- mid_offset: int32 [8], replicated, may hold values from 0 to 3
- far_offset: int32 [8], replicated, may hold values from 0 to 31
Outputs:
- grad_queries: bfloat16 [16384, 1024], P(('seq', 'lvl'))
- grad_keys: bfloat16 [16384, 1024], P(('seq', 'lvl'))
- grad_values: bfloat16 [16384, 1024], P(('seq', 'lvl'))
The draws below stay inside these ranges and needn't reach their ends.
All inputs are finite; a program needn't handle non-finite values.
Results may differ from the reference program's by a relative error of at most 0.0087.
Values may be sent and summed in bfloat16 or wider, within the bound.
No kernel may reach another device: no remote copies, remote signals or barrier semaphores. Data moves between devices by JAX's collectives and lax.ppermute only.
A program may use at most 128 MiB of HBM per device.

```python
import jax
import jax.numpy as jnp
from jax import lax

H = 8
DH = 128
TOK = 512
SEQ_LEN = 16384
R_MID = 4
R_FAR = 32


def drawn_pair(key):
    base_key = jax.random.fold_in(key, 4021)
    subkeys = jax.random.split(base_key, 2)
    shape = (SEQ_LEN, H, DH)
    query_rows = jnp.clip(jax.random.normal(subkeys[0], shape, jnp.float32), -6.0, 6.0)
    key_rows = jnp.clip(jax.random.normal(subkeys[1], shape, jnp.float32), -6.0, 6.0)
    query_rows = jnp.clip(query_rows, -24.0, 24.0).reshape(SEQ_LEN, H * DH)
    key_rows = jnp.clip(key_rows, -24.0, 24.0).reshape(SEQ_LEN, H * DH)
    return (query_rows.astype(jnp.bfloat16), key_rows.astype(jnp.bfloat16))


def draw_queries(key, part):
    return drawn_pair(key)[0]


def draw_keys(key, part):
    return drawn_pair(key)[1]


def set_ends(drawn, rng, least, largest):
    dims = drawn.shape
    place = [jax.random.randint(jax.random.fold_in(rng, axis), (), 0, dims[axis]) for axis in range(len(dims))]
    drawn = drawn.at[tuple(place)].set(least)
    longest = dims.index(max(dims))
    place[longest] = (place[longest] + 1) % dims[longest]
    return drawn.at[tuple(place)].set(largest)


def level_of(key, extent, cuts, smallest, top_value):
    def one(dim, parts):
        steps = jax.random.uniform(jax.random.fold_in(jax.random.fold_in(key, 6), dim), (parts,), jnp.float32, smallest / len(cuts), top_value / len(cuts))
        return jnp.repeat(jnp.exp(steps), extent[dim] // parts).reshape((-1,) + (1,) * (len(extent) - dim - 1))

    level = one(*cuts[0])
    for cut in cuts[1:]:
        level = level * one(*cut)
    return level


def centred(key, dims, scale, reach, cuts=(), held_as=jnp.bfloat16):
    entries = jax.random.normal(key, dims, jnp.float32) * scale
    if len(cuts) > 0:
        entries = level_of(key, dims, cuts, -0.22, 0.18) * entries
    return jnp.clip(entries, min=-reach, max=reach).astype(held_as)


def setup_inputs(seed: int = 0) -> dict:
    splits = jax.random.split(jax.random.key(seed), 7)
    return {
        "queries": draw_queries(jax.random.fold_in(splits[6], 71), 0),
        "keys": draw_keys(jax.random.fold_in(splits[6], 71), 0),
        "values": centred(splits[2], (SEQ_LEN, H * DH), 1.0, 6.0, ((0, 32),)),
        "grad_out": centred(splits[3], (SEQ_LEN, H * DH), 1.0, 6.0, ((0, 32),)),
        "mid_offset": set_ends(jax.random.randint(splits[4], (H,), 0, R_MID), jax.random.fold_in(splits[4], 1), 0, R_MID - 1).astype(jnp.int32),
        "far_offset": set_ends(jax.random.randint(splits[5], (H,), 0, R_FAR), jax.random.fold_in(splits[5], 1), 0, R_FAR - 1).astype(jnp.int32),
    }


def onehot_table(offset, stride):
    return (jnp.arange(stride)[:, None] == offset[None, :]).astype(jnp.float32)


def select_rows(source, offset, stride):
    if stride == 1:
        return source
    groups = source.shape[0] // stride
    onehot = onehot_table(offset, stride)
    if source.ndim == 3:
        shaped = source.reshape(groups, stride, source.shape[1], source.shape[2]).astype(jnp.float32)
        return jnp.einsum("nrhd,rh->nhd", shaped, onehot).astype(source.dtype)
    shaped = source.reshape(groups, stride, source.shape[1])
    return jnp.sum(shaped * onehot[None], axis=1)


def spread_rows(pieces, offset, stride):
    if stride == 1:
        return pieces
    onehot = onehot_table(offset, stride)
    whole_rows = pieces[:, None] * onehot[None, :, :, None]
    return whole_rows.reshape(pieces.shape[0] * stride, pieces.shape[1], pieces.shape[2])


def spread_stats(stat_rows, offset, stride):
    chosen = jnp.arange(stride)[:, None] == offset[None, :]
    whole_rows = jnp.where(chosen[None], stat_rows[:, None, :], -jnp.inf)
    return whole_rows.reshape(stat_rows.shape[0] * stride, stat_rows.shape[1])


def segment_scores(query_part, key_part):
    return jnp.einsum("qhd,khd->hqk", query_part.astype(jnp.float32), key_part.astype(jnp.float32)) * (DH ** -0.5)


def masked_logs(scores, allowed):
    peak_score = jnp.max(jnp.where(allowed[None], scores, -jnp.inf), axis=2)
    exp_total = jnp.sum(jnp.where(allowed[None], jnp.exp(scores - peak_score[:, :, None]), 0.0), axis=2)
    return (peak_score + jnp.log(exp_total)).T


def soft_weights(scores, allowed, log_part):
    return jnp.where(allowed[None], jnp.exp(scores - log_part.T[:, :, None]), 0.0)


def reference(queries, keys, values, grad_out, mid_offset, far_offset):
    shape = (SEQ_LEN, H, DH)
    query_rows = queries.reshape(shape)
    key_rows = keys.reshape(shape)
    value_rows = values.reshape(shape)
    grad_rows = grad_out.reshape(shape)
    levels = ((1, jnp.zeros((H,), jnp.int32)), (R_MID, mid_offset), (R_FAR, far_offset))
    allowed = jnp.arange(TOK)[None, :] <= jnp.arange(TOK)[:, None]

    def blocks(source, offset, stride):
        picked = select_rows(source, offset, stride)
        return picked.reshape((picked.shape[0] // TOK, TOK) + picked.shape[1:])

    def logs_block(block):
        return masked_logs(segment_scores(block[0], block[1]), allowed)

    def output_block(block):
        query_part, key_part, value_part, log_part = block
        soft = soft_weights(segment_scores(query_part, key_part), allowed, log_part)
        soft_cast = lax.optimization_barrier(soft.astype(jnp.bfloat16)).astype(jnp.float32)
        return jnp.einsum("hqk,khd->qhd", soft_cast, value_part.astype(jnp.float32))

    def grad_block(block):
        query_part, key_part, value_part, grad_part, log_part, delta_part = block
        soft = soft_weights(segment_scores(query_part, key_part), allowed, log_part)
        soft_cast = lax.optimization_barrier(soft.astype(jnp.bfloat16)).astype(jnp.float32)
        grad_weights = jnp.einsum("qhd,khd->hqk", grad_part.astype(jnp.float32), value_part.astype(jnp.float32))
        grad_scores = soft * (grad_weights - delta_part.T[:, :, None]) * (DH ** -0.5)
        grad_scores = lax.optimization_barrier(grad_scores.astype(jnp.bfloat16)).astype(jnp.float32)
        grad_query = jnp.einsum("hqk,khd->qhd", grad_scores, key_part.astype(jnp.float32))
        grad_key = jnp.einsum("hqk,qhd->khd", grad_scores, query_part.astype(jnp.float32))
        grad_value = jnp.einsum("hqk,qhd->khd", soft_cast, grad_part.astype(jnp.float32))
        return grad_query, grad_key, grad_value

    log_total = None
    for stride, offset in levels:
        level_logs = lax.map(logs_block, (blocks(query_rows, offset, stride), blocks(key_rows, offset, stride)))
        spread = spread_stats(level_logs.reshape(-1, H), offset, stride)
        log_total = spread if log_total is None else jnp.logaddexp(log_total, spread)

    merged = jnp.zeros(shape, jnp.float32)
    for stride, offset in levels:
        outputs = lax.map(output_block, (blocks(query_rows, offset, stride), blocks(key_rows, offset, stride), blocks(value_rows, offset, stride), blocks(log_total, offset, stride)))
        merged = merged + spread_rows(outputs.reshape(-1, H, DH), offset, stride)
    delta_rows = jnp.sum(grad_rows.astype(jnp.float32) * merged, axis=2)

    grad_query = jnp.zeros(shape, jnp.float32)
    grad_key = jnp.zeros(shape, jnp.float32)
    grad_value = jnp.zeros(shape, jnp.float32)
    for stride, offset in levels:
        results = lax.map(grad_block, (blocks(query_rows, offset, stride), blocks(key_rows, offset, stride), blocks(value_rows, offset, stride), blocks(grad_rows, offset, stride), blocks(log_total, offset, stride), blocks(delta_rows, offset, stride)))
        grad_query = grad_query + spread_rows(results[0].reshape(-1, H, DH), offset, stride)
        grad_key = grad_key + spread_rows(results[1].reshape(-1, H, DH), offset, stride)
        grad_value = grad_value + spread_rows(results[2].reshape(-1, H, DH), offset, stride)
    flat = (SEQ_LEN, H * DH)
    return (grad_query.reshape(flat).astype(jnp.bfloat16), grad_key.reshape(flat).astype(jnp.bfloat16), grad_value.reshape(flat).astype(jnp.bfloat16))
```

```python
import functools

import jax
import jax.numpy as jnp
from jax import lax
from jax.experimental import pallas as pl
from jax.experimental.pallas import tpu as pltpu
from jax.sharding import PartitionSpec as P

F32 = jnp.float32
BF16 = jnp.bfloat16
LANES = 128
LOW = -1e30
VMEM_LIMIT = 48 * 1024 * 1024


def mm(a, b):
    return lax.dot_general(a, b, (((1,), (0,)), ((), ())), preferred_element_type=F32)


def mm_t(a, b):
    return lax.dot_general(a, b, (((1,), (1,)), ((), ())), preferred_element_type=F32)


def t_mm(a, b):
    return lax.dot_general(a, b, (((0,), (0,)), ((), ())), preferred_element_type=F32)


def exact(a, b):
    return lax.dot_general(
        a, b, (((1,), (0,)), ((), ())), preferred_element_type=F32, precision=lax.Precision.HIGHEST
    )


def iota(shape, axis):
    return lax.broadcasted_iota(jnp.int32, shape, axis)


def params():
    return pltpu.CompilerParams(
        vmem_limit_bytes=VMEM_LIMIT, dimension_semantics=("arbitrary",)
    )


def smem():
    return pl.BlockSpec(memory_space=pltpu.SMEM)


def columns(rows, width):
    return pl.BlockSpec((rows, width), lambda h: (0, h))


def fixed(shape):
    return pl.BlockSpec(shape, lambda h: (0,) * len(shape))


def pick_lane(ref, head):
    block = ref[...]
    return jnp.sum(jnp.where(iota(block.shape, 1) == head, block, 0.0), axis=1, keepdims=True)


def put_lane(ref, rows, head, value):
    block = ref[rows, :]
    ref[rows, :] = jnp.where(iota(block.shape, 1) == head, value, block)


def select_kernel(place, mid_off, far_off, q, k, v, g, kv, qg, far, *pays):
    head = pl.program_id(0)
    level = place[1]
    rows = q.shape[0]
    whole = jnp.concatenate([k[...], v[...], q[...], g[...]], axis=1)

    def picked(count, offset):
        stride = rows // count
        table = iota((count, rows), 1) == iota((count, rows), 0) * stride + offset
        return mm(table.astype(BF16), whole).astype(BF16)

    mid = picked(kv.shape[0], mid_off[head])
    half = kv.shape[1]
    kv[...] = mid[:, :half]
    qg[...] = mid[:, half:]
    for step, pay in enumerate(pays, 1):
        upward = (level ^ step) > level

        @pl.when(upward)
        def _():
            pay[...] = mid[:, :half]

        @pl.when(jnp.logical_not(upward))
        def _():
            pay[...] = mid[:, half:]

    far[...] = picked(far.shape[0], far_off[head])


def near_stats_kernel(scale, parts, q, k, v, g, logs, dots):
    head = pl.program_id(0)

    @pl.when(head == 0)
    def _():
        logs[...] = jnp.zeros_like(logs)
        dots[...] = jnp.zeros_like(dots)

    size = q.shape[0] // parts
    for part in range(parts):
        rows = slice(part * size, (part + 1) * size)
        width = (part + 1) * size
        scores = mm_t(q[rows, :], k[:width, :]) * scale
        grads = mm_t(g[rows, :], v[:width, :])
        seen = iota((size, width), 1) <= iota((size, width), 0) + part * size
        log_part, dot_part = row_stats(jnp.where(seen, scores, LOW), grads)
        put_lane(logs, rows, head, log_part)
        put_lane(dots, rows, head, dot_part)


def row_stats(scores, grads):
    peak = jnp.max(scores, axis=1, keepdims=True)
    weights = jnp.exp(scores - peak)
    total = jnp.sum(weights, axis=1, keepdims=True)
    return peak + jnp.log(total), jnp.sum(weights * grads, axis=1, keepdims=True) / total


def choose(first, when_first, otherwise):
    return (first & when_first) | (jnp.logical_not(first) & otherwise)


def mid_mask(count, total, level, back):
    row, col = iota((count, total), 0), iota((count, total), 1)
    slot, rest = col // count, col % count
    other = slot ^ level
    if back:
        return choose(slot == 0, rest >= row, other > level)
    return choose(slot == 0, rest <= row, other < level)


def far_mask(count, total, block, level, ring, back):
    row, col = iota((count, total), 0), iota((count, total), 1)
    ring_slot, in_block = col // block, col % block
    slot, rest = in_block // count, in_block % count
    ring_other, other = ring_slot ^ ring, slot ^ level
    if back:
        own = choose(slot == 0, rest >= row, other > level)
        return choose(ring_slot == 0, own, ring_other > ring)
    own = choose(slot == 0, rest <= row, other < level)
    return choose(ring_slot == 0, own, ring_other < ring)


def stack(refs, first):
    blocks = [ref[:, first : first + LANES] for ref in refs]
    return blocks[0] if len(blocks) == 1 else jnp.concatenate(blocks, axis=0)


def repeat_table(rows, count):
    return (iota((rows, count), 0) // (rows // count) == iota((rows, count), 1)).astype(F32)


def gather_table(rows, count):
    return (iota((count, rows), 1) // (rows // count) == iota((count, rows), 0)).astype(F32)


def level_stats_kernel(scale, mids, fars, block, *refs):
    place, mid_lane, far_lane, kv, qg, far_own, near_logs, near_dots = refs[:8]
    mid_in = refs[8 : 8 + mids]
    far_in = refs[8 + mids : 8 + mids + fars]
    (log_all, dot_all, mid_log, mid_dot, far_log, far_dot, mid_row, far_row) = refs[8 + mids + fars :][:8]
    mlog, mdot, flog, fdot = refs[16 + mids + fars :]
    head = pl.program_id(0)
    ring, level = place[0], place[1]
    mid_count, far_count = kv.shape[0], far_own.shape[0]

    @pl.when(head == 0)
    def _():
        for ref in (mlog, mdot, flog, fdot):
            ref[...] = jnp.zeros_like(ref)

    keys = stack((kv,) + mid_in, 0)
    vals = stack((kv,) + mid_in, LANES)
    scores = mm_t(qg[:, :LANES], keys) * scale
    grads = mm_t(qg[:, LANES:], vals)
    seen = mid_mask(mid_count, keys.shape[0], level, False)
    log_part, dot_part = row_stats(jnp.where(seen, scores, LOW), grads)
    every = slice(None)
    put_lane(mlog, every, head, log_part)
    put_lane(mdot, every, head, dot_part)

    keys = stack(far_in, 0)
    vals = stack(far_in, LANES)
    scores = mm_t(far_own[:, 2 * LANES : 3 * LANES], keys) * scale
    grads = mm_t(far_own[:, 3 * LANES :], vals)
    seen = far_mask(far_count, keys.shape[0], block, level, ring, False)
    log_part, dot_part = row_stats(jnp.where(seen, scores, LOW), grads)
    put_lane(flog, every, head, log_part)
    put_lane(fdot, every, head, dot_part)

    @pl.when(head == pl.num_programs(0) - 1)
    def _():
        rows = near_logs.shape[0]
        row = iota((rows, LANES), 0)
        mid_here = row % (rows // mid_count) == mid_lane[...]
        far_here = row % (rows // far_count) == far_lane[...]
        mid_table, far_table = repeat_table(rows, mid_count), repeat_table(rows, far_count)
        near = near_logs[...]
        mid = jnp.where(mid_here, exact(mid_table, mlog[...]), LOW)
        far = jnp.where(far_here, exact(far_table, flog[...]), LOW)
        peak = jnp.maximum(near, jnp.maximum(mid, far))
        near, mid, far = jnp.exp(near - peak), jnp.exp(mid - peak), jnp.exp(far - peak)
        total = near + mid + far
        logs = peak + jnp.log(total)
        dots = (
            near * near_dots[...]
            + mid * exact(mid_table, mdot[...])
            + far * exact(far_table, fdot[...])
        ) / total
        log_all[...] = logs
        dot_all[...] = dots
        heads = mid_row.shape[0] // 2
        for here, count, outs, flat in (
            (mid_here, mid_count, (mid_log, mid_dot), mid_row),
            (far_here, far_count, (far_log, far_dot), far_row),
        ):
            table = gather_table(rows, count)
            for place_row, (source, out) in enumerate(zip((logs, dots), outs)):
                chosen = exact(table, jnp.where(here, source, 0.0))
                out[...] = chosen
                flat[place_row * heads : (place_row + 1) * heads, :] = chosen.T[:heads, :]


def near_grads_kernel(scale, parts, q, k, v, g, logs, dots, dq, dk, dv):
    head = pl.program_id(0)
    size = q.shape[0] // parts
    log_all, dot_all = pick_lane(logs, head), pick_lane(dots, head)
    for part in reversed(range(parts)):
        rows = slice(part * size, (part + 1) * size)
        width = (part + 1) * size
        scores = mm_t(q[rows, :], k[:width, :]) * scale
        grads = mm_t(g[rows, :], v[:width, :])
        seen = iota((size, width), 1) <= iota((size, width), 0) + part * size
        soft = jnp.exp(jnp.where(seen, scores - log_all[rows, :], LOW))
        slopes = (soft * (grads - dot_all[rows, :]) * scale).astype(BF16)
        dq[rows, :] = mm(slopes, k[:width, :])
        key_part = t_mm(slopes, q[rows, :])
        value_part = t_mm(soft.astype(BF16), g[rows, :])
        if part == parts - 1:
            dk[...] = key_part
            dv[...] = value_part
        else:
            dk[:width, :] += key_part
            dv[:width, :] += value_part


def spread(rows, offset, piece):
    count = piece.shape[0]
    table = (iota((rows, count), 0) == iota((rows, count), 1) * (rows // count) + offset).astype(BF16)
    high = piece.astype(BF16)
    low = (piece - high.astype(F32)).astype(BF16)
    return mm(table, high) + mm(table, low)


def query_grads_kernel(scale, mids, fars, block, *refs):
    place, mid_off, far_off, kv, qg, far_own, near = refs[:7]
    mid_log, mid_dot, far_log, far_dot = refs[7:11]
    mid_in = refs[11 : 11 + mids]
    far_in = refs[11 + mids : 11 + mids + fars]
    out = refs[-1]
    head = pl.program_id(0)
    ring, level = place[0], place[1]
    rows = out.shape[0]

    keys = stack((kv,) + mid_in, 0)
    vals = stack((kv,) + mid_in, LANES)
    scores = mm_t(qg[:, :LANES], keys) * scale
    grads = mm_t(qg[:, LANES:], vals)
    seen = mid_mask(kv.shape[0], keys.shape[0], level, False)
    soft = jnp.exp(jnp.where(seen, scores - pick_lane(mid_log, head), LOW))
    slopes = (soft * (grads - pick_lane(mid_dot, head)) * scale).astype(BF16)
    total = near[...] + spread(rows, mid_off[head], mm(slopes, keys))

    keys = stack(far_in, 0)
    vals = stack(far_in, LANES)
    scores = mm_t(far_own[:, 2 * LANES : 3 * LANES], keys) * scale
    grads = mm_t(far_own[:, 3 * LANES :], vals)
    seen = far_mask(far_own.shape[0], keys.shape[0], block, level, ring, False)
    soft = jnp.exp(jnp.where(seen, scores - pick_lane(far_log, head), LOW))
    slopes = (soft * (grads - pick_lane(far_dot, head)) * scale).astype(BF16)
    out[...] = (total + spread(rows, far_off[head], mm(slopes, keys))).astype(BF16)


def key_grads_kernel(scale, mids, fars, block, *refs):
    place, mid_off, far_off, kv, qg, far_own, near_dk, near_dv, mid_rows, far_rows = refs[:10]
    mid_in = refs[10 : 10 + mids]
    far_in = refs[10 + mids : 10 + mids + fars]
    out_k, out_v = refs[-2:]
    head = pl.program_id(0)
    ring, level = place[0], place[1]
    rows = out_k.shape[0]
    heads = mid_rows.shape[0] // 2

    def one(keys, vals, queries, cots, seen, stats):
        logs = stats[pl.ds(head, 1), :]
        dots = stats[pl.ds(head + heads, 1), :]
        scores = mm_t(keys, queries) * scale
        grads = mm_t(vals, cots)
        soft = jnp.exp(jnp.where(seen, scores - logs, LOW))
        slopes = (soft * (grads - dots) * scale).astype(BF16)
        return mm(slopes, queries), mm(soft.astype(BF16), cots)

    queries, cots = stack((qg,) + mid_in, 0), stack((qg,) + mid_in, LANES)
    seen = mid_mask(kv.shape[0], queries.shape[0], level, True)
    mid_k, mid_v = one(kv[:, :LANES], kv[:, LANES:], queries, cots, seen, mid_rows)
    queries, cots = stack(far_in, 0), stack(far_in, LANES)
    seen = far_mask(far_own.shape[0], queries.shape[0], block, level, ring, True)
    far_k, far_v = one(
        far_own[:, :LANES], far_own[:, LANES : 2 * LANES], queries, cots, seen, far_rows
    )
    out_k[...] = (
        near_dk[...] + spread(rows, mid_off[head], mid_k) + spread(rows, far_off[head], far_k)
    ).astype(BF16)
    out_v[...] = (
        near_dv[...] + spread(rows, mid_off[head], mid_v) + spread(rows, far_off[head], far_v)
    ).astype(BF16)


def ring_payload_kernel(place, kv_in, qg_in, *pays):
    ring = place[0]
    for step, pay in enumerate(pays, 1):
        upward = (ring ^ step) > ring

        @pl.when(upward)
        def _():
            pay[...] = kv_in[...]

        @pl.when(jnp.logical_not(upward))
        def _():
            pay[...] = qg_in[...]


def swap(array, axis, size, step):
    return lax.ppermute(array, axis, [(i, i ^ step) for i in range(size)])


def call(kernel, heads, ins, outs, scratch, cost):
    specs, arrays = zip(*ins)
    out_specs, out_shapes = zip(*outs)
    return pl.pallas_call(
        kernel,
        grid=(heads,),
        in_specs=list(specs),
        out_specs=list(out_specs),
        out_shape=list(out_shapes),
        scratch_shapes=scratch,
        compiler_params=params(),
        cost_estimate=pl.CostEstimate(flops=cost[0], bytes_accessed=cost[1], transcendentals=cost[2]),
    )(*arrays)


def local(queries, keys, values, grad_out, mid_offset, far_offset):
    rows, flat = queries.shape
    heads = mid_offset.shape[0]
    width = flat // heads
    scale = width ** (-0.5)
    levels, rings = lax.axis_size("lvl"), lax.axis_size("seq")
    mid_count, far_count = rows // levels, rows // (levels * rings)
    block = far_count * levels
    place = jnp.stack([lax.axis_index("seq"), lax.axis_index("lvl")]).astype(jnp.int32)
    mid_lane = jnp.tile(mid_offset, LANES // heads)[None, :]
    far_lane = jnp.tile(far_offset, LANES // heads)[None, :]
    shape = jax.ShapeDtypeStruct
    parts = 2
    tile = columns(rows, width)
    sources = [(tile, queries), (tile, keys), (tile, values), (tile, grad_out)]
    scalars = [(smem(), place), (smem(), mid_offset), (smem(), far_offset)]
    unit = rows * rows * width * 2 * heads

    kv, qg, far, *pays = call(
        select_kernel,
        heads,
        scalars + sources,
        [(columns(mid_count, 2 * width), shape((mid_count, 2 * flat), BF16))] * 2
        + [(columns(far_count, 4 * width), shape((far_count, 4 * flat), BF16))]
        + [(columns(mid_count, 2 * width), shape((mid_count, 2 * flat), BF16))] * (levels - 1),
        [],
        (unit, rows * flat * 8, 0),
    )
    far_level = [far] + [swap(far, "lvl", levels, step) for step in range(1, levels)]
    mid_in = [swap(pays[step - 1], "lvl", levels, step) for step in range(1, levels)]

    split = [piece.reshape(far_count, heads, 2, 2 * width) for piece in far_level]
    split = jnp.concatenate(split, axis=0)
    column_kv = split[:, :, 0].reshape(block, 2 * flat)
    column_qg = split[:, :, 1].reshape(block, 2 * flat)
    whole_column = columns(block, 2 * width)
    ring_pays = call(
        ring_payload_kernel,
        heads,
        scalars[:1] + [(whole_column, column_kv), (whole_column, column_qg)],
        [(whole_column, shape((block, 2 * flat), BF16))] * (rings - 1),
        [],
        (0, block * flat * 4 * (rings + 1), 0),
    )
    far_ring = [swap(ring_pays[step - 1], "seq", rings, step) for step in range(1, rings)]

    stat = shape((rows, LANES), F32)
    stat_spec = fixed((rows, LANES))
    near_logs, near_dots = call(
        functools.partial(near_stats_kernel, scale, parts),
        heads,
        sources,
        [(stat_spec, stat)] * 2,
        [],
        (2 * unit, rows * flat * 8, rows * rows * heads),
    )

    def far_list(own):
        pieces = [own] + far_ring
        if block % 16:
            pieces = [jnp.concatenate(pieces, axis=0)]
        return [(columns(piece.shape[0], 2 * width), piece) for piece in pieces]

    far_kv, far_qg = far_list(column_kv), far_list(column_qg)
    mid_spec = columns(mid_count, 2 * width)
    mid_list = [(mid_spec, piece) for piece in mid_in]
    own = [(mid_spec, kv), (mid_spec, qg), (columns(far_count, 4 * width), far)]
    mid_stat, far_stat = shape((mid_count, LANES), F32), shape((far_count, LANES), F32)
    counts = (len(mid_list), len(far_kv), block)
    log_all, dot_all, mid_log, mid_dot, far_log, far_dot, mid_row, far_row = call(
        functools.partial(level_stats_kernel, scale, *counts),
        heads,
        [scalars[0], (fixed((1, LANES)), mid_lane), (fixed((1, LANES)), far_lane)]
        + own
        + [(stat_spec, near_logs), (stat_spec, near_dots)]
        + mid_list
        + far_kv,
        [
            (stat_spec, stat),
            (stat_spec, stat),
            (fixed(mid_stat.shape), mid_stat),
            (fixed(mid_stat.shape), mid_stat),
            (fixed(far_stat.shape), far_stat),
            (fixed(far_stat.shape), far_stat),
            (fixed((2 * heads, mid_count)), shape((2 * heads, mid_count), F32)),
            (fixed((2 * heads, far_count)), shape((2 * heads, far_count), F32)),
        ],
        [pltpu.VMEM((mid_count, LANES), F32)] * 2 + [pltpu.VMEM((far_count, LANES), F32)] * 2,
        (unit, rows * flat * 16, rows * mid_count * heads),
    )

    both = jnp.concatenate([mid_row, far_row], axis=1)
    stat_in = [both] + [swap(both, "lvl", levels, step) for step in range(1, levels)]
    mid_rows = jnp.concatenate([piece[:, :mid_count] for piece in stat_in], axis=1)
    far_block = jnp.concatenate([piece[:, mid_count:] for piece in stat_in], axis=1)
    far_rows = jnp.concatenate(
        [far_block] + [swap(far_block, "seq", rings, step) for step in range(1, rings)], axis=1
    )

    grad_tile = shape((rows, flat), F32)
    near_dq, near_dk, near_dv = call(
        functools.partial(near_grads_kernel, scale, parts),
        heads,
        sources + [(stat_spec, log_all), (stat_spec, dot_all)],
        [(tile, grad_tile)] * 3,
        [],
        (5 * unit, rows * flat * 20, rows * rows * heads),
    )
    out = shape((rows, flat), BF16)
    (grad_query,) = call(
        functools.partial(query_grads_kernel, scale, *counts),
        heads,
        scalars
        + own
        + [(tile, near_dq)]
        + [(fixed(mid_stat.shape), mid_log), (fixed(mid_stat.shape), mid_dot)]
        + [(fixed(far_stat.shape), far_log), (fixed(far_stat.shape), far_dot)]
        + mid_list
        + far_kv,
        [(tile, out)],
        [],
        (unit, rows * flat * 16, rows * mid_count * heads),
    )
    row_spec = fixed((2 * heads, rows))
    grad_key, grad_value = call(
        functools.partial(key_grads_kernel, scale, *counts),
        heads,
        scalars
        + own
        + [(tile, near_dk), (tile, near_dv), (row_spec, mid_rows), (row_spec, far_rows)]
        + mid_list
        + far_qg,
        [(tile, out)] * 2,
        [],
        (2 * unit, rows * flat * 16, rows * mid_count * heads),
    )
    return grad_query, grad_key, grad_value


def solution(mesh):
    row_spec = P(("seq", "lvl"), None)
    return jax.shard_map(
        local,
        mesh=mesh,
        in_specs=(row_spec, row_spec, row_spec, row_spec, P(), P()),
        out_specs=(row_spec, row_spec, row_spec),
        check_vma=False,
    )
```

```python
import functools

import jax
import jax.numpy as jnp
from jax import lax
from jax.experimental import pallas as pl
from jax.experimental.pallas import tpu as pltpu
from jax.sharding import PartitionSpec as P

F32 = jnp.float32
BF16 = jnp.bfloat16
LANES = 128
LOW = -1e30
VMEM_LIMIT = 60 * 1024 * 1024
GROUP = 2


def mm(a, b):
    return lax.dot_general(a, b, (((1,), (0,)), ((), ())), preferred_element_type=F32)


def mm_t(a, b):
    return lax.dot_general(a, b, (((1,), (1,)), ((), ())), preferred_element_type=F32)


def t_mm(a, b):
    return lax.dot_general(a, b, (((0,), (0,)), ((), ())), preferred_element_type=F32)


def exact(a, b):
    return lax.dot_general(
        a, b, (((1,), (0,)), ((), ())), preferred_element_type=F32, precision=lax.Precision.HIGHEST
    )


def iota(shape, axis):
    return lax.broadcasted_iota(jnp.int32, shape, axis)


def params():
    return pltpu.CompilerParams(
        vmem_limit_bytes=VMEM_LIMIT, dimension_semantics=("arbitrary",)
    )


def smem():
    return pl.BlockSpec(memory_space=pltpu.SMEM)


def columns(rows, width):
    return pl.BlockSpec((rows, width), lambda h: (0, h))


def fixed(shape):
    return pl.BlockSpec(shape, lambda h: (0,) * len(shape))


def pick_lane(ref, head):
    block = ref[...]
    return jnp.sum(jnp.where(iota(block.shape, 1) == head, block, 0.0), axis=1, keepdims=True)


def put_lane(ref, rows, head, value):
    block = ref[rows, :]
    ref[rows, :] = jnp.where(iota(block.shape, 1) == head, value, block)


def select_kernel(place, mid_off, far_off, q, k, v, g, kv, qg, far, *pays):
    level = place[1]
    rows = q.shape[0]
    for at in range(GROUP):
        head = pl.program_id(0) * GROUP + at
        cut = slice(at * LANES, (at + 1) * LANES)
        wide = slice(2 * at * LANES, 2 * (at + 1) * LANES)
        whole = jnp.concatenate([k[:, cut], v[:, cut], q[:, cut], g[:, cut]], axis=1)

        def picked(count, offset):
            stride = rows // count
            table = iota((count, rows), 1) == iota((count, rows), 0) * stride + offset
            return mm(table.astype(BF16), whole).astype(BF16)

        mid = picked(kv.shape[0], mid_off[head])
        half = 2 * LANES
        kv[:, wide] = mid[:, :half]
        qg[:, wide] = mid[:, half:]
        picks = picked(far.shape[1], far_off[head])
        far[0, :, wide] = picks[:, :half]
        far[1, :, wide] = picks[:, half:]
    for step, pay in enumerate(pays, 1):
        upward = (level ^ step) > level

        @pl.when(upward)
        def _():
            pay[...] = kv[...]

        @pl.when(jnp.logical_not(upward))
        def _():
            pay[...] = qg[...]


def near_kernel(scale, parts, q, k, v, g, logs, dots, soft_out, slope_out):
    @pl.when(pl.program_id(0) == 0)
    def _():
        logs[...] = jnp.zeros_like(logs)
        dots[...] = jnp.zeros_like(dots)

    size = q.shape[0] // parts
    for at in range(GROUP):
        head = pl.program_id(0) * GROUP + at
        cut = slice(at * LANES, (at + 1) * LANES)
        for part in range(parts):
            rows = slice(part * size, (part + 1) * size)
            width = (part + 1) * size
            scores = mm_t(q[rows, cut], k[:width, cut]) * scale
            grads = mm_t(g[rows, cut], v[:width, cut])
            seen = iota((size, width), 1) <= iota((size, width), 0) + part * size
            scores = jnp.where(seen, scores, LOW)
            peak = jnp.max(scores, axis=1, keepdims=True)
            weights = jnp.exp(scores - peak)
            total = jnp.sum(weights, axis=1, keepdims=True)
            soft = weights / total
            dot_part = jnp.sum(soft * grads, axis=1, keepdims=True)
            soft_out[at, rows, :width] = soft.astype(BF16)
            slope_out[at, rows, :width] = (soft * (grads - dot_part)).astype(BF16)
            put_lane(logs, rows, head, peak + jnp.log(total))
            put_lane(dots, rows, head, dot_part)


def row_stats(scores, grads):
    peak = jnp.max(scores, axis=1, keepdims=True)
    weights = jnp.exp(scores - peak)
    total = jnp.sum(weights, axis=1, keepdims=True)
    return peak + jnp.log(total), jnp.sum(weights * grads, axis=1, keepdims=True) / total


def mid_places(count, total, level):
    col = iota((count, total), 1)
    other = ((col >> (count.bit_length() - 1)) ^ level) * count + (col & (count - 1))
    return other, level * count + iota((count, total), 0)


def far_places(count, total, flat):
    return iota((count, total), 1), flat * count + iota((count, total), 0)


def bias(seen):
    return jnp.where(seen, 0.0, LOW)


def stack(refs, cut):
    return jnp.concatenate([ref[:, cut] for ref in refs], axis=0)


def repeat_table(rows, count):
    return (iota((rows, count), 0) // (rows // count) == iota((rows, count), 1)).astype(F32)


def gather_table(rows, count):
    return (iota((count, rows), 1) // (rows // count) == iota((count, rows), 0)).astype(F32)


def lane_offsets(offsets, heads):
    lane = iota((1, LANES), 1)
    values = jnp.zeros((1, LANES), jnp.int32)
    for head in range(heads):
        values = jnp.where(lane == head, offsets[head], values)
    return values


def level_stats_kernel(scale, heads, levels, mids, *refs):
    place, mid_off, far_off, kv, qg, far_own, near_logs, near_dots, far_in = refs[:9]
    mid_in = refs[9 : 9 + mids]
    (factors, shifts, mid_log, mid_dot, far_log, far_dot, mid_row, far_pack) = refs[9 + mids :][:8]
    mlog, mdot, flog, fdot = refs[17 + mids :]
    ring, level = place[0], place[1]
    mid_count, far_count = kv.shape[0], far_own.shape[1]
    total = mid_count * levels

    @pl.when(pl.program_id(0) == 0)
    def _():
        for ref in (mlog, mdot, flog, fdot):
            ref[...] = jnp.zeros_like(ref)

    keys_at, query_at = mid_places(mid_count, total, level)
    mid_bias = bias(keys_at <= query_at)
    keys_at, query_at = far_places(far_count, total, ring * levels + level)
    far_bias = bias(keys_at <= query_at)
    far_all = far_in[...].reshape(total, GROUP * 2 * LANES)
    every = slice(None)
    for at in range(GROUP):
        head = pl.program_id(0) * GROUP + at
        low = slice(2 * at * LANES, (2 * at + 1) * LANES)
        high = slice((2 * at + 1) * LANES, (2 * at + 2) * LANES)
        scores = mm_t(qg[:, low], stack((kv,) + mid_in, low)) * scale + mid_bias
        grads = mm_t(qg[:, high], stack((kv,) + mid_in, high))
        log_part, dot_part = row_stats(scores, grads)
        put_lane(mlog, every, head, log_part)
        put_lane(mdot, every, head, dot_part)
        scores = mm_t(far_own[1, :, low], far_all[:, low]) * scale + far_bias
        grads = mm_t(far_own[1, :, high], far_all[:, high])
        log_part, dot_part = row_stats(scores, grads)
        put_lane(flog, every, head, log_part)
        put_lane(fdot, every, head, dot_part)

    @pl.when(pl.program_id(0) == pl.num_programs(0) - 1)
    def _():
        rows = near_logs.shape[0]
        row = iota((rows, LANES), 0)
        mid_here = (row & (rows // mid_count - 1)) == lane_offsets(mid_off, heads)
        far_here = (row & (rows // far_count - 1)) == lane_offsets(far_off, heads)
        mid_table, far_table = repeat_table(rows, mid_count), repeat_table(rows, far_count)
        near = near_logs[...]
        mid = jnp.where(mid_here, exact(mid_table, mlog[...]), LOW)
        far = jnp.where(far_here, exact(far_table, flog[...]), LOW)
        peak = jnp.maximum(near, jnp.maximum(mid, far))
        near_part = jnp.exp(near - peak)
        mid, far = jnp.exp(mid - peak), jnp.exp(far - peak)
        whole = near_part + mid + far
        logs = peak + jnp.log(whole)
        dots = (
            near_part * near_dots[...]
            + mid * exact(mid_table, mdot[...])
            + far * exact(far_table, fdot[...])
        ) / whole
        factors[...] = jnp.exp(near - logs)
        shifts[...] = dots - near_dots[...]
        table = gather_table(rows, mid_count)
        mid_log[...] = exact(table, jnp.where(mid_here, logs, 0.0))
        mid_dot[...] = exact(table, jnp.where(mid_here, dots, 0.0))
        mid_row[:heads, :] = mid_log[...].T[:heads, :]
        mid_row[heads:, :] = mid_dot[...].T[:heads, :]
        table = gather_table(rows, far_count)
        far_log[...] = exact(table, jnp.where(far_here, logs, 0.0))
        far_dot[...] = exact(table, jnp.where(far_here, dots, 0.0))
        pack = jnp.concatenate([far_log[:, :heads], far_dot[:, :heads]], axis=1)
        far_pack[...] = jnp.broadcast_to(pack[None], far_pack.shape)


def spread(rows, offset, piece):
    count = piece.shape[0]
    table = (iota((rows, count), 0) == iota((rows, count), 1) * (rows // count) + offset).astype(BF16)
    high = piece.astype(BF16)
    low = (piece - high.astype(F32)).astype(BF16)
    return mm(table, high) + mm(table, low)


def grads_kernel(scale, heads, levels, parts, mids, *refs):
    place, mid_off, far_off, q, k, v, g, soft_in, slope_in, kv, qg, far_own, far_kv, far_qg = refs[:14]
    factors, shifts, mid_log, mid_dot, far_log, far_dot, mid_row, far_pack = refs[14:22]
    mid_in = refs[22 : 22 + mids]
    mid_rows = (mid_row,) + refs[22 + mids : 22 + 2 * mids]
    out_q, out_k, out_v, far_rows = refs[22 + 2 * mids :]
    ring, level = place[0], place[1]
    rows = q.shape[0]
    mid_count, far_count = kv.shape[0], far_own.shape[1]
    total = mid_count * levels
    size = rows // parts

    @pl.when(pl.program_id(0) == 0)
    def _():
        far_rows[...] = far_pack[...].reshape(total, 2 * heads).T

    other, own = mid_places(mid_count, total, level)
    mid_bias, mid_back = bias(other <= own), bias(other >= own)
    other, own = far_places(far_count, total, ring * levels + level)
    far_bias, far_back = bias(other <= own), bias(other >= own)
    far_k = far_kv[...].reshape(total, GROUP * 2 * LANES)
    far_q = far_qg[...].reshape(total, GROUP * 2 * LANES)

    def row_side(queries, cots, keys, vals, hide, logs, dots):
        scores = mm_t(queries, keys) * scale + hide
        soft = jnp.exp(scores - logs)
        slopes = soft * (mm_t(cots, vals) - dots)
        return soft.astype(BF16), slopes.astype(BF16)

    for at in range(GROUP):
        head = pl.program_id(0) * GROUP + at
        cut = slice(at * LANES, (at + 1) * LANES)
        low = slice(2 * at * LANES, (2 * at + 1) * LANES)
        high = slice((2 * at + 1) * LANES, (2 * at + 2) * LANES)
        mid_at, far_at = mid_off[head], far_off[head]

        keys = stack((kv,) + mid_in, low)
        vals = stack((kv,) + mid_in, high)
        _, slopes = row_side(
            qg[:, low], qg[:, high], keys, vals, mid_bias, pick_lane(mid_log, head), pick_lane(mid_dot, head)
        )
        mid_dq = mm(slopes, keys)
        queries = stack((qg,) + mid_in, low)
        cots = stack((qg,) + mid_in, high)
        logs = jnp.concatenate([ref[pl.ds(head, 1), :] for ref in mid_rows], axis=1)
        dots = jnp.concatenate([ref[pl.ds(head + heads, 1), :] for ref in mid_rows], axis=1)
        soft, slopes = row_side(kv[:, low], kv[:, high], queries, cots, mid_back, logs, dots)
        mid_dk, mid_dv = mm(slopes, queries), mm(soft, cots)

        _, slopes = row_side(
            far_own[1, :, low],
            far_own[1, :, high],
            far_k[:, low],
            far_k[:, high],
            far_bias,
            pick_lane(far_log, head),
            pick_lane(far_dot, head),
        )
        far_dq = mm(slopes, far_k[:, low])
        soft, slopes = row_side(
            far_own[0, :, low],
            far_own[0, :, high],
            far_q[:, low],
            far_q[:, high],
            far_back,
            far_rows[pl.ds(head, 1), :],
            far_rows[pl.ds(head + heads, 1), :],
        )
        far_dk, far_dv = mm(slopes, far_q[:, low]), mm(soft, far_q[:, high])

        whole = spread(rows, mid_at, jnp.concatenate([mid_dq, mid_dk, mid_dv], axis=1))
        whole += spread(rows, far_at, jnp.concatenate([far_dq, far_dk, far_dv], axis=1))
        dq, dk, dv = (whole[:, i * LANES : (i + 1) * LANES] for i in range(3))

        factor, shift = pick_lane(factors, head), pick_lane(shifts, head)
        for part in range(parts):
            part_rows = slice(part * size, (part + 1) * size)
            width = (part + 1) * size
            soft = soft_in[at, part_rows, :width].astype(F32)
            slopes = slope_in[at, part_rows, :width].astype(F32)
            slopes = (factor[part_rows] * (slopes - soft * shift[part_rows])).astype(BF16)
            soft = (factor[part_rows] * soft).astype(BF16)
            near_dq = mm(slopes, k[:width, cut])
            out_q[part_rows, cut] = ((dq[part_rows] + near_dq) * scale).astype(BF16)
            key_part = t_mm(slopes, q[part_rows, cut])
            value_part = t_mm(soft, g[part_rows, cut])
            if width < rows:
                rest = jnp.zeros((rows - width, LANES), F32)
                key_part = jnp.concatenate([key_part, rest], axis=0)
                value_part = jnp.concatenate([value_part, rest], axis=0)
            dk, dv = dk + key_part, dv + value_part
        out_k[:, cut] = (dk * scale).astype(BF16)
        out_v[:, cut] = dv.astype(BF16)


def swap(array, axis, size, step):
    return lax.ppermute(array, axis, [(i, i ^ step) for i in range(size)])


def call(kernel, steps, ins, outs, scratch, cost):
    specs, arrays = zip(*ins)
    out_specs, out_shapes = zip(*outs)
    return pl.pallas_call(
        kernel,
        grid=(steps,),
        in_specs=list(specs),
        out_specs=list(out_specs),
        out_shape=list(out_shapes),
        scratch_shapes=scratch,
        compiler_params=params(),
        cost_estimate=pl.CostEstimate(flops=cost[0], bytes_accessed=cost[1], transcendentals=cost[2]),
    )(*arrays)


def local(queries, keys, values, grad_out, mid_offset, far_offset):
    rows, flat = queries.shape
    heads = mid_offset.shape[0]
    width = flat // heads
    scale = width ** (-0.5)
    levels, rings = lax.axis_size("lvl"), lax.axis_size("seq")
    mid_count, far_count = rows // levels, rows // (levels * rings)
    block = far_count * levels
    level = lax.axis_index("lvl")
    place = jnp.stack([lax.axis_index("seq"), level]).astype(jnp.int32)
    shape = jax.ShapeDtypeStruct
    parts = 2
    steps = heads // GROUP
    tile = columns(rows, GROUP * width)
    mid_spec = columns(mid_count, GROUP * 2 * width)
    far_spec = pl.BlockSpec((2, far_count, GROUP * 2 * width), lambda h: (0, 0, h))
    sources = [(tile, queries), (tile, keys), (tile, values), (tile, grad_out)]
    scalars = [(smem(), place), (smem(), mid_offset), (smem(), far_offset)]
    unit = rows * rows * width * 2 * heads
    mid_shape = shape((mid_count, 2 * flat), BF16)

    kv, qg, far, *pays = call(
        select_kernel,
        steps,
        scalars + sources,
        [(mid_spec, mid_shape)] * 2
        + [(far_spec, shape((2, far_count, 2 * flat), BF16))]
        + [(mid_spec, mid_shape)] * (levels - 1),
        [],
        (unit, rows * flat * 16, 0),
    )
    pieces = [far] + [swap(far, "lvl", levels, step) for step in range(1, levels)]
    mid_in = [swap(pays[step - 1], "lvl", levels, step) for step in range(1, levels)]

    def at_level(where):
        chosen = pieces[0]
        for step in range(1, levels):
            chosen = jnp.where((where ^ level) == step, pieces[step], chosen)
        return chosen

    column = jnp.concatenate([at_level(where) for where in range(levels)], axis=1)
    far_all = lax.all_gather(column, "seq", axis=0)

    stat, stat_spec = shape((rows, LANES), F32), fixed((rows, LANES))
    square = shape((heads, rows, rows), BF16)
    square_spec = pl.BlockSpec((GROUP, rows, rows), lambda h: (h, 0, 0))
    near_logs, near_dots, near_soft, near_slopes = call(
        functools.partial(near_kernel, scale, parts),
        steps,
        sources,
        [(stat_spec, stat)] * 2 + [(square_spec, square)] * 2,
        [],
        (2 * unit, rows * flat * 8 + rows * rows * heads * 4, rows * rows * heads),
    )

    def gathered(which):
        spec = pl.BlockSpec((rings, 1, block, GROUP * 2 * width), lambda h: (0, which, 0, h))
        return (spec, far_all)

    mid_list = [(mid_spec, piece) for piece in mid_in]
    own = [(mid_spec, kv), (mid_spec, qg), (far_spec, far)]
    mid_stat, far_stat = shape((mid_count, LANES), F32), shape((far_count, LANES), F32)
    row_shape = shape((2 * heads, mid_count), F32)
    pack_shape = shape((levels * rings, far_count, 2 * heads), F32)
    stat_outs = [stat] * 2 + [mid_stat] * 2 + [far_stat] * 2 + [row_shape, pack_shape]
    stats = call(
        functools.partial(level_stats_kernel, scale, heads, levels, levels - 1),
        steps,
        scalars
        + own
        + [(stat_spec, near_logs), (stat_spec, near_dots)]
        + [gathered(0)]
        + mid_list,
        [(fixed(out.shape), out) for out in stat_outs],
        [pltpu.VMEM((mid_count, LANES), F32)] * 2 + [pltpu.VMEM((far_count, LANES), F32)] * 2,
        (unit, rows * flat * 16, rows * mid_count * heads),
    )
    mid_row, far_pack = stats[-2:]
    row_in = [swap(mid_row, "lvl", levels, step) for step in range(1, levels)]
    far_pack = lax.all_to_all(far_pack, ("seq", "lvl"), 0, 0, tiled=True)

    out = shape((rows, flat), BF16)
    stat_ins = [(fixed(array.shape), array) for array in list(stats[:-1]) + [far_pack] + row_in]
    return call(
        functools.partial(grads_kernel, scale, heads, levels, parts, levels - 1),
        steps,
        scalars
        + sources
        + [(square_spec, near_soft), (square_spec, near_slopes)]
        + own
        + [gathered(0), gathered(1)]
        + stat_ins[:8]
        + mid_list
        + stat_ins[8:],
        [(tile, out)] * 3,
        [pltpu.VMEM((2 * heads, rows), F32)],
        (6 * unit, rows * flat * 24 + rows * rows * heads * 4, rows * mid_count * heads),
    )


def solution(mesh):
    row_spec = P(("seq", "lvl"), None)
    return jax.shard_map(
        local,
        mesh=mesh,
        in_specs=(row_spec, row_spec, row_spec, row_spec, P(), P()),
        out_specs=(row_spec, row_spec, row_spec),
        check_vma=False,
    )
```

```python
import functools

import jax
import jax.numpy as jnp
from jax import lax
from jax.experimental import pallas as pl
from jax.experimental.pallas import tpu as pltpu
from jax.sharding import PartitionSpec as P

F32 = jnp.float32
BF16 = jnp.bfloat16
LANES = 128
LOW = -1e30
MIB = 1024 * 1024
GROUP = 4
LIMIT = 28


def mm(a, b):
    return lax.dot_general(a, b, (((1,), (0,)), ((), ())), preferred_element_type=F32)


def mm_t(a, b):
    return lax.dot_general(a, b, (((1,), (1,)), ((), ())), preferred_element_type=F32)


def t_mm(a, b):
    return lax.dot_general(a, b, (((0,), (0,)), ((), ())), preferred_element_type=F32)


def exact(a, b):
    return lax.dot_general(
        a, b, (((1,), (0,)), ((), ())), preferred_element_type=F32, precision=lax.Precision.HIGHEST
    )


def iota(shape, axis):
    return lax.broadcasted_iota(jnp.int32, shape, axis)


def params(limit):
    return pltpu.CompilerParams(
        vmem_limit_bytes=limit * MIB, dimension_semantics=("arbitrary",)
    )


def smem():
    return pl.BlockSpec(memory_space=pltpu.SMEM)


def columns(rows, width):
    return pl.BlockSpec((rows, width), lambda h: (0, h))


def fixed(shape):
    return pl.BlockSpec(shape, lambda h: (0,) * len(shape))


def pick_lane(ref, head):
    block = ref[...]
    return jnp.sum(jnp.where(iota(block.shape, 1) == head, block, 0.0), axis=1, keepdims=True)


def put_lane(ref, rows, head, value):
    block = ref[rows, :]
    ref[rows, :] = jnp.where(iota(block.shape, 1) == head, value, block)


def select_kernel(place, mid_off, far_off, q, k, v, g, kv, qg, far, *pays):
    level = place[1]
    rows = q.shape[0]
    for at in range(GROUP):
        head = pl.program_id(0) * GROUP + at
        cut = slice(at * LANES, (at + 1) * LANES)
        wide = slice(2 * at * LANES, 2 * (at + 1) * LANES)
        whole = jnp.concatenate([k[:, cut], v[:, cut], q[:, cut], g[:, cut]], axis=1)

        def picked(count, offset):
            stride = rows // count
            table = iota((count, rows), 1) == iota((count, rows), 0) * stride + offset
            return mm(table.astype(BF16), whole).astype(BF16)

        mid = picked(kv.shape[0], mid_off[head])
        half = 2 * LANES
        kv[:, wide] = mid[:, :half]
        qg[:, wide] = mid[:, half:]
        picks = picked(far.shape[1], far_off[head])
        far[0, :, wide] = picks[:, :half]
        far[1, :, wide] = picks[:, half:]
    for step, pay in enumerate(pays, 1):
        upward = (level ^ step) > level

        @pl.when(upward)
        def _():
            pay[...] = kv[...]

        @pl.when(jnp.logical_not(upward))
        def _():
            pay[...] = qg[...]


def near_kernel(scale, parts, q, k, v, g, logs, dots, soft_out, slope_out):
    @pl.when(pl.program_id(0) == 0)
    def _():
        logs[...] = jnp.zeros_like(logs)
        dots[...] = jnp.zeros_like(dots)

    size = q.shape[0] // parts
    for at in range(GROUP):
        head = pl.program_id(0) * GROUP + at
        cut = slice(at * LANES, (at + 1) * LANES)
        for part in range(parts):
            rows = slice(part * size, (part + 1) * size)
            width = (part + 1) * size
            scores = mm_t(q[rows, cut], k[:width, cut]) * scale
            grads = mm_t(g[rows, cut], v[:width, cut])
            seen = iota((size, width), 1) <= iota((size, width), 0) + part * size
            scores = jnp.where(seen, scores, LOW)
            peak = jnp.max(scores, axis=1, keepdims=True)
            weights = jnp.exp(scores - peak)
            total = jnp.sum(weights, axis=1, keepdims=True)
            soft = weights / total
            dot_part = jnp.sum(soft * grads, axis=1, keepdims=True)
            soft_out[at, rows, :width] = soft.astype(BF16)
            slope_out[at, rows, :width] = (soft * (grads - dot_part)).astype(BF16)
            put_lane(logs, rows, head, peak + jnp.log(total))
            put_lane(dots, rows, head, dot_part)


def row_stats(scores, grads):
    peak = jnp.max(scores, axis=1, keepdims=True)
    weights = jnp.exp(scores - peak)
    total = jnp.sum(weights, axis=1, keepdims=True)
    return peak + jnp.log(total), jnp.sum(weights * grads, axis=1, keepdims=True) / total


def mid_places(count, total, level):
    col = iota((count, total), 1)
    other = ((col >> (count.bit_length() - 1)) ^ level) * count + (col & (count - 1))
    return other, level * count + iota((count, total), 0)


def far_places(count, total, levels, level, ring):
    col = iota((count, total), 1)
    bits, level_bits = count.bit_length() - 1, levels.bit_length() - 1
    slot, ring_slot = (col >> bits) & (levels - 1), col >> (bits + level_bits)
    other = ((ring_slot ^ ring) * levels + (slot ^ level)) * count + (col & (count - 1))
    return other, (ring * levels + level) * count + iota((count, total), 0)


def bias(seen):
    return jnp.where(seen, 0.0, LOW)


def stack(refs, cut):
    return jnp.concatenate([ref[:, cut] for ref in refs], axis=0)


def repeat_table(rows, count):
    return (iota((rows, count), 0) // (rows // count) == iota((rows, count), 1)).astype(F32)


def gather_table(rows, count):
    return (iota((count, rows), 1) // (rows // count) == iota((count, rows), 0)).astype(F32)


def lane_offsets(offsets, heads):
    lane = iota((1, LANES), 1)
    values = jnp.zeros((1, LANES), jnp.int32)
    for head in range(heads):
        values = jnp.where(lane == head, offsets[head], values)
    return values


def column_kernel(levels, bits, *refs):
    place = refs[0]
    pieces = refs[1 : 1 + levels]
    col_kv, col_qg = refs[1 + levels : 3 + levels]
    pays = refs[3 + levels :]
    col_kv[...] = jnp.concatenate([piece[0] for piece in pieces], axis=0)
    col_qg[...] = jnp.concatenate([piece[1] for piece in pieces], axis=0)
    for bit in range(bits):
        upward = ((place[0] >> bit) & 1) == 0

        @pl.when(upward)
        def _():
            pays[bit][...] = col_kv[...]

        @pl.when(jnp.logical_not(upward))
        def _():
            pays[bit][...] = col_qg[...]


def cuts(at):
    low = slice(2 * at * LANES, (2 * at + 1) * LANES)
    return low, slice((2 * at + 1) * LANES, (2 * at + 2) * LANES)


def level_stats_kernel(scale, heads, levels, mids, fars, *refs):
    place, mid_off, far_off, kv, qg, far_own, near_logs, near_dots = refs[:8]
    mid_in, far_in = refs[8 : 8 + mids], refs[8 + mids : 8 + mids + fars]
    factors, shifts, mid_log, mid_dot, far_log, far_dot, sent = refs[8 + mids + fars :][:7]
    mlog, mdot, flog, fdot = refs[15 + mids + fars :]
    ring, level = place[0], place[1]
    mid_count, far_count = kv.shape[0], far_own.shape[1]
    total = mid_count * levels

    @pl.when(pl.program_id(0) == 0)
    def _():
        for ref in (mlog, mdot, flog, fdot):
            ref[...] = jnp.zeros_like(ref)

    other, own = mid_places(mid_count, total, level)
    mid_bias = bias(other <= own)
    other, own = far_places(far_count, total, levels, level, ring)
    far_bias = bias(other <= own)
    every = slice(None)
    for at in range(GROUP):
        head = pl.program_id(0) * GROUP + at
        low, high = cuts(at)
        scores = mm_t(qg[:, low], stack((kv,) + mid_in, low)) * scale + mid_bias
        grads = mm_t(qg[:, high], stack((kv,) + mid_in, high))
        log_part, dot_part = row_stats(scores, grads)
        put_lane(mlog, every, head, log_part)
        put_lane(mdot, every, head, dot_part)
        scores = mm_t(far_own[1, :, low], stack(far_in, low)) * scale + far_bias
        grads = mm_t(far_own[1, :, high], stack(far_in, high))
        log_part, dot_part = row_stats(scores, grads)
        put_lane(flog, every, head, log_part)
        put_lane(fdot, every, head, dot_part)

    @pl.when(pl.program_id(0) == pl.num_programs(0) - 1)
    def _():
        rows = near_logs.shape[0]
        row = iota((rows, LANES), 0)
        mid_here = (row & (rows // mid_count - 1)) == lane_offsets(mid_off, heads)
        far_here = (row & (rows // far_count - 1)) == lane_offsets(far_off, heads)
        mid_table, far_table = repeat_table(rows, mid_count), repeat_table(rows, far_count)
        near = near_logs[...]
        mid = jnp.where(mid_here, exact(mid_table, mlog[...]), LOW)
        far = jnp.where(far_here, exact(far_table, flog[...]), LOW)
        peak = jnp.maximum(near, jnp.maximum(mid, far))
        near_part = jnp.exp(near - peak)
        mid, far = jnp.exp(mid - peak), jnp.exp(far - peak)
        whole = near_part + mid + far
        logs = peak + jnp.log(whole)
        dots = (
            near_part * near_dots[...]
            + mid * exact(mid_table, mdot[...])
            + far * exact(far_table, fdot[...])
        ) / whole
        factors[...] = jnp.exp(near - logs)
        shifts[...] = dots - near_dots[...]
        for here, count, log_out, dot_out, first in (
            (mid_here, mid_count, mid_log, mid_dot, 0),
            (far_here, far_count, far_log, far_dot, mid_count),
        ):
            table = gather_table(rows, count)
            log_out[...] = exact(table, jnp.where(here, logs, 0.0))
            dot_out[...] = exact(table, jnp.where(here, dots, 0.0))
            sent[:heads, first : first + count] = log_out[...].T[:heads, :]
            sent[heads:, first : first + count] = dot_out[...].T[:heads, :]


def row_side(scale, queries, cots, keys, vals, hide, logs, dots):
    scores = mm_t(queries, keys) * scale + hide
    soft = jnp.exp(scores - logs)
    slopes = soft * (mm_t(cots, vals) - dots)
    return soft.astype(BF16), slopes.astype(BF16)


def level_queries_kernel(scale, levels, mids, fars, *refs):
    place, kv, qg, far_own, mid_log, mid_dot, far_log, far_dot = refs[:8]
    mid_in, far_in = refs[8 : 8 + mids], refs[8 + mids : 8 + mids + fars]
    mid_dq, far_dq = refs[8 + mids + fars :]
    ring, level = place[0], place[1]
    mid_count, far_count = kv.shape[0], far_own.shape[1]
    total = mid_count * levels
    other, own = mid_places(mid_count, total, level)
    mid_bias = bias(other <= own)
    other, own = far_places(far_count, total, levels, level, ring)
    far_bias = bias(other <= own)
    for at in range(GROUP):
        head = pl.program_id(0) * GROUP + at
        cut = slice(at * LANES, (at + 1) * LANES)
        low, high = cuts(at)
        keys, vals = stack((kv,) + mid_in, low), stack((kv,) + mid_in, high)
        logs, dots = pick_lane(mid_log, head), pick_lane(mid_dot, head)
        _, slopes = row_side(scale, qg[:, low], qg[:, high], keys, vals, mid_bias, logs, dots)
        mid_dq[:, cut] = mm(slopes, keys)
        keys, vals = stack(far_in, low), stack(far_in, high)
        logs, dots = pick_lane(far_log, head), pick_lane(far_dot, head)
        _, slopes = row_side(
            scale, far_own[1, :, low], far_own[1, :, high], keys, vals, far_bias, logs, dots
        )
        far_dq[:, cut] = mm(slopes, keys)


def spread(rows, offset, piece):
    count = piece.shape[0]
    table = (iota((rows, count), 0) == iota((rows, count), 1) * (rows // count) + offset).astype(BF16)
    high = piece.astype(BF16)
    low = (piece - high.astype(F32)).astype(BF16)
    return mm(table, high) + mm(table, low)


def near_grads_kernel(scale, parts, mid_off, far_off, q, k, g, soft_in, slope_in, *refs):
    factors, shifts, mid_dq, far_dq, out_q, out_k, out_v = refs
    rows = q.shape[0]
    size = rows // parts
    for at in range(GROUP):
        head = pl.program_id(0) * GROUP + at
        cut = slice(at * LANES, (at + 1) * LANES)
        dq = spread(rows, mid_off[head], mid_dq[:, cut]) + spread(rows, far_off[head], far_dq[:, cut])
        factor, shift = pick_lane(factors, head), pick_lane(shifts, head)
        for part in reversed(range(parts)):
            part_rows = slice(part * size, (part + 1) * size)
            width = (part + 1) * size
            soft = soft_in[at, part_rows, :width].astype(F32)
            slopes = slope_in[at, part_rows, :width].astype(F32)
            slopes = (factor[part_rows] * (slopes - soft * shift[part_rows])).astype(BF16)
            soft = (factor[part_rows] * soft).astype(BF16)
            near_dq = mm(slopes, k[:width, cut])
            out_q[part_rows, cut] = ((dq[part_rows] + near_dq) * scale).astype(BF16)
            key_part = t_mm(slopes, q[part_rows, cut])
            value_part = t_mm(soft, g[part_rows, cut])
            if part == parts - 1:
                out_k[:, cut] = key_part
                out_v[:, cut] = value_part
            else:
                out_k[:width, cut] += key_part
                out_v[:width, cut] += value_part


def level_keys_kernel(scale, heads, levels, mids, fars, *refs):
    place, mid_off, far_off, kv, qg, far_own, near_dk, near_dv = refs[:8]
    mid_in, far_in = refs[8 : 8 + mids], refs[8 + mids : 8 + mids + fars]
    mid_stats = refs[8 + mids + fars :][: mids + 1]
    far_stats = refs[9 + 2 * mids + fars : 9 + 2 * mids + 2 * fars]
    out_k, out_v, mid_rows, far_rows = refs[9 + 2 * mids + 2 * fars :]
    ring, level = place[0], place[1]
    rows = out_k.shape[0]
    mid_count, far_count = kv.shape[0], far_own.shape[1]
    total = mid_count * levels

    @pl.when(pl.program_id(0) == 0)
    def _():
        mid_rows[...] = jnp.concatenate([ref[:, :mid_count] for ref in mid_stats], axis=1)
        far_rows[...] = jnp.concatenate([ref[...] for ref in far_stats], axis=1)

    other, own = mid_places(mid_count, total, level)
    mid_bias = bias(other >= own)
    other, own = far_places(far_count, total, levels, level, ring)
    far_bias = bias(other >= own)
    for at in range(GROUP):
        head = pl.program_id(0) * GROUP + at
        cut = slice(at * LANES, (at + 1) * LANES)
        low, high = cuts(at)

        def one(keys, vals, queries, cots, hide, stats):
            logs, dots = stats[pl.ds(head, 1), :], stats[pl.ds(head + heads, 1), :]
            soft, slopes = row_side(scale, keys, vals, queries, cots, hide, logs, dots)
            return jnp.concatenate([mm(slopes, queries), mm(soft, cots)], axis=1)

        queries, cots = stack((qg,) + mid_in, low), stack((qg,) + mid_in, high)
        mid = one(kv[:, low], kv[:, high], queries, cots, mid_bias, mid_rows)
        queries, cots = stack(far_in, low), stack(far_in, high)
        far = one(far_own[0, :, low], far_own[0, :, high], queries, cots, far_bias, far_rows)
        whole = spread(rows, mid_off[head], mid) + spread(rows, far_off[head], far)
        out_k[:, cut] = ((near_dk[:, cut] + whole[:, :LANES]) * scale).astype(BF16)
        out_v[:, cut] = (near_dv[:, cut] + whole[:, LANES:]).astype(BF16)


def swap(array, axis, size, step):
    return lax.ppermute(array, axis, [(i, i ^ step) for i in range(size)])


def call(kernel, steps, ins, outs, scratch, limit=LIMIT):
    specs, arrays = zip(*ins)
    out_specs, out_shapes = zip(*outs)
    return pl.pallas_call(
        kernel,
        grid=(steps,),
        in_specs=list(specs),
        out_specs=list(out_specs),
        out_shape=list(out_shapes),
        scratch_shapes=scratch,
        compiler_params=params(limit),
        cost_estimate=pl.CostEstimate(flops=0, bytes_accessed=0, transcendentals=0),
    )(*arrays)


def local(queries, keys, values, grad_out, mid_offset, far_offset):
    rows, flat = queries.shape
    heads = mid_offset.shape[0]
    width = flat // heads
    scale = width ** (-0.5)
    levels, rings = lax.axis_size("lvl"), lax.axis_size("seq")
    mid_count, far_count = rows // levels, rows // (levels * rings)
    block = far_count * levels
    level = lax.axis_index("lvl")
    place = jnp.stack([lax.axis_index("seq"), level]).astype(jnp.int32)
    shape = jax.ShapeDtypeStruct
    parts = 2
    steps = heads // GROUP
    tile = columns(rows, GROUP * width)
    mid_spec = columns(mid_count, GROUP * 2 * width)
    far_spec = pl.BlockSpec((2, far_count, GROUP * 2 * width), lambda h: (0, 0, h))
    sources = [(tile, queries), (tile, keys), (tile, values), (tile, grad_out)]
    scalars = [(smem(), place), (smem(), mid_offset), (smem(), far_offset)]
    mid_shape = shape((mid_count, 2 * flat), BF16)

    kv, qg, far, *pays = call(
        select_kernel,
        steps,
        scalars + sources,
        [(mid_spec, mid_shape)] * 2
        + [(far_spec, shape((2, far_count, 2 * flat), BF16))]
        + [(mid_spec, mid_shape)] * (levels - 1),
        [],
        60,
    )
    far_level = [far] + [swap(far, "lvl", levels, step) for step in range(1, levels)]
    mid_in = [swap(pays[step - 1], "lvl", levels, step) for step in range(1, levels)]
    stat, stat_spec = shape((rows, LANES), F32), fixed((rows, LANES))
    square = shape((heads, rows, rows), BF16)
    square_spec = pl.BlockSpec((GROUP, rows, rows), lambda h: (h, 0, 0))
    near_logs, near_dots, near_soft, near_slopes = call(
        functools.partial(near_kernel, scale, parts),
        steps,
        sources,
        [(stat_spec, stat)] * 2 + [(square_spec, square)] * 2,
        [],
    )
    far_level, near_logs = lax.optimization_barrier((far_level, near_logs))
    ring_bits = rings.bit_length() - 1
    col_shape = shape((block, 2 * flat), BF16)
    col_kv, col_qg, *ring_pays = call(
        functools.partial(column_kernel, levels, ring_bits),
        1,
        scalars[:1] + [(fixed(piece.shape), piece) for piece in far_level],
        [(fixed(col_shape.shape), col_shape)] * (2 + ring_bits),
        [],
    )
    far_ring = [None] * rings
    for step in range(2, rings, 2):
        far_ring[step] = swap(ring_pays[step.bit_length() - 1], "seq", rings, step)
    far_ring[1] = swap(ring_pays[0], "seq", rings, 1)
    for step in range(3, rings, 2):
        far_ring[step] = swap(far_ring[step - 1], "seq", rings, 1)

    col_spec = columns(block, GROUP * 2 * width)
    mid_list = [(mid_spec, piece) for piece in mid_in]
    far_rest = [(col_spec, piece) for piece in far_ring[1:]]
    far_kv, far_qg = [(col_spec, col_kv)] + far_rest, [(col_spec, col_qg)] + far_rest
    own = [(mid_spec, kv), (mid_spec, qg), (far_spec, far)]
    mid_stat, far_stat = shape((mid_count, LANES), F32), shape((far_count, LANES), F32)
    sent_shape = shape((2 * heads, mid_count + far_count), F32)
    stat_outs = [stat] * 2 + [mid_stat] * 2 + [far_stat] * 2 + [sent_shape]
    factors, shifts, mid_log, mid_dot, far_log, far_dot, sent = call(
        functools.partial(level_stats_kernel, scale, heads, levels, levels - 1, rings),
        steps,
        scalars + own + [(stat_spec, near_logs), (stat_spec, near_dots)] + mid_list + far_kv,
        [(fixed(out.shape), out) for out in stat_outs],
        [pltpu.VMEM((mid_count, LANES), F32)] * 2 + [pltpu.VMEM((far_count, LANES), F32)] * 2,
    )

    sent_in = [sent] + [swap(sent, "lvl", levels, step) for step in range(1, levels)]
    mid_dq, far_dq = call(
        functools.partial(level_queries_kernel, scale, levels, levels - 1, rings),
        steps,
        scalars[:1]
        + own
        + [(fixed(mid_stat.shape), mid_log), (fixed(mid_stat.shape), mid_dot)]
        + [(fixed(far_stat.shape), far_log), (fixed(far_stat.shape), far_dot)]
        + mid_list
        + far_kv,
        [
            (columns(mid_count, GROUP * width), shape((mid_count, flat), F32)),
            (columns(far_count, GROUP * width), shape((far_count, flat), F32)),
        ],
        [],
    )
    sent_in, mid_dq = lax.optimization_barrier((sent_in, mid_dq))
    far_sent = jnp.concatenate([piece[:, mid_count:] for piece in sent_in], axis=1)
    far_sent_in = [far_sent] + [swap(far_sent, "seq", rings, step) for step in range(1, rings)]

    out, grad = shape((rows, flat), BF16), shape((rows, flat), F32)
    grad_query, near_dk, near_dv = call(
        functools.partial(near_grads_kernel, scale, parts),
        steps,
        scalars[1:]
        + [(tile, queries), (tile, keys), (tile, grad_out)]
        + [(square_spec, near_soft), (square_spec, near_slopes)]
        + [(stat_spec, factors), (stat_spec, shifts)]
        + [(columns(mid_count, GROUP * width), mid_dq), (columns(far_count, GROUP * width), far_dq)],
        [(tile, out), (tile, grad), (tile, grad)],
        [],
    )
    grad_key, grad_value = call(
        functools.partial(level_keys_kernel, scale, heads, levels, levels - 1, rings),
        steps,
        scalars
        + own
        + [(tile, near_dk), (tile, near_dv)]
        + mid_list
        + far_qg
        + [(fixed(piece.shape), piece) for piece in sent_in + far_sent_in],
        [(tile, out)] * 2,
        [pltpu.VMEM((2 * heads, rows), F32)] * 2,
    )
    return grad_query, grad_key, grad_value


def solution(mesh):
    row_spec = P(("seq", "lvl"), None)
    return jax.shard_map(
        local,
        mesh=mesh,
        in_specs=(row_spec, row_spec, row_spec, row_spec, P(), P()),
        out_specs=(row_spec, row_spec, row_spec),
        check_vma=False,
    )
```

```python
import functools

import jax
import jax.numpy as jnp
from jax import lax
from jax.experimental import pallas as pl
from jax.experimental.pallas import tpu as pltpu
from jax.sharding import PartitionSpec as P

F32 = jnp.float32
BF16 = jnp.bfloat16
LANES = 128
LOW = -1e30
MIB = 1024 * 1024
GROUP = 4
LIMIT = 22


def mm(a, b):
    return lax.dot_general(a, b, (((1,), (0,)), ((), ())), preferred_element_type=F32)


def mm_t(a, b):
    return lax.dot_general(a, b, (((1,), (1,)), ((), ())), preferred_element_type=F32)


def t_mm(a, b):
    return lax.dot_general(a, b, (((0,), (0,)), ((), ())), preferred_element_type=F32)


def exact(a, b):
    return lax.dot_general(
        a, b, (((1,), (0,)), ((), ())), preferred_element_type=F32, precision=lax.Precision.HIGHEST
    )


def iota(shape, axis):
    return lax.broadcasted_iota(jnp.int32, shape, axis)


def params(limit):
    return pltpu.CompilerParams(
        vmem_limit_bytes=limit * MIB, dimension_semantics=("arbitrary",)
    )


def smem():
    return pl.BlockSpec(memory_space=pltpu.SMEM)


def columns(rows, width):
    return pl.BlockSpec((rows, width), lambda h: (0, h))


def fixed(shape):
    return pl.BlockSpec(shape, lambda h: (0,) * len(shape))


def pick_lane(ref, head):
    block = ref[...]
    return jnp.sum(jnp.where(iota(block.shape, 1) == head, block, 0.0), axis=1, keepdims=True)


def put_lane(ref, rows, head, value):
    block = ref[rows, :]
    ref[rows, :] = jnp.where(iota(block.shape, 1) == head, value, block)


def select_kernel(mid_off, far_off, q, k, v, g, kv, qg, far, *pays):
    level = lax.axis_index("lvl")
    rows = q.shape[0]
    for at in range(GROUP):
        head = pl.program_id(0) * GROUP + at
        cut = slice(at * LANES, (at + 1) * LANES)
        wide = slice(2 * at * LANES, 2 * (at + 1) * LANES)
        whole = jnp.concatenate([k[:, cut], v[:, cut], q[:, cut], g[:, cut]], axis=1)

        def picked(count, offset):
            stride = rows // count
            table = iota((count, rows), 1) == iota((count, rows), 0) * stride + offset
            return mm(table.astype(BF16), whole).astype(BF16)

        mid = picked(kv.shape[0], mid_off[head])
        half = 2 * LANES
        kv[:, wide] = mid[:, :half]
        qg[:, wide] = mid[:, half:]
        picks = picked(far.shape[1], far_off[head])
        far[0, :, wide] = picks[:, :half]
        far[1, :, wide] = picks[:, half:]
    firsts, seconds = pays[: len(pays) // 2], pays[len(pays) // 2 :]
    for step, (first, second) in enumerate(zip(firsts, seconds), 1):
        upward = (level ^ step) > level

        @pl.when(upward & (pl.program_id(0) == 0))
        def _():
            first[...] = kv[...]

        @pl.when(upward & (pl.program_id(0) == 1))
        def _():
            second[...] = kv[...]

        @pl.when(jnp.logical_not(upward) & (pl.program_id(0) == 0))
        def _():
            second[...] = qg[...]

        @pl.when(jnp.logical_not(upward) & (pl.program_id(0) == 1))
        def _():
            first[...] = qg[...]


def near_kernel(scale, parts, group, q, k, v, g, logs, dots, soft_out, slope_out, base):
    logs[...] = jnp.zeros_like(logs)
    dots[...] = jnp.zeros_like(dots)
    size = q.shape[0] // parts
    for at in range(GROUP):
        cut = slice(at * LANES, (at + 1) * LANES)
        low, high = cuts(at)
        for part in range(parts):
            rows = slice(part * size, (part + 1) * size)
            width = (part + 1) * size
            scores = mm_t(q[rows, cut], k[:width, cut]) * scale
            grads = mm_t(g[rows, cut], v[:width, cut])
            seen = iota((size, width), 1) <= iota((size, width), 0) + part * size
            scores = jnp.where(seen, scores, LOW)
            peak = jnp.max(scores, axis=1, keepdims=True)
            weights = jnp.exp(scores - peak)
            total = jnp.sum(weights, axis=1, keepdims=True)
            soft = weights / total
            dot_part = jnp.sum(soft * grads, axis=1, keepdims=True)
            slopes = (soft * (grads - dot_part)).astype(BF16)
            soft = soft.astype(BF16)
            base[rows, low] = mm(slopes, k[:width, cut])
            base[rows, high] = mm(soft, k[:width, cut])
            soft_out[at, :width, rows] = soft.T
            slope_out[at, :width, rows] = slopes.T
            put_lane(logs, rows, group * GROUP + at, peak + jnp.log(total))
            put_lane(dots, rows, group * GROUP + at, dot_part)


def row_stats(scores, grads):
    peak = jnp.max(scores, axis=1, keepdims=True)
    weights = jnp.exp(scores - peak)
    total = jnp.sum(weights, axis=1, keepdims=True)
    return peak + jnp.log(total), jnp.sum(weights * grads, axis=1, keepdims=True) / total


def mid_places(count, total, level):
    col = iota((count, total), 1)
    other = ((col >> (count.bit_length() - 1)) ^ level) * count + (col & (count - 1))
    return other, level * count + iota((count, total), 0)


def far_places(count, total, levels, level, ring):
    col = iota((count, total), 1)
    bits, level_bits = count.bit_length() - 1, levels.bit_length() - 1
    slot, ring_slot = (col >> bits) & (levels - 1), col >> (bits + level_bits)
    other = ((ring_slot ^ ring) * levels + (slot ^ level)) * count + (col & (count - 1))
    return other, (ring * levels + level) * count + iota((count, total), 0)


def bias(seen):
    return jnp.where(seen, 0.0, LOW)


def stack(refs, cut):
    return jnp.concatenate([ref[:, cut] for ref in refs], axis=0)


def repeat_table(rows, count):
    return (iota((rows, count), 0) // (rows // count) == iota((rows, count), 1)).astype(F32)


def gather_table(rows, count):
    return (iota((count, rows), 1) // (rows // count) == iota((count, rows), 0)).astype(F32)


def lane_offsets(offsets, heads):
    lane = iota((1, LANES), 1)
    values = jnp.zeros((1, LANES), jnp.int32)
    for head in range(heads):
        values = jnp.where(lane == head, offsets[head], values)
    return values


def column_kernel(levels, bits, *refs):
    pieces = refs[:levels]
    col_kv, col_qg = refs[levels : 2 + levels]
    pays = refs[2 + levels :]
    ring = lax.axis_index("seq")
    col_kv[...] = jnp.concatenate([piece[0] for piece in pieces], axis=0)
    col_qg[...] = jnp.concatenate([piece[1] for piece in pieces], axis=0)
    for bit in range(bits):
        upward = ((ring >> bit) & 1) == 0

        @pl.when(upward)
        def _():
            pays[bit][...] = col_kv[...]

        @pl.when(jnp.logical_not(upward))
        def _():
            pays[bit][...] = col_qg[...]


def cuts(at):
    low = slice(2 * at * LANES, (2 * at + 1) * LANES)
    return low, slice((2 * at + 1) * LANES, (2 * at + 2) * LANES)


def column_stats(scores, grads):
    peak = jnp.max(scores, axis=0, keepdims=True)
    weights = jnp.exp(scores - peak)
    total = jnp.sum(weights, axis=0, keepdims=True)
    return peak + jnp.log(total), jnp.sum(weights * grads, axis=0, keepdims=True) / total


def level_stats_kernel(scale, levels, mids, fars, *refs):
    kv, qg, far_own = refs[:3]
    mid_in, far_in = refs[3 : 3 + mids], refs[3 + mids : 3 + mids + fars]
    mlog, mdot, flog, fdot = refs[3 + mids + fars :][:4]
    backs = refs[7 + mids + fars :]
    step = pl.program_id(0)
    ring, level = lax.axis_index("seq"), lax.axis_index("lvl")
    mid_count, far_count = kv.shape[0], far_own.shape[1]
    total = mid_count * levels
    every = slice(None)

    @pl.when(step == 0)
    def _():
        for ref in (mlog, mdot, flog, fdot):
            ref[...] = jnp.zeros_like(ref)
        other, own = mid_places(mid_count, total, level)
        hide = bias(other <= own)
        for at in range(GROUP):
            low, high = cuts(at)
            scores = mm_t(qg[:, low], stack((kv,) + mid_in, low)) * scale + hide
            grads = mm_t(qg[:, high], stack((kv,) + mid_in, high))
            log_part, dot_part = row_stats(scores, grads)
            put_lane(mlog, every, at, log_part)
            put_lane(mdot, every, at, dot_part)

    @pl.when(step == 1)
    def _():
        other, own = mid_places(mid_count, mid_count, level)
        hide = bias(other <= own)
        for at in range(GROUP):
            low, high = cuts(at)
            scores = mm_t(qg[:, low], kv[:, low]) * scale + hide
            log_part, dot_part = row_stats(scores, mm_t(qg[:, high], kv[:, high]))
            put_lane(mlog, every, GROUP + at, log_part)
            put_lane(mdot, every, GROUP + at, dot_part)
            scores = mm_t(kv[:, low], stack(mid_in, low)) * scale
            log_part, dot_part = column_stats(scores, mm_t(kv[:, high], stack(mid_in, high)))
            for slot, back in enumerate(backs):
                where = slice(slot * mid_count, (slot + 1) * mid_count)
                back[at : at + 1, :] = log_part[:, where]
                back[GROUP + at : GROUP + at + 1, :] = dot_part[:, where]

    other, own = far_places(far_count, total, levels, level, ring)
    hide = bias(other <= own)
    for at in range(GROUP):
        head = step * GROUP + at
        low, high = cuts(at)
        scores = mm_t(far_own[1, :, low], stack(far_in, low)) * scale + hide
        grads = mm_t(far_own[1, :, high], stack(far_in, high))
        log_part, dot_part = row_stats(scores, grads)
        put_lane(flog, every, head, log_part)
        put_lane(fdot, every, head, dot_part)


def merge_kernel(heads, mids, *refs):
    mid_off, far_off, logs_a, dots_a, logs_b, dots_b, mlog, mdot, flog, fdot = refs[:10]
    backs = refs[10 : 10 + mids]
    outs = refs[10 + mids :]
    factors, shifts, mid_factor, mid_shift, far_factor, far_shift, mid_log, mid_dot = outs[:8]
    level = lax.axis_index("lvl")
    rows, mid_count, far_count = logs_a.shape[0], mlog.shape[0], flog.shape[0]

    lane = iota((mid_count, LANES), 1)
    theirs = (lane >= GROUP) & (lane < 2 * GROUP)
    logs, dots = [mlog[...]], [mdot[...]]
    head_rows, tail_rows = GROUP, LANES - 2 * GROUP
    for slot, back in enumerate(backs, 1):
        lower = theirs & ((iota((mid_count, LANES), 0) * 0 + (slot ^ level)) < level)
        parts = []
        for first in (0, GROUP):
            block = [jnp.zeros((head_rows, mid_count), F32), back[first : first + GROUP, :]]
            block.append(jnp.zeros((tail_rows, mid_count), F32))
            parts.append(jnp.concatenate(block, axis=0).T)
        logs.append(jnp.where(lower, parts[0], LOW))
        dots.append(parts[1])
    peak = functools.reduce(jnp.maximum, logs)
    weights = [jnp.exp(part - peak) for part in logs]
    whole = functools.reduce(jnp.add, weights)
    mid_logs = peak + jnp.log(whole)
    mid_dots = functools.reduce(jnp.add, [w * d for w, d in zip(weights, dots)]) / whole

    row = iota((rows, LANES), 0)
    mid_here = (row & (rows // mid_count - 1)) == lane_offsets(mid_off, heads)
    far_here = (row & (rows // far_count - 1)) == lane_offsets(far_off, heads)
    mid_table, far_table = repeat_table(rows, mid_count), repeat_table(rows, far_count)
    near, near_dots = logs_a[...] + logs_b[...], dots_a[...] + dots_b[...]
    mid = jnp.where(mid_here, exact(mid_table, mid_logs), LOW)
    far = jnp.where(far_here, exact(far_table, flog[...]), LOW)
    peak = jnp.maximum(near, jnp.maximum(mid, far))
    near_part = jnp.exp(near - peak)
    mid, far = jnp.exp(mid - peak), jnp.exp(far - peak)
    whole = near_part + mid + far
    logs = peak + jnp.log(whole)
    dots = (
        near_part * near_dots
        + mid * exact(mid_table, mid_dots)
        + far * exact(far_table, fdot[...])
    ) / whole
    factors[...] = jnp.exp(near - logs)
    shifts[...] = dots - near_dots
    for here, count, sent in ((mid_here, mid_count, outs[8]), (far_here, far_count, outs[9])):
        table = gather_table(rows, count)
        log_rows = exact(table, jnp.where(here, logs, 0.0))
        dot_rows = exact(table, jnp.where(here, dots, 0.0))
        sent[:heads, :] = log_rows.T[:heads, :]
        sent[heads:, :] = dot_rows.T[:heads, :]
        if count == mid_count:
            mid_log[...], mid_dot[...] = log_rows, dot_rows
            mid_factor[...] = jnp.exp(mid_logs - log_rows)
            mid_shift[...] = dot_rows - mid_dots
        else:
            far_factor[...] = jnp.exp(flog[...] - log_rows)
            far_shift[...] = dot_rows - fdot[...]


def row_side(scale, queries, cots, keys, vals, hide, logs, dots):
    scores = mm_t(queries, keys) * scale + hide
    soft = jnp.exp(scores - logs)
    slopes = soft * (mm_t(cots, vals) - dots)
    return soft.astype(BF16), slopes.astype(BF16)


def mid_queries(scale, levels, level, kv, qg, mid_in, mid_log, mid_dot, at, head):
    other, own = mid_places(kv.shape[0], kv.shape[0] * levels, level)
    low, high = cuts(at)
    keys, vals = stack((kv,) + mid_in, low), stack((kv,) + mid_in, high)
    logs, dots = pick_lane(mid_log, head), pick_lane(mid_dot, head)
    hide = bias(other <= own)
    _, slopes = row_side(scale, qg[:, low], qg[:, high], keys, vals, hide, logs, dots)
    return mm(slopes, keys)


def key_side(scale, keys, vals, queries, cots, hide, stats, head, heads):
    logs, dots = stats[pl.ds(head, 1), :], stats[pl.ds(head + heads, 1), :]
    soft, slopes = row_side(scale, keys, vals, queries, cots, hide, logs, dots)
    return jnp.concatenate([mm(slopes, queries), mm(soft, cots)], axis=1)


def mid_keys(scale, levels, level, kv, qg, mid_in, stats, at, head, heads):
    other, own = mid_places(kv.shape[0], kv.shape[0] * levels, level)
    low, high = cuts(at)
    queries, cots = stack((qg,) + mid_in, low), stack((qg,) + mid_in, high)
    return key_side(
        scale, kv[:, low], kv[:, high], queries, cots, bias(other >= own), stats, head, heads
    )


def level_base_kernel(scale, levels, mids, fars, *refs):
    kv, qg, far_own, mlog, mdot, flog, fdot = refs[:7]
    mid_in, far_in = refs[7 : 7 + mids], refs[7 + mids : 7 + mids + fars]
    mid_base, far_base = refs[7 + mids + fars :]
    step = pl.program_id(0)
    ring, level = lax.axis_index("seq"), lax.axis_index("lvl")
    far_count = far_own.shape[1]

    @pl.when(step == 0)
    def _():
        other, own = mid_places(kv.shape[0], kv.shape[0] * levels, level)
        hide = bias(other <= own)
        for at in range(GROUP):
            low, high = cuts(at)
            keys, vals = stack((kv,) + mid_in, low), stack((kv,) + mid_in, high)
            logs, dots = pick_lane(mlog, at), pick_lane(mdot, at)
            soft, slopes = row_side(scale, qg[:, low], qg[:, high], keys, vals, hide, logs, dots)
            mid_base[:, low] = mm(slopes, keys)
            mid_base[:, high] = mm(soft, keys)

    other, own = far_places(far_count, kv.shape[0] * levels, levels, level, ring)
    hide = bias(other <= own)
    for at in range(GROUP):
        head = step * GROUP + at
        low, high = cuts(at)
        keys, vals = stack(far_in, low), stack(far_in, high)
        logs, dots = pick_lane(flog, head), pick_lane(fdot, head)
        soft, slopes = row_side(
            scale, far_own[1, :, low], far_own[1, :, high], keys, vals, hide, logs, dots
        )
        far_base[:, low] = mm(slopes, keys)
        far_base[:, high] = mm(soft, keys)


def spread(rows, offsets, pieces):
    tables = []
    for offset, piece in zip(offsets, pieces):
        count = piece.shape[0]
        at = iota((rows, count), 0) - iota((rows, count), 1) * (rows // count)
        tables.append((at == offset).astype(BF16))
    table = tables[0] if len(tables) == 1 else jnp.concatenate(tables, axis=1)
    whole = pieces[0] if len(pieces) == 1 else jnp.concatenate(pieces, axis=0)
    return mm(table, whole.astype(BF16))


def rescaled(base, at, factors, shifts, head):
    low, high = cuts(at)
    return pick_lane(factors, head) * (base[:, low] - pick_lane(shifts, head) * base[:, high])


def near_grads_kernel(parts, group, mid_off, far_off, q, g, soft_in, slope_in, base, *refs):
    factors, shifts, mid_factor, mid_shift, far_factor, far_shift = refs[:6]
    mid_base, far_base, out_q, out_k, out_v = refs[6:]
    rows = q.shape[0]
    size = rows // parts
    for at in range(GROUP):
        head = group * GROUP + at
        cut = slice(at * LANES, (at + 1) * LANES)
        low, high = cuts(at)
        factor, shift = pick_lane(factors, head), pick_lane(shifts, head)
        far = rescaled(far_base, at, far_factor, far_shift, head)
        offsets, pieces = [far_off[head]], [far]
        if group == 0:
            offsets.insert(0, mid_off[head])
            pieces.insert(0, rescaled(mid_base, at, mid_factor, mid_shift, head))
        near = factor * (base[:, low] - shift * base[:, high])
        out_q[:, cut] = near + spread(rows, offsets, pieces)
        queries = factor * q[:, cut].astype(F32)
        shifted = (shift * queries).astype(BF16)
        queries = queries.astype(BF16)
        both = jnp.concatenate([(factor * g[:, cut].astype(F32)).astype(BF16), shifted], axis=1)
        for part in range(parts):
            keys = slice(part * size, (part + 1) * size)
            first = part * size
            value = mm(soft_in[at, keys, first:], both[first:])
            out_v[keys, cut] = value[:, :LANES]
            out_k[keys, cut] = mm(slope_in[at, keys, first:], queries[first:]) - value[:, LANES:]


def queries_kernel(scale, levels, mids, *refs):
    mid_off, kv, qg, dq_a, dq_b, mid_log, mid_dot = refs[:7]
    mid_in, out_q = refs[7 : 7 + mids], refs[7 + mids]
    level = lax.axis_index("lvl")
    rows = out_q.shape[0]

    @pl.when(pl.program_id(0) == 0)
    def _():
        out_q[...] = (dq_a[...] * scale).astype(BF16)

    @pl.when(pl.program_id(0) == 1)
    def _():
        for at in range(GROUP):
            head = GROUP + at
            cut = slice(at * LANES, (at + 1) * LANES)
            part = mid_queries(scale, levels, level, kv, qg, mid_in, mid_log, mid_dot, at, head)
            whole = dq_b[:, cut] + spread(rows, [mid_off[head]], [part])
            out_q[:, cut] = (whole * scale).astype(BF16)


def keys_kernel(scale, heads, levels, mids, fars, *refs):
    mid_off, far_off, kv, qg, far_own, dk_a, dv_a, dk_b, dv_b = refs[:9]
    first_in, second_in = refs[9 : 9 + mids], refs[9 + mids : 9 + 2 * mids]
    far_in = refs[9 + 2 * mids : 9 + 2 * mids + fars]
    stats = refs[9 + 2 * mids + fars : 10 + 3 * mids + fars]
    out_k, out_v, mid_rows, far_rows = refs[10 + 3 * mids + fars :]
    step = pl.program_id(0)
    ring, level = lax.axis_index("seq"), lax.axis_index("lvl")
    rows = out_k.shape[0]
    mid_count, far_count = kv.shape[0], far_own.shape[1]

    @pl.when(step == 0)
    def _():
        mid_rows[...] = jnp.concatenate([ref[:, :mid_count] for ref in stats], axis=1)
        for slot in range(fars):
            source = mid_count + (slot // 2 + slot % 2 * (fars // 2)) * far_count
            for low, ref in enumerate(stats):
                place = (slot * levels + low) * far_count
                far_rows[:, place : place + far_count] = ref[:, source : source + far_count]

    other, own = far_places(far_count, mid_count * levels, levels, level, ring)
    hide = bias(other >= own)

    def finish(group, mid_in, dk, dv):
        for at in range(GROUP):
            head = group * GROUP + at
            cut = slice(at * LANES, (at + 1) * LANES)
            low, high = cuts(at)
            mid = mid_keys(scale, levels, level, kv, qg, mid_in, mid_rows, at, head, heads)
            queries, cots = stack(far_in, low), stack(far_in, high)
            keys, vals = far_own[0, :, low], far_own[0, :, high]
            far = key_side(scale, keys, vals, queries, cots, hide, far_rows, head, heads)
            whole = spread(rows, [mid_off[head], far_off[head]], [mid, far])
            out_k[:, cut] = ((dk[:, cut] + whole[:, :LANES]) * scale).astype(BF16)
            out_v[:, cut] = (dv[:, cut] + whole[:, LANES:]).astype(BF16)

    @pl.when(step == 0)
    def _():
        finish(0, second_in, dk_a, dv_a)

    @pl.when(step == 1)
    def _():
        finish(1, first_in, dk_b, dv_b)


def pack_kernel(*refs):
    out, first = refs[-1], 0
    for ref in refs[:-1]:
        out[:, first : first + ref.shape[1]] = ref[...]
        first += ref.shape[1]


def pack(pieces):
    width = sum(piece.shape[1] for piece in pieces)
    out = jax.ShapeDtypeStruct((pieces[0].shape[0], width), F32)
    ins = [(fixed(piece.shape), piece) for piece in pieces]
    return call(pack_kernel, 1, ins, [(fixed(out.shape), out)], [])[0]


def swap(array, axis, size, step):
    return lax.ppermute(array, axis, [(i, i ^ step) for i in range(size)])


def call(kernel, steps, ins, outs, scratch, limit=LIMIT):
    specs, arrays = zip(*ins)
    out_specs, out_shapes = zip(*outs)
    return pl.pallas_call(
        kernel,
        grid=(steps,),
        in_specs=list(specs),
        out_specs=list(out_specs),
        out_shape=list(out_shapes),
        scratch_shapes=scratch,
        compiler_params=params(limit),
        cost_estimate=pl.CostEstimate(flops=0, bytes_accessed=0, transcendentals=0),
    )(*arrays)


def local(queries, keys, values, grad_out, mid_offset, far_offset):
    rows, flat = queries.shape
    heads = mid_offset.shape[0]
    width = flat // heads
    scale = width ** (-0.5)
    levels, rings = lax.axis_size("lvl"), lax.axis_size("seq")
    mid_count, far_count = rows // levels, rows // (levels * rings)
    block = far_count * levels
    shape = jax.ShapeDtypeStruct
    parts = 2
    steps = heads // GROUP
    tile = columns(rows, GROUP * width)
    mid_spec = columns(mid_count, GROUP * 2 * width)
    far_spec = pl.BlockSpec((2, far_count, GROUP * 2 * width), lambda h: (0, 0, h))
    sources = [(tile, queries), (tile, keys), (tile, values), (tile, grad_out)]
    scalars = [(smem(), mid_offset), (smem(), far_offset)]
    mid_shape = shape((mid_count, 2 * flat), BF16)

    half_shape, half_spec = shape((mid_count, flat), BF16), fixed((mid_count, flat))
    mids = levels - 1

    kv, qg, far, *pays = call(
        select_kernel,
        steps,
        scalars + [(spec, pltpu.with_memory_space_constraint(x, pltpu.HBM)) for spec, x in sources],
        [(mid_spec, mid_shape)] * 2
        + [(far_spec, shape((2, far_count, 2 * flat), BF16))]
        + [(half_spec, half_shape)] * (2 * mids),
        [],
    )
    far_level = [far] + [swap(far, "lvl", levels, step) for step in range(1, levels)]
    first_in = [swap(pays[step - 1], "lvl", levels, step) for step in range(1, levels)]

    stat, stat_spec = shape((rows, LANES), F32), fixed((rows, LANES))
    half = shape((rows, flat // 2), F32)
    square = shape((GROUP, rows, rows), BF16)

    def group_tile(group):
        return pl.BlockSpec((rows, GROUP * width), lambda h: (0, group))

    def group_sources(group, arrays):
        return [(group_tile(group), array) for array in arrays]

    def whole(array):
        return (fixed(array.shape), array)

    def result(*dims):
        return (fixed(dims), shape(dims, F32))

    def near_call(group, arrays):
        return call(
            functools.partial(near_kernel, scale, parts, group),
            1,
            group_sources(group, arrays),
            [(stat_spec, stat)] * 2
            + [(fixed(square.shape), square)] * 2
            + [result(rows, flat)],
            [],
        )

    inputs = (queries, keys, values, grad_out)
    near_a = near_call(0, inputs)
    far_level, near_a = lax.optimization_barrier((far_level, near_a))
    ring_bits = rings.bit_length() - 1
    col_shape = shape((block, 2 * flat), BF16)
    col_kv, col_qg, *ring_pays = call(
        functools.partial(column_kernel, levels, ring_bits),
        1,
        [(fixed(piece.shape), piece) for piece in far_level],
        [(fixed(col_shape.shape), col_shape)] * (2 + ring_bits),
        [],
    )
    far_ring = [None] * rings
    for step in range(2, rings, 2):
        far_ring[step] = swap(ring_pays[step.bit_length() - 1], "seq", rings, step)
    inputs, col_kv = lax.optimization_barrier((inputs, col_kv))
    near_b = near_call(1, inputs)
    far_ring[2::2], near_b = lax.optimization_barrier((far_ring[2::2], near_b))
    far_ring[1] = swap(ring_pays[0], "seq", rings, 1)
    for step in range(3, rings, 2):
        far_ring[step] = swap(far_ring[step - 1], "seq", rings, 1)

    col_spec = columns(block, GROUP * 2 * width)
    first_list = [(half_spec, piece) for piece in first_in]
    far_rest = [(col_spec, piece) for piece in far_ring[1:]]
    far_kv, far_qg = [(col_spec, col_kv)] + far_rest, [(col_spec, col_qg)] + far_rest
    mid_own = [(mid_spec, kv), (mid_spec, qg)]
    own = mid_own + [(far_spec, far)]
    mid_stat, far_stat = result(mid_count, LANES), result(far_count, LANES)
    level_stats = call(
        functools.partial(level_stats_kernel, scale, levels, mids, rings),
        steps,
        own + first_list + far_kv,
        [mid_stat] * 2 + [far_stat] * 2 + [result(2 * GROUP, mid_count)] * mids,
        [],
    )
    backs = [swap(level_stats[3 + step], "lvl", levels, step) for step in range(1, levels)]
    level_stats = level_stats[:4]
    later, backs = lax.optimization_barrier((pays[mids + 1 :], backs))
    second = [pays[mids]] + list(later)
    second[0], first_in[-1] = lax.optimization_barrier((second[0], first_in[-1]))
    second_in = [swap(second[step - 1], "lvl", levels, step) for step in range(1, levels)]
    second_list = [(half_spec, piece) for piece in second_in]
    mid_base, far_base = call(
        functools.partial(level_base_kernel, scale, levels, mids, rings),
        steps,
        own + [whole(array) for array in level_stats] + first_list + far_kv,
        [
            (fixed((mid_count, flat)), shape((mid_count, flat), F32)),
            (columns(far_count, GROUP * 2 * width), shape((far_count, 2 * flat), F32)),
        ],
        [],
    )
    backs, mid_base = lax.optimization_barrier((backs, mid_base))
    merged = call(
        functools.partial(merge_kernel, heads, mids),
        1,
        scalars + [whole(array) for array in [*near_a[:2], *near_b[:2], *level_stats, *backs]],
        [(stat_spec, stat)] * 2
        + [mid_stat] * 2
        + [far_stat] * 2
        + [mid_stat] * 2
        + [result(2 * heads, mid_count), result(2 * heads, far_count)],
        [],
    )
    mid_log, mid_dot, mid_sent, far_sent = merged[6:]
    near_sent = [far_sent] + [swap(far_sent, "seq", rings, step) for step in range(2, rings, 2)]

    def near_grads(group, near):
        far_spec = pl.BlockSpec((far_count, GROUP * 2 * width), lambda h: (0, group))
        return call(
            functools.partial(near_grads_kernel, parts, group),
            1,
            scalars
            + group_sources(group, (queries, grad_out))
            + [whole(array) for array in near[2:]]
            + [whole(array) for array in merged[:6]]
            + [whole(mid_base), (far_spec, far_base)],
            [result(rows, flat // 2)] * 3,
            [],
        )

    grads_a = near_grads(0, near_a)
    near_sent, grads_a = lax.optimization_barrier((near_sent, grads_a))
    near_sent = pack(near_sent)
    other_sent = swap(near_sent, "seq", rings, 1)
    grads_b = near_grads(1, near_b)
    other_sent, grads_b = lax.optimization_barrier((other_sent, grads_b))
    sent = pack([mid_sent, near_sent, other_sent])
    sent_in = [sent] + [swap(sent, "lvl", levels, step) for step in range(1, levels)]
    out = shape((rows, flat), BF16)
    group_mid = pl.BlockSpec((mid_count, GROUP * 2 * width), lambda h: (0, 1))
    (grad_query,) = call(
        functools.partial(queries_kernel, scale, levels, mids),
        steps,
        scalars[:1]
        + [(group_mid, kv), (group_mid, qg)]
        + [whole(array) for array in (grads_a[0], grads_b[0], mid_log, mid_dot)]
        + second_list,
        [(tile, out)],
        [],
    )
    sent_in, grad_query = lax.optimization_barrier((sent_in, grad_query))
    grad_key, grad_value = call(
        functools.partial(keys_kernel, scale, heads, levels, mids, rings),
        steps,
        scalars
        + own
        + [whole(array) for array in (*grads_a[1:], *grads_b[1:])]
        + first_list
        + second_list
        + far_qg
        + [whole(piece) for piece in sent_in],
        [(tile, out)] * 2,
        [pltpu.VMEM((2 * heads, rows), F32)] * 2,
    )
    return grad_query, grad_key, grad_value


def solution(mesh):
    row_spec = P(("seq", "lvl"), None)
    return jax.shard_map(
        local,
        mesh=mesh,
        in_specs=(row_spec, row_spec, row_spec, row_spec, P(), P()),
        out_specs=(row_spec, row_spec, row_spec),
        check_vma=False,
    )
```

```python
import functools

import jax
import jax.numpy as jnp
from jax import lax
from jax.experimental import pallas as pl
from jax.experimental.pallas import tpu as pltpu
from jax.sharding import PartitionSpec as P

F32 = jnp.float32
BF16 = jnp.bfloat16
LANES = 128
LOW = -1e30
MIB = 1024 * 1024
GROUP = 4
LIMIT = 22


def mm(a, b):
    return lax.dot_general(a, b, (((1,), (0,)), ((), ())), preferred_element_type=F32)


def mm_t(a, b):
    return lax.dot_general(a, b, (((1,), (1,)), ((), ())), preferred_element_type=F32)


def t_mm(a, b):
    return lax.dot_general(a, b, (((0,), (0,)), ((), ())), preferred_element_type=F32)


def exact(a, b):
    return lax.dot_general(
        a, b, (((1,), (0,)), ((), ())), preferred_element_type=F32, precision=lax.Precision.HIGHEST
    )


def iota(shape, axis):
    return lax.broadcasted_iota(jnp.int32, shape, axis)


def params(limit):
    return pltpu.CompilerParams(
        vmem_limit_bytes=limit * MIB, dimension_semantics=("arbitrary",)
    )


def smem():
    return pl.BlockSpec(memory_space=pltpu.SMEM)


def columns(rows, width):
    return pl.BlockSpec((rows, width), lambda h: (0, h))


def fixed(shape):
    return pl.BlockSpec(shape, lambda h: (0,) * len(shape))


def pick_lane(ref, head):
    block = ref[...]
    return jnp.sum(jnp.where(iota(block.shape, 1) == head, block, 0.0), axis=1, keepdims=True)


def put_lane(ref, rows, head, value):
    block = ref[rows, :]
    ref[rows, :] = jnp.where(iota(block.shape, 1) == head, value, block)


def select_kernel(mid_off, far_off, q, k, v, g, kv, qg, far, *pays):
    level = lax.axis_index("lvl")
    rows = q.shape[0]
    for at in range(GROUP):
        head = pl.program_id(0) * GROUP + at
        cut = slice(at * LANES, (at + 1) * LANES)
        wide = slice(2 * at * LANES, 2 * (at + 1) * LANES)
        whole = jnp.concatenate([k[:, cut], v[:, cut], q[:, cut], g[:, cut]], axis=1)

        def picked(count, offset):
            stride = rows // count
            table = iota((count, rows), 1) == iota((count, rows), 0) * stride + offset
            return mm(table.astype(BF16), whole).astype(BF16)

        mid = picked(kv.shape[0], mid_off[head])
        half = 2 * LANES
        kv[:, wide] = mid[:, :half]
        qg[:, wide] = mid[:, half:]
        picks = picked(far.shape[1], far_off[head])
        far[0, :, wide] = picks[:, :half]
        far[1, :, wide] = picks[:, half:]
    firsts, seconds = pays[: len(pays) // 2], pays[len(pays) // 2 :]
    for step, (first, second) in enumerate(zip(firsts, seconds), 1):
        upward = (level ^ step) > level

        @pl.when(upward & (pl.program_id(0) == 0))
        def _():
            first[...] = kv[...]

        @pl.when(upward & (pl.program_id(0) == 1))
        def _():
            second[...] = kv[...]

        @pl.when(jnp.logical_not(upward) & (pl.program_id(0) == 0))
        def _():
            second[...] = qg[...]

        @pl.when(jnp.logical_not(upward) & (pl.program_id(0) == 1))
        def _():
            first[...] = qg[...]


def near_kernel(scale, parts, group, q, k, v, g, logs, dots, soft_out, slope_out, base):
    logs[...] = jnp.zeros_like(logs)
    dots[...] = jnp.zeros_like(dots)
    size = q.shape[0] // parts
    for at in range(GROUP):
        cut = slice(at * LANES, (at + 1) * LANES)
        low, high = cuts(at)
        for part in range(parts):
            rows = slice(part * size, (part + 1) * size)
            width = (part + 1) * size
            scores = mm_t(q[rows, cut], k[:width, cut]) * scale
            grads = mm_t(g[rows, cut], v[:width, cut])
            seen = iota((size, width), 1) <= iota((size, width), 0) + part * size
            scores = jnp.where(seen, scores, LOW)
            peak = jnp.max(scores, axis=1, keepdims=True)
            weights = jnp.exp(scores - peak)
            total = jnp.sum(weights, axis=1, keepdims=True)
            soft = weights / total
            dot_part = jnp.sum(soft * grads, axis=1, keepdims=True)
            slopes = (soft * (grads - dot_part)).astype(BF16)
            soft = soft.astype(BF16)
            base[rows, low] = mm(slopes, k[:width, cut])
            base[rows, high] = mm(soft, k[:width, cut])
            soft_out[at, :width, rows] = soft.T
            slope_out[at, :width, rows] = slopes.T
            put_lane(logs, rows, group * GROUP + at, peak + jnp.log(total))
            put_lane(dots, rows, group * GROUP + at, dot_part)


def row_stats(scores, grads):
    peak = jnp.max(scores, axis=1, keepdims=True)
    weights = jnp.exp(scores - peak)
    total = jnp.sum(weights, axis=1, keepdims=True)
    return peak + jnp.log(total), jnp.sum(weights * grads, axis=1, keepdims=True) / total


def mid_places(count, total, level):
    col = iota((count, total), 1)
    other = ((col >> (count.bit_length() - 1)) ^ level) * count + (col & (count - 1))
    return other, level * count + iota((count, total), 0)


def far_places(count, total, levels, level, ring):
    col = iota((count, total), 1)
    bits, level_bits = count.bit_length() - 1, levels.bit_length() - 1
    slot, ring_slot = (col >> bits) & (levels - 1), col >> (bits + level_bits)
    evens = total >> (bits + level_bits + 1)
    ring_slot = (ring_slot & (evens - 1)) * 2 + (ring_slot >> (evens.bit_length() - 1))
    other = ((ring_slot ^ ring) * levels + (slot ^ level)) * count + (col & (count - 1))
    return other, (ring * levels + level) * count + iota((count, total), 0)


def bias(seen):
    return jnp.where(seen, 0.0, LOW)


def stack(refs, cut):
    return jnp.concatenate([ref[:, cut] for ref in refs], axis=0)


def repeat_table(rows, count):
    return (iota((rows, count), 0) // (rows // count) == iota((rows, count), 1)).astype(F32)


def gather_table(rows, count):
    return (iota((count, rows), 1) // (rows // count) == iota((count, rows), 0)).astype(F32)


def lane_offsets(offsets, heads):
    lane = iota((1, LANES), 1)
    values = jnp.zeros((1, LANES), jnp.int32)
    for head in range(heads):
        values = jnp.where(lane == head, offsets[head], values)
    return values


def column_kernel(levels, bits, *refs):
    pieces = refs[:levels]
    col_kv, col_qg = refs[levels : 2 + levels]
    pays = refs[2 + levels :]
    ring = lax.axis_index("seq")
    col_kv[...] = jnp.concatenate([piece[0] for piece in pieces], axis=0)
    col_qg[...] = jnp.concatenate([piece[1] for piece in pieces], axis=0)
    for bit in range(bits):
        upward = ((ring >> bit) & 1) == 0

        @pl.when(upward)
        def _():
            pays[bit][...] = col_kv[...]

        @pl.when(jnp.logical_not(upward))
        def _():
            pays[bit][...] = col_qg[...]


def cuts(at):
    low = slice(2 * at * LANES, (2 * at + 1) * LANES)
    return low, slice((2 * at + 1) * LANES, (2 * at + 2) * LANES)


def column_stats(scores, grads):
    peak = jnp.max(scores, axis=0, keepdims=True)
    weights = jnp.exp(scores - peak)
    total = jnp.sum(weights, axis=0, keepdims=True)
    return peak + jnp.log(total), jnp.sum(weights * grads, axis=0, keepdims=True) / total


def mid_stats_kernel(scale, levels, mids, *refs):
    kv, qg = refs[:2]
    mid_in = refs[2 : 2 + mids]
    mlog, mdot = refs[2 + mids : 4 + mids]
    backs = refs[4 + mids :]
    step = pl.program_id(0)
    level = lax.axis_index("lvl")
    mid_count = kv.shape[0]
    every = slice(None)

    @pl.when(step == 0)
    def _():
        for ref in (mlog, mdot):
            ref[...] = jnp.zeros_like(ref)
        other, own = mid_places(mid_count, mid_count * levels, level)
        hide = bias(other <= own)
        for at in range(GROUP):
            low, high = cuts(at)
            scores = mm_t(qg[:, low], stack((kv,) + mid_in, low)) * scale + hide
            grads = mm_t(qg[:, high], stack((kv,) + mid_in, high))
            log_part, dot_part = row_stats(scores, grads)
            put_lane(mlog, every, at, log_part)
            put_lane(mdot, every, at, dot_part)

    @pl.when(step == 1)
    def _():
        other, own = mid_places(mid_count, mid_count, level)
        hide = bias(other <= own)
        for at in range(GROUP):
            low, high = cuts(at)
            scores = mm_t(qg[:, low], kv[:, low]) * scale + hide
            log_part, dot_part = row_stats(scores, mm_t(qg[:, high], kv[:, high]))
            put_lane(mlog, every, GROUP + at, log_part)
            put_lane(mdot, every, GROUP + at, dot_part)
            scores = mm_t(kv[:, low], stack(mid_in, low)) * scale
            log_part, dot_part = column_stats(scores, mm_t(kv[:, high], stack(mid_in, high)))
            for slot, back in enumerate(backs):
                where = slice(slot * mid_count, (slot + 1) * mid_count)
                back[at : at + 1, :] = log_part[:, where]
                back[GROUP + at : GROUP + at + 1, :] = dot_part[:, where]


def merge_kernel(heads, mids, *refs):
    mid_off, far_off, logs_a, dots_a, logs_b, dots_b, mlog, mdot, flog, fdot = refs[:10]
    backs = refs[10 : 10 + mids]
    outs = refs[10 + mids :]
    factors, shifts, mid_factor, mid_shift, far_factor, far_shift, mid_log, mid_dot = outs[:8]
    level = lax.axis_index("lvl")
    rows, mid_count, far_count = logs_a.shape[0], mlog.shape[0], flog.shape[0]

    lane = iota((mid_count, LANES), 1)
    theirs = (lane >= GROUP) & (lane < 2 * GROUP)
    logs, dots = [mlog[...]], [mdot[...]]
    head_rows, tail_rows = GROUP, LANES - 2 * GROUP
    for slot, back in enumerate(backs, 1):
        lower = theirs & ((iota((mid_count, LANES), 0) * 0 + (slot ^ level)) < level)
        parts = []
        for first in (0, GROUP):
            block = [jnp.zeros((head_rows, mid_count), F32), back[first : first + GROUP, :]]
            block.append(jnp.zeros((tail_rows, mid_count), F32))
            parts.append(jnp.concatenate(block, axis=0).T)
        logs.append(jnp.where(lower, parts[0], LOW))
        dots.append(parts[1])
    peak = functools.reduce(jnp.maximum, logs)
    weights = [jnp.exp(part - peak) for part in logs]
    whole = functools.reduce(jnp.add, weights)
    mid_logs = peak + jnp.log(whole)
    mid_dots = functools.reduce(jnp.add, [w * d for w, d in zip(weights, dots)]) / whole

    row = iota((rows, LANES), 0)
    mid_here = (row & (rows // mid_count - 1)) == lane_offsets(mid_off, heads)
    far_here = (row & (rows // far_count - 1)) == lane_offsets(far_off, heads)
    mid_wide = exact(repeat_table(rows, mid_count), jnp.concatenate([mid_logs, mid_dots], axis=1))
    far_wide = exact(repeat_table(rows, far_count), jnp.concatenate([flog[...], fdot[...]], axis=1))
    near, near_dots = logs_a[...] + logs_b[...], dots_a[...] + dots_b[...]
    mid = jnp.where(mid_here, mid_wide[:, :LANES], LOW)
    far = jnp.where(far_here, far_wide[:, :LANES], LOW)
    peak = jnp.maximum(near, jnp.maximum(mid, far))
    near_part = jnp.exp(near - peak)
    mid, far = jnp.exp(mid - peak), jnp.exp(far - peak)
    whole = near_part + mid + far
    logs = peak + jnp.log(whole)
    dots = (
        near_part * near_dots
        + mid * mid_wide[:, LANES:]
        + far * far_wide[:, LANES:]
    ) / whole
    factors[...] = jnp.exp(near - logs)
    shifts[...] = dots - near_dots
    for here, count, sent in ((mid_here, mid_count, outs[8]), (far_here, far_count, outs[9])):
        table = gather_table(rows, count)
        chosen = [jnp.where(here, logs, 0.0), jnp.where(here, dots, 0.0)]
        chosen = exact(table, jnp.concatenate(chosen, axis=1))
        log_rows, dot_rows = chosen[:, :LANES], chosen[:, LANES:]
        sent[:heads, :] = log_rows.T[:heads, :]
        sent[heads:, :] = dot_rows.T[:heads, :]
        if count == mid_count:
            mid_log[...], mid_dot[...] = log_rows, dot_rows
            mid_factor[...] = jnp.exp(mid_logs - log_rows)
            mid_shift[...] = dot_rows - mid_dots
        else:
            far_factor[...] = jnp.exp(flog[...] - log_rows)
            far_shift[...] = dot_rows - fdot[...]


def row_side(scale, queries, cots, keys, vals, hide, logs, dots):
    scores = mm_t(queries, keys) * scale + hide
    soft = jnp.exp(scores - logs)
    slopes = soft * (mm_t(cots, vals) - dots)
    return soft.astype(BF16), slopes.astype(BF16)


def mid_queries(scale, levels, level, kv, qg, mid_in, mid_log, mid_dot, at, head):
    other, own = mid_places(kv.shape[0], kv.shape[0] * levels, level)
    low, high = cuts(at)
    keys, vals = stack((kv,) + mid_in, low), stack((kv,) + mid_in, high)
    logs, dots = pick_lane(mid_log, head), pick_lane(mid_dot, head)
    hide = bias(other <= own)
    _, slopes = row_side(scale, qg[:, low], qg[:, high], keys, vals, hide, logs, dots)
    return mm(slopes, keys)


def key_side(scale, keys, vals, queries, cots, hide, stats, head, heads):
    logs, dots = stats[pl.ds(head, 1), :], stats[pl.ds(head + heads, 1), :]
    soft, slopes = row_side(scale, keys, vals, queries, cots, hide, logs, dots)
    return jnp.concatenate([mm(slopes, queries), mm(soft, cots)], axis=1)


def mid_keys(scale, levels, level, kv, qg, mid_in, stats, at, head, heads):
    other, own = mid_places(kv.shape[0], kv.shape[0] * levels, level)
    low, high = cuts(at)
    queries, cots = stack((qg,) + mid_in, low), stack((qg,) + mid_in, high)
    return key_side(
        scale, kv[:, low], kv[:, high], queries, cots, bias(other >= own), stats, head, heads
    )


def level_base_kernel(scale, levels, mids, fars, *refs):
    kv, qg, far_own, mlog, mdot = refs[:5]
    mid_in, far_in = refs[5 : 5 + mids], refs[5 + mids : 5 + mids + fars]
    mid_base, far_base, flog, fdot = refs[5 + mids + fars :]
    step = pl.program_id(0)
    ring, level = lax.axis_index("seq"), lax.axis_index("lvl")
    far_count = far_own.shape[1]
    every = slice(None)

    @pl.when(step == 0)
    def _():
        for ref in (flog, fdot):
            ref[...] = jnp.zeros_like(ref)
        other, own = mid_places(kv.shape[0], kv.shape[0] * levels, level)
        hide = bias(other <= own)
        for at in range(GROUP):
            low, high = cuts(at)
            keys, vals = stack((kv,) + mid_in, low), stack((kv,) + mid_in, high)
            logs, dots = pick_lane(mlog, at), pick_lane(mdot, at)
            soft, slopes = row_side(scale, qg[:, low], qg[:, high], keys, vals, hide, logs, dots)
            mid_base[:, low] = mm(slopes, keys)
            mid_base[:, high] = mm(soft, keys)

    other, own = far_places(far_count, kv.shape[0] * levels, levels, level, ring)
    hide = bias(other <= own)
    for at in range(GROUP):
        head = step * GROUP + at
        low, high = cuts(at)
        keys = stack(far_in, low)
        scores = mm_t(far_own[1, :, low], keys) * scale + hide
        grads = mm_t(far_own[1, :, high], stack(far_in, high))
        peak = jnp.max(scores, axis=1, keepdims=True)
        weights = jnp.exp(scores - peak)
        total = jnp.sum(weights, axis=1, keepdims=True)
        soft = weights / total
        dots = jnp.sum(soft * grads, axis=1, keepdims=True)
        put_lane(flog, every, head, peak + jnp.log(total))
        put_lane(fdot, every, head, dots)
        far_base[:, low] = mm((soft * (grads - dots)).astype(BF16), keys)
        far_base[:, high] = mm(soft.astype(BF16), keys)


def put_rows(ref, at, offset, piece):
    count = piece.shape[0]
    rows = pl.ds(offset, count, stride=ref.shape[1] // count)
    ref[at, rows, :] += piece


def rescaled(base, at, factors, shifts, head):
    low, high = cuts(at)
    return pick_lane(factors, head) * (base[:, low] - pick_lane(shifts, head) * base[:, high])


def near_grads_kernel(parts, group, mid_off, far_off, q, g, soft_in, slope_in, base, *refs):
    factors, shifts, mid_factor, mid_shift, far_factor, far_shift = refs[:6]
    mid_base, far_base, out_q, out_k, out_v, work = refs[6:]
    rows = q.shape[0]
    size = rows // parts
    for at in range(GROUP):
        head = group * GROUP + at
        cut = slice(at * LANES, (at + 1) * LANES)
        low, high = cuts(at)
        factor, shift = pick_lane(factors, head), pick_lane(shifts, head)
        far = rescaled(far_base, at, far_factor, far_shift, head)
        work[at] = factor * (base[:, low] - shift * base[:, high])
        put_rows(work, at, far_off[head], far)
        if group == 0:
            mid = rescaled(mid_base, at, mid_factor, mid_shift, head)
            put_rows(work, at, mid_off[head], mid)
        out_q[:, cut] = work[at]
        queries = factor * q[:, cut].astype(F32)
        shifted = (shift * queries).astype(BF16)
        queries = queries.astype(BF16)
        both = jnp.concatenate([(factor * g[:, cut].astype(F32)).astype(BF16), shifted], axis=1)
        for part in range(parts):
            keys = slice(part * size, (part + 1) * size)
            first = part * size
            value = mm(soft_in[at, keys, first:], both[first:])
            out_v[keys, cut] = value[:, :LANES]
            out_k[keys, cut] = mm(slope_in[at, keys, first:], queries[first:]) - value[:, LANES:]


def queries_kernel(scale, levels, mids, *refs):
    mid_off, kv, qg, dq_a, dq_b, mid_log, mid_dot = refs[:7]
    mid_in, out_q, work = refs[7 : 7 + mids], refs[7 + mids], refs[8 + mids]
    level = lax.axis_index("lvl")

    @pl.when(pl.program_id(0) == 0)
    def _():
        out_q[...] = (dq_a[...] * scale).astype(BF16)

    @pl.when(pl.program_id(0) == 1)
    def _():
        for at in range(GROUP):
            head = GROUP + at
            cut = slice(at * LANES, (at + 1) * LANES)
            part = mid_queries(scale, levels, level, kv, qg, mid_in, mid_log, mid_dot, at, head)
            work[at] = dq_b[:, cut]
            put_rows(work, at, mid_off[head], part)
            out_q[:, cut] = (work[at] * scale).astype(BF16)


def keys_kernel(scale, heads, levels, rings, mids, fars, *refs):
    mid_off, far_off, kv, qg, far_own, dk_a, dv_a, dk_b, dv_b = refs[:9]
    first_in, second_in = refs[9 : 9 + mids], refs[9 + mids : 9 + 2 * mids]
    far_in = refs[9 + 2 * mids : 9 + 2 * mids + fars]
    stats = refs[9 + 2 * mids + fars : 10 + 3 * mids + fars]
    out_k, out_v, mid_rows, far_rows, work = refs[10 + 3 * mids + fars :]
    step = pl.program_id(0)
    ring, level = lax.axis_index("seq"), lax.axis_index("lvl")
    mid_count, far_count = kv.shape[0], far_own.shape[1]

    @pl.when(step == 0)
    def _():
        mid_rows[...] = jnp.concatenate([ref[:, :mid_count] for ref in stats], axis=1)
        for slot in range(rings):
            source = mid_count + slot * far_count
            for low, ref in enumerate(stats):
                place = (slot * levels + low) * far_count
                far_rows[:, place : place + far_count] = ref[:, source : source + far_count]

    other, own = far_places(far_count, mid_count * levels, levels, level, ring)
    hide = bias(other >= own)

    def finish(group, mid_in, dk, dv):
        for at in range(GROUP):
            head = group * GROUP + at
            cut = slice(at * LANES, (at + 1) * LANES)
            low, high = cuts(at)
            mid = mid_keys(scale, levels, level, kv, qg, mid_in, mid_rows, at, head, heads)
            queries, cots = stack(far_in, low), stack(far_in, high)
            keys, vals = far_own[0, :, low], far_own[0, :, high]
            far = key_side(scale, keys, vals, queries, cots, hide, far_rows, head, heads)
            one, two = 2 * at, 2 * at + 1
            work[one], work[two] = dk[:, cut], dv[:, cut]
            for where, first in ((one, 0), (two, LANES)):
                put_rows(work, where, mid_off[head], mid[:, first : first + LANES])
                put_rows(work, where, far_off[head], far[:, first : first + LANES])
            out_k[:, cut] = (work[one] * scale).astype(BF16)
            out_v[:, cut] = work[two].astype(BF16)

    @pl.when(step == 0)
    def _():
        finish(0, second_in, dk_a, dv_a)

    @pl.when(step == 1)
    def _():
        finish(1, first_in, dk_b, dv_b)


def join_kernel(*refs):
    out, first = refs[-1], 0
    for ref in refs[:-2]:
        out[first : first + ref.shape[0], :] = ref[...]
        first += ref.shape[0]


def join(pieces, after):
    rows = sum(piece.shape[0] for piece in pieces)
    out = jax.ShapeDtypeStruct((rows, pieces[0].shape[1]), BF16)
    ins = [(fixed(piece.shape), piece) for piece in pieces + [after]]
    return call(join_kernel, 1, ins, [(fixed(out.shape), out)], [])[0]


def pack_kernel(*refs):
    out, first = refs[-1], 0
    for ref in refs[:-1]:
        out[:, first : first + ref.shape[1]] = ref[...]
        first += ref.shape[1]


def pack(pieces):
    width = sum(piece.shape[1] for piece in pieces)
    out = jax.ShapeDtypeStruct((pieces[0].shape[0], width), F32)
    ins = [(fixed(piece.shape), piece) for piece in pieces]
    return call(pack_kernel, 1, ins, [(fixed(out.shape), out)], [])[0]


def swap(array, axis, size, step):
    return lax.ppermute(array, axis, [(i, i ^ step) for i in range(size)])


def call(kernel, steps, ins, outs, scratch, limit=LIMIT, flops=0):
    specs, arrays = zip(*ins)
    out_specs, out_shapes = zip(*outs)
    return pl.pallas_call(
        kernel,
        grid=(steps,),
        in_specs=list(specs),
        out_specs=list(out_specs),
        out_shape=list(out_shapes),
        scratch_shapes=scratch,
        compiler_params=params(limit),
        cost_estimate=pl.CostEstimate(flops=flops, bytes_accessed=0, transcendentals=0),
    )(*arrays)


def local(queries, keys, values, grad_out, mid_offset, far_offset):
    rows, flat = queries.shape
    heads = mid_offset.shape[0]
    width = flat // heads
    scale = width ** (-0.5)
    levels, rings = lax.axis_size("lvl"), lax.axis_size("seq")
    mid_count, far_count = rows // levels, rows // (levels * rings)
    block = far_count * levels
    shape = jax.ShapeDtypeStruct
    parts = 2
    steps = heads // GROUP
    tile = columns(rows, GROUP * width)
    mid_spec = columns(mid_count, GROUP * 2 * width)
    far_spec = pl.BlockSpec((2, far_count, GROUP * 2 * width), lambda h: (0, 0, h))
    sources = [(tile, queries), (tile, keys), (tile, values), (tile, grad_out)]
    scalars = [(smem(), mid_offset), (smem(), far_offset)]
    mid_shape = shape((mid_count, 2 * flat), BF16)

    half_shape, half_spec = shape((mid_count, flat), BF16), fixed((mid_count, flat))
    mids = levels - 1

    kv, qg, far, *pays = call(
        select_kernel,
        steps,
        scalars + [(spec, pltpu.with_memory_space_constraint(x, pltpu.HBM)) for spec, x in sources],
        [(mid_spec, mid_shape)] * 2
        + [(far_spec, shape((2, far_count, 2 * flat), BF16))]
        + [(half_spec, half_shape)] * (2 * mids),
        [],
    )
    far_level = [far] + [swap(far, "lvl", levels, step) for step in range(1, levels)]
    first = list(pays[:mids])
    first_in = [None] * mids
    first_in[1] = swap(first[1], "lvl", levels, 2)
    for step in range(1, levels):
        if step != 2:
            first_in[step - 1] = swap(first[step - 1], "lvl", levels, step)

    stat, stat_spec = shape((rows, LANES), F32), fixed((rows, LANES))
    half = shape((rows, flat // 2), F32)
    square = shape((GROUP, rows, rows), BF16)

    def group_tile(group):
        return pl.BlockSpec((rows, GROUP * width), lambda h: (0, group))

    def group_sources(group, arrays):
        return [(group_tile(group), array) for array in arrays]

    def whole(array):
        return (fixed(array.shape), array)

    def result(*dims):
        return (fixed(dims), shape(dims, F32))

    def near_call(group, arrays):
        return call(
            functools.partial(near_kernel, scale, parts, group),
            1,
            group_sources(group, arrays),
            [(stat_spec, stat)] * 2
            + [(fixed(square.shape), square)] * 2
            + [result(rows, flat)],
            [],
        )

    inputs = (queries, keys, values, grad_out)
    near_a = near_call(0, inputs)
    inputs, near_a = lax.optimization_barrier((inputs, near_a))
    near_b = near_call(1, inputs)
    far_level, near_b = lax.optimization_barrier((far_level, near_b))
    ring_bits = rings.bit_length() - 1
    col_shape = shape((block, 2 * flat), BF16)
    col_kv, col_qg, *ring_pays = call(
        functools.partial(column_kernel, levels, ring_bits),
        1,
        [(fixed(piece.shape), piece) for piece in far_level],
        [(fixed(col_shape.shape), col_shape)] * (2 + ring_bits),
        [],
        flops=4000000000,
    )
    far_ring = [None] * rings
    for step in range(2, rings, 2):
        far_ring[step] = swap(ring_pays[step.bit_length() - 1], "seq", rings, step)
    pieces = [ring_pays[0]] + far_ring[2::2]
    here = first_in[0][:16, :LANES] + first_in[1][:16, :LANES] + first_in[2][:16, :LANES]
    across = swap(join(pieces, swap(here, "seq", rings, 1)), "seq", rings, 1)

    col_spec = columns(block, GROUP * 2 * width)
    first_list = [(half_spec, piece) for piece in first_in]
    far_rest = [(col_spec, piece) for piece in far_ring[2::2]]
    across_spec = columns(across.shape[0], GROUP * 2 * width)
    far_rest.append((across_spec, across))
    far_kv, far_qg = [(col_spec, col_kv)] + far_rest, [(col_spec, col_qg)] + far_rest
    fars = len(far_kv)
    mid_own = [(mid_spec, kv), (mid_spec, qg)]
    own = mid_own + [(far_spec, far)]
    mid_stat, far_stat = result(mid_count, LANES), result(far_count, LANES)
    mid_stats = call(
        functools.partial(mid_stats_kernel, scale, levels, mids),
        steps,
        mid_own + first_list,
        [mid_stat] * 2 + [result(2 * GROUP, mid_count)] * mids,
        [],
    )
    backs = [swap(mid_stats[1 + step], "lvl", levels, step) for step in range(1, levels)]
    second = list(pays[mids:])
    mid_base, far_base, *far_stats = call(
        functools.partial(level_base_kernel, scale, levels, mids, fars),
        steps,
        own + [whole(array) for array in mid_stats[:2]] + first_list + far_kv,
        [
            (fixed((mid_count, flat)), shape((mid_count, flat), F32)),
            (columns(far_count, GROUP * 2 * width), shape((far_count, 2 * flat), F32)),
        ]
        + [far_stat] * 2,
        [],
    )
    level_stats = [*mid_stats[:2], *far_stats]
    second, backs, mid_base = lax.optimization_barrier((second, backs, mid_base))
    second_in = [swap(second[step - 1], "lvl", levels, step) for step in range(1, levels)]
    second_list = [(half_spec, piece) for piece in second_in]
    merged = call(
        functools.partial(merge_kernel, heads, mids),
        1,
        scalars + [whole(array) for array in [*near_a[:2], *near_b[:2], *level_stats, *backs]],
        [(stat_spec, stat)] * 2
        + [mid_stat] * 2
        + [far_stat] * 2
        + [mid_stat] * 2
        + [result(2 * heads, mid_count), result(2 * heads, far_count)],
        [],
    )
    mid_log, mid_dot, mid_sent, far_sent = merged[6:]
    near_sent = [far_sent] + [swap(far_sent, "seq", rings, step) for step in range(2, rings, 2)]

    def near_grads(group, near):
        far_spec = pl.BlockSpec((far_count, GROUP * 2 * width), lambda h: (0, group))
        return call(
            functools.partial(near_grads_kernel, parts, group),
            1,
            scalars
            + group_sources(group, (queries, grad_out))
            + [whole(array) for array in near[2:]]
            + [whole(array) for array in merged[:6]]
            + [whole(mid_base), (far_spec, far_base)],
            [result(rows, flat // 2)] * 3,
            [pltpu.VMEM((GROUP, rows, LANES), F32)],
        )

    grads_a = near_grads(0, near_a)
    near_sent, grads_a = lax.optimization_barrier((near_sent, grads_a))
    near_sent = pack(near_sent)
    other_sent = swap(near_sent, "seq", rings, 1)
    grads_b = near_grads(1, near_b)
    other_sent, grads_b = lax.optimization_barrier((other_sent, grads_b))
    sent = pack([mid_sent, near_sent, other_sent])
    sent_in = [sent] + [swap(sent, "lvl", levels, step) for step in range(1, levels)]
    out = shape((rows, flat), BF16)
    group_mid = pl.BlockSpec((mid_count, GROUP * 2 * width), lambda h: (0, 1))
    (grad_query,) = call(
        functools.partial(queries_kernel, scale, levels, mids),
        steps,
        scalars[:1]
        + [(group_mid, kv), (group_mid, qg)]
        + [whole(array) for array in (grads_a[0], grads_b[0], mid_log, mid_dot)]
        + second_list,
        [(tile, out)],
        [pltpu.VMEM((GROUP, rows, LANES), F32)],
    )
    sent_in, grad_query = lax.optimization_barrier((sent_in, grad_query))
    grad_key, grad_value = call(
        functools.partial(keys_kernel, scale, heads, levels, rings, mids, fars),
        steps,
        scalars
        + own
        + [whole(array) for array in (*grads_a[1:], *grads_b[1:])]
        + first_list
        + second_list
        + far_qg
        + [whole(piece) for piece in sent_in],
        [(tile, out)] * 2,
        [pltpu.VMEM((2 * heads, rows), F32)] * 2 + [pltpu.VMEM((2 * GROUP, rows, LANES), F32)],
    )
    return grad_query, grad_key, grad_value


def solution(mesh):
    row_spec = P(("seq", "lvl"), None)
    return jax.shard_map(
        local,
        mesh=mesh,
        in_specs=(row_spec, row_spec, row_spec, row_spec, P(), P()),
        out_specs=(row_spec, row_spec, row_spec),
        check_vma=False,
    )
```

```python
import functools

import jax
import jax.numpy as jnp
from jax import lax
from jax.experimental import pallas as pl
from jax.experimental.pallas import tpu as pltpu
from jax.sharding import PartitionSpec as P

F32 = jnp.float32
BF16 = jnp.bfloat16
LANES = 128
LOW = -1e30
MIB = 1024 * 1024
LIMIT = 22


def mm(a, b):
    return lax.dot_general(a, b, (((1,), (0,)), ((), ())), preferred_element_type=F32)


def mm_t(a, b):
    return lax.dot_general(a, b, (((1,), (1,)), ((), ())), preferred_element_type=F32)


def iota(shape, axis):
    return lax.broadcasted_iota(jnp.int32, shape, axis)


def params(limit):
    return pltpu.CompilerParams(
        vmem_limit_bytes=limit * MIB, dimension_semantics=("arbitrary",)
    )


def smem():
    return pl.BlockSpec(memory_space=pltpu.SMEM)


def columns(rows, width):
    return pl.BlockSpec((rows, width), lambda h: (0, h))


def fixed(shape):
    return pl.BlockSpec(shape, lambda h: (0,) * len(shape))


def pick_lane(ref, head):
    block = ref[...]
    return jnp.sum(jnp.where(iota(block.shape, 1) == head, block, 0.0), axis=1, keepdims=True)


def put_lane(ref, rows, head, value):
    block = ref[rows, :]
    ref[rows, :] = jnp.where(iota(block.shape, 1) == head, value, block)


def select_kernel(mid_off, far_off, q, k, v, g, kv, qg, far, *refs):
    per = q.shape[1] // LANES
    pays, work = refs[:-1], refs[-1]
    level = lax.axis_index("lvl")
    rows = q.shape[0]
    mid_count, far_count = kv.shape[0], far.shape[1]
    for at in range(per):
        head = pl.program_id(0) * per + at
        cut = slice(at * LANES, (at + 1) * LANES)
        mid_rows = pl.ds(mid_off[head], mid_count, stride=rows // mid_count)
        far_rows = pl.ds(far_off[head], far_count, stride=rows // far_count)
        for place, source in enumerate((k, v, q, g)):
            side, slot = divmod(place, 2)
            spot = 4 * at + place
            work[spot] = source[:, cut].astype(F32)
            wide = slice((2 * at + slot) * LANES, (2 * at + slot + 1) * LANES)
            (kv, qg)[side][:, wide] = work[spot, mid_rows, :].astype(BF16)
            far[side, :, wide] = work[spot, far_rows, :].astype(BF16)
    firsts, seconds = pays[: len(pays) // 2], pays[len(pays) // 2 :]
    for step, (first, second) in enumerate(zip(firsts, seconds), 1):
        upward = (level ^ step) > level

        @pl.when(upward & (pl.program_id(0) == 0))
        def _():
            first[...] = kv[...]

        @pl.when(upward & (pl.program_id(0) == 1))
        def _():
            second[...] = kv[...]

        @pl.when(jnp.logical_not(upward) & (pl.program_id(0) == 0))
        def _():
            second[...] = qg[...]

        @pl.when(jnp.logical_not(upward) & (pl.program_id(0) == 1))
        def _():
            first[...] = qg[...]


def near_kernel(scale, parts, q, k, v, g, stats, soft_out, slope_out, base, work):
    per = q.shape[1] // LANES
    work[...] = jnp.zeros_like(work)
    size = q.shape[0] // parts
    for at in range(per):
        cut = slice(at * LANES, (at + 1) * LANES)
        low, high = cuts(at)
        for part in range(parts):
            rows = slice(part * size, (part + 1) * size)
            width = (part + 1) * size
            scores = mm_t(q[rows, cut], k[:width, cut]) * scale
            grads = mm_t(g[rows, cut], v[:width, cut])
            seen = iota((size, width), 1) <= iota((size, width), 0) + part * size
            scores = jnp.where(seen, scores, LOW)
            peak = jnp.max(scores, axis=1, keepdims=True)
            weights = jnp.exp(scores - peak)
            total = jnp.sum(weights, axis=1, keepdims=True)
            soft = weights / total
            dot_part = jnp.sum(soft * grads, axis=1, keepdims=True)
            slopes = (soft * (grads - dot_part)).astype(BF16)
            soft = soft.astype(BF16)
            base[rows, low] = mm(slopes, k[:width, cut])
            base[rows, high] = mm(soft, k[:width, cut])
            soft_out[at, :width, rows] = soft.T
            slope_out[at, :width, rows] = slopes.T
            put_lane(work, rows, at, peak + jnp.log(total))
            put_lane(work, rows, per + at, dot_part)
    stats[...] = work[...].T[: 2 * per, :]


def row_stats(scores, grads):
    peak = jnp.max(scores, axis=1, keepdims=True)
    weights = jnp.exp(scores - peak)
    total = jnp.sum(weights, axis=1, keepdims=True)
    return peak + jnp.log(total), jnp.sum(weights * grads, axis=1, keepdims=True) / total


def mid_places(count, total, level):
    col = iota((count, total), 1)
    other = ((col >> (count.bit_length() - 1)) ^ level) * count + (col & (count - 1))
    return other, level * count + iota((count, total), 0)


def far_places(count, total, levels, level, ring):
    col = iota((count, total), 1)
    bits, level_bits = count.bit_length() - 1, levels.bit_length() - 1
    slot, ring_slot = (col >> bits) & (levels - 1), col >> (bits + level_bits)
    evens = total >> (bits + level_bits + 1)
    ring_slot = (ring_slot & (evens - 1)) * 2 + (ring_slot >> (evens.bit_length() - 1))
    other = ((ring_slot ^ ring) * levels + (slot ^ level)) * count + (col & (count - 1))
    return other, (ring * levels + level) * count + iota((count, total), 0)


def bias(seen):
    return jnp.where(seen, 0.0, LOW)


def stack(refs, cut):
    return jnp.concatenate([ref[:, cut] for ref in refs], axis=0)


def repeat_table(rows, count):
    return (iota((rows, count), 0) // (rows // count) == iota((rows, count), 1)).astype(F32)


def gather_table(rows, count):
    return (iota((count, rows), 1) // (rows // count) == iota((count, rows), 0)).astype(F32)


def column_kernel(levels, bits, *refs):
    pieces = refs[:levels]
    col_kv, col_qg = refs[levels : 2 + levels]
    pays = refs[2 + levels :]
    ring = lax.axis_index("seq")
    col_kv[...] = jnp.concatenate([piece[0] for piece in pieces], axis=0)
    col_qg[...] = jnp.concatenate([piece[1] for piece in pieces], axis=0)
    for bit in range(bits):
        upward = ((ring >> bit) & 1) == 0

        @pl.when(upward)
        def _():
            pays[bit][...] = col_kv[...]

        @pl.when(jnp.logical_not(upward))
        def _():
            pays[bit][...] = col_qg[...]


def cuts(at):
    low = slice(2 * at * LANES, (2 * at + 1) * LANES)
    return low, slice((2 * at + 1) * LANES, (2 * at + 2) * LANES)


def column_stats(scores, grads):
    peak = jnp.max(scores, axis=0, keepdims=True)
    weights = jnp.exp(scores - peak)
    total = jnp.sum(weights, axis=0, keepdims=True)
    return peak + jnp.log(total), jnp.sum(weights * grads, axis=0, keepdims=True) / total


def mid_stats_kernel(scale, levels, mids, *refs):
    per = refs[0].shape[1] // (2 * LANES)
    kv, qg = refs[:2]
    mid_in = refs[2 : 2 + mids]
    mlog, mdot = refs[2 + mids : 4 + mids]
    backs = refs[4 + mids :]
    step = pl.program_id(0)
    level = lax.axis_index("lvl")
    mid_count = kv.shape[0]
    every = slice(None)

    @pl.when(step == 0)
    def _():
        for ref in (mlog, mdot):
            ref[...] = jnp.zeros_like(ref)
        other, own = mid_places(mid_count, mid_count * levels, level)
        hide = bias(other <= own)
        for at in range(per):
            low, high = cuts(at)
            scores = mm_t(qg[:, low], stack((kv,) + mid_in, low)) * scale + hide
            grads = mm_t(qg[:, high], stack((kv,) + mid_in, high))
            log_part, dot_part = row_stats(scores, grads)
            put_lane(mlog, every, at, log_part)
            put_lane(mdot, every, at, dot_part)

    @pl.when(step == 1)
    def _():
        other, own = mid_places(mid_count, mid_count, level)
        hide = bias(other <= own)
        for at in range(per):
            low, high = cuts(at)
            scores = mm_t(qg[:, low], kv[:, low]) * scale + hide
            log_part, dot_part = row_stats(scores, mm_t(qg[:, high], kv[:, high]))
            put_lane(mlog, every, per + at, log_part)
            put_lane(mdot, every, per + at, dot_part)
            scores = mm_t(kv[:, low], stack(mid_in, low)) * scale
            log_part, dot_part = column_stats(scores, mm_t(kv[:, high], stack(mid_in, high)))
            for slot, back in enumerate(backs):
                where = slice(slot * mid_count, (slot + 1) * mid_count)
                back[at : at + 1, :] = log_part[:, where]
                back[per + at : per + at + 1, :] = dot_part[:, where]


def parts_of(block):
    high = block.astype(BF16)
    rest = block - high.astype(F32)
    middle = rest.astype(BF16)
    return jnp.concatenate([high, middle, (rest - middle.astype(F32)).astype(BF16)], axis=0)


def move(block, table):
    moved = mm(parts_of(block), table.astype(BF16))
    count = block.shape[0]
    return moved[:count] + moved[count : 2 * count] + moved[2 * count :]


def head_column(offsets, heads):
    row = iota((heads, 1), 0)
    values = jnp.zeros((heads, 1), jnp.int32)
    for head in range(heads):
        values = jnp.where(row == head, offsets[head], values)
    return values


def as_columns(blocks):
    height = sum(block.shape[0] for block in blocks)
    width = blocks[0].shape[1]
    fill = jnp.zeros((LANES - height, width), F32)
    whole = jnp.concatenate(blocks + [fill], axis=0)
    if width < LANES:
        whole = jnp.concatenate([whole, jnp.zeros((LANES, LANES - width), F32)], axis=1)
    return whole.T[:width, :]


def merge_kernel(heads, mids, *refs):
    per = heads // 2
    mid_off, far_off, rows_a, rows_b, mlog, mdot, flog, fdot = refs[:8]
    backs = refs[8 : 8 + mids]
    near_cols, mid_cols, far_cols, mid_sent, far_sent = refs[8 + mids :]
    level = lax.axis_index("lvl")
    rows, mid_count, far_count = rows_a.shape[1], mlog.shape[0], flog.shape[0]

    logs, dots = [mlog[...].T[:heads, :]], [mdot[...].T[:heads, :]]
    empty = jnp.zeros((heads - per, mid_count), F32)
    for slot, back in enumerate(backs, 1):
        hidden = jnp.where((slot ^ level) < level, 0.0, LOW)
        logs.append(jnp.concatenate([empty + LOW, back[:per, :] + hidden], axis=0))
        dots.append(jnp.concatenate([empty, back[per:, :]], axis=0))
    peak = functools.reduce(jnp.maximum, logs)
    weights = [jnp.exp(part - peak) for part in logs]
    whole = functools.reduce(jnp.add, weights)
    mid_logs = peak + jnp.log(whole)
    mid_dots = functools.reduce(jnp.add, [w * d for w, d in zip(weights, dots)]) / whole
    far_logs, far_dots = flog[...].T[:heads, :], fdot[...].T[:heads, :]

    lane = iota((heads, rows), 1)
    mid_here = (lane & (rows // mid_count - 1)) == head_column(mid_off, heads)
    far_here = (lane & (rows // far_count - 1)) == head_column(far_off, heads)
    mid_wide = move(jnp.concatenate([mid_logs, mid_dots], axis=0), gather_table(rows, mid_count))
    far_wide = move(jnp.concatenate([far_logs, far_dots], axis=0), gather_table(rows, far_count))
    near = jnp.concatenate([rows_a[:per, :], rows_b[:per, :]], axis=0)
    near_dots = jnp.concatenate([rows_a[per:, :], rows_b[per:, :]], axis=0)
    mid = jnp.where(mid_here, mid_wide[:heads], LOW)
    far = jnp.where(far_here, far_wide[:heads], LOW)
    peak = jnp.maximum(near, jnp.maximum(mid, far))
    near_part = jnp.exp(near - peak)
    mid, far = jnp.exp(mid - peak), jnp.exp(far - peak)
    whole = near_part + mid + far
    logs = peak + jnp.log(whole)
    dots = (near_part * near_dots + mid * mid_wide[heads:] + far * far_wide[heads:]) / whole
    near_cols[...] = as_columns([jnp.exp(near - logs), dots - near_dots])
    both = []
    for here, count in ((mid_here, mid_count), (far_here, far_count)):
        chosen = [jnp.where(here, logs, 0.0), jnp.where(here, dots, 0.0)]
        both.append(move(jnp.concatenate(chosen, axis=0), repeat_table(rows, count)))
    mid_sent[...], far_sent[...] = both
    log_rows, dot_rows = both[0][:heads], both[0][heads:]
    mid_cols[...] = as_columns(
        [jnp.exp(mid_logs - log_rows), dot_rows - mid_dots, log_rows, dot_rows]
    )
    log_rows, dot_rows = both[1][:heads], both[1][heads:]
    far_cols[...] = as_columns([jnp.exp(far_logs - log_rows), dot_rows - far_dots])


def row_side(scale, queries, cots, keys, vals, hide, logs, dots):
    scores = mm_t(queries, keys) * scale + hide
    soft = jnp.exp(scores - logs)
    slopes = soft * (mm_t(cots, vals) - dots)
    return soft.astype(BF16), slopes.astype(BF16)


def mid_queries(scale, levels, level, kv, qg, mid_in, mid_cols, at, head, heads):
    other, own = mid_places(kv.shape[0], kv.shape[0] * levels, level)
    low, high = cuts(at)
    keys, vals = stack((kv,) + mid_in, low), stack((kv,) + mid_in, high)
    logs, dots = pick_lane(mid_cols, 2 * heads + head), pick_lane(mid_cols, 3 * heads + head)
    hide = bias(other <= own)
    _, slopes = row_side(scale, qg[:, low], qg[:, high], keys, vals, hide, logs, dots)
    return mm(slopes, keys)


def key_side(scale, keys, vals, queries, cots, hide, stats, head, heads):
    logs, dots = stats[pl.ds(head, 1), :], stats[pl.ds(head + heads, 1), :]
    soft, slopes = row_side(scale, keys, vals, queries, cots, hide, logs, dots)
    return jnp.concatenate([mm(slopes, queries), mm(soft, cots)], axis=1)


def mid_keys(scale, levels, level, kv, qg, mid_in, stats, at, head, heads):
    other, own = mid_places(kv.shape[0], kv.shape[0] * levels, level)
    low, high = cuts(at)
    queries, cots = stack((qg,) + mid_in, low), stack((qg,) + mid_in, high)
    return key_side(
        scale, kv[:, low], kv[:, high], queries, cots, bias(other >= own), stats, head, heads
    )


def far_stats_kernel(scale, levels, total, fars, far_own, *refs):
    per = far_own.shape[2] // (2 * LANES)
    far_in = refs[:fars]
    far_base, flog, fdot = refs[fars:]
    step = pl.program_id(0)
    ring, level = lax.axis_index("seq"), lax.axis_index("lvl")
    every = slice(None)

    @pl.when(step == 0)
    def _():
        for ref in (flog, fdot):
            ref[...] = jnp.zeros_like(ref)

    other, own = far_places(far_own.shape[1], total, levels, level, ring)
    hide = bias(other <= own)
    for at in range(per):
        head = step * per + at
        low, high = cuts(at)
        keys = stack(far_in, low)
        scores = mm_t(far_own[1, :, low], keys) * scale + hide
        grads = mm_t(far_own[1, :, high], stack(far_in, high))
        peak = jnp.max(scores, axis=1, keepdims=True)
        weights = jnp.exp(scores - peak)
        whole = jnp.sum(weights, axis=1, keepdims=True)
        soft = weights / whole
        dots = jnp.sum(soft * grads, axis=1, keepdims=True)
        put_lane(flog, every, head, peak + jnp.log(whole))
        put_lane(fdot, every, head, dots)
        far_base[:, low] = mm((soft * (grads - dots)).astype(BF16), keys)
        far_base[:, high] = mm(soft.astype(BF16), keys)


def mid_base_kernel(scale, levels, mids, kv, qg, mlog, mdot, *refs):
    per = kv.shape[1] // (2 * LANES)
    mid_in, mid_base = refs[:mids], refs[mids]
    level = lax.axis_index("lvl")
    other, own = mid_places(kv.shape[0], kv.shape[0] * levels, level)
    hide = bias(other <= own)
    for at in range(per):
        low, high = cuts(at)
        keys, vals = stack((kv,) + mid_in, low), stack((kv,) + mid_in, high)
        logs, dots = pick_lane(mlog, at), pick_lane(mdot, at)
        soft, slopes = row_side(scale, qg[:, low], qg[:, high], keys, vals, hide, logs, dots)
        mid_base[:, low] = mm(slopes, keys)
        mid_base[:, high] = mm(soft, keys)


def far_raw_kernel(scale, levels, total, fars, far_own, *refs):
    per = far_own.shape[2] // (2 * LANES)
    far_in = refs[:fars]
    raw_scores, raw_grads = refs[fars:]
    ring, level = lax.axis_index("seq"), lax.axis_index("lvl")
    far_count = far_own.shape[1]
    other, own = far_places(far_count, total, levels, level, ring)
    hide = bias(other >= own)
    for at in range(per):
        low, high = cuts(at)
        rows = slice(at * far_count, (at + 1) * far_count)
        raw_scores[rows, :] = mm_t(far_own[0, :, low], stack(far_in, low)) * scale + hide
        raw_grads[rows, :] = mm_t(far_own[0, :, high], stack(far_in, high))


def put_rows(ref, at, offset, piece):
    count = piece.shape[0]
    rows = pl.ds(offset, count, stride=ref.shape[1] // count)
    ref[at, rows, :] += piece


def rescaled(base, at, cols, head, heads):
    low, high = cuts(at)
    factor, shift = pick_lane(cols, head), pick_lane(cols, heads + head)
    return factor * (base[:, low] - shift * base[:, high])


def near_grads_kernel(parts, group, heads, mid_off, far_off, q, g, soft_in, slope_in, base, *refs):
    per = q.shape[1] // LANES
    near_cols, mid_cols, far_cols = refs[:3]
    mid_base, far_base, out_q, out_k, out_v, work = refs[3:]
    rows = q.shape[0]
    size = rows // parts
    for at in range(per):
        head = group * per + at
        cut = slice(at * LANES, (at + 1) * LANES)
        low, high = cuts(at)
        factor, shift = pick_lane(near_cols, head), pick_lane(near_cols, heads + head)
        far = rescaled(far_base, at, far_cols, head, heads)
        work[at] = factor * (base[:, low] - shift * base[:, high])
        put_rows(work, at, far_off[head], far)
        if group == 0:
            mid = rescaled(mid_base, at, mid_cols, head, heads)
            put_rows(work, at, mid_off[head], mid)
        out_q[:, cut] = work[at]
        queries = factor * q[:, cut].astype(F32)
        shifted = (shift * queries).astype(BF16)
        queries = queries.astype(BF16)
        both = jnp.concatenate([(factor * g[:, cut].astype(F32)).astype(BF16), shifted], axis=1)
        for part in range(parts):
            keys = slice(part * size, (part + 1) * size)
            first = part * size
            value = mm(soft_in[at, keys, first:], both[first:])
            out_v[keys, cut] = value[:, :LANES]
            out_k[keys, cut] = mm(slope_in[at, keys, first:], queries[first:]) - value[:, LANES:]


def queries_kernel(scale, heads, levels, mids, *refs):
    per = heads // 2
    mid_off, kv, qg, dq_a, dq_b, mid_cols = refs[:6]
    mid_in, out_q, work = refs[6 : 6 + mids], refs[6 + mids], refs[7 + mids]
    level = lax.axis_index("lvl")

    @pl.when(pl.program_id(0) == 0)
    def _():
        out_q[...] = (dq_a[...] * scale).astype(BF16)

    @pl.when(pl.program_id(0) == 1)
    def _():
        for at in range(per):
            head = per + at
            cut = slice(at * LANES, (at + 1) * LANES)
            part = mid_queries(scale, levels, level, kv, qg, mid_in, mid_cols, at, head, heads)
            work[at] = dq_b[:, cut]
            put_rows(work, at, mid_off[head], part)
            out_q[:, cut] = (work[at] * scale).astype(BF16)


def keys_kernel(scale, heads, levels, rings, mids, seconds, fars, *refs):
    per = heads // 2
    mid_off, far_off, kv, qg, raw_scores, raw_grads, dk_a, dv_a, dk_b, dv_b = refs[:10]
    first_in, refs = refs[10 : 10 + mids], refs[10 + mids :]
    second_in, refs = refs[:seconds], refs[seconds:]
    far_in, refs = refs[:fars], refs[fars:]
    stats, refs = refs[: mids + 1], refs[mids + 1 :]
    out_k, out_v, mid_rows, far_rows, work = refs
    step = pl.program_id(0)
    level = lax.axis_index("lvl")
    mid_count, far_count = kv.shape[0], raw_scores.shape[0] // per

    @pl.when(step == 0)
    def _():
        mid_rows[...] = jnp.concatenate([ref[:, :mid_count] for ref in stats], axis=1)
        for slot in range(rings):
            source = mid_count + slot * far_count
            for low, ref in enumerate(stats):
                place = (slot * levels + low) * far_count
                far_rows[:, place : place + far_count] = ref[:, source : source + far_count]

    def finish(group, mid_in, dk, dv):
        for at in range(per):
            head = group * per + at
            cut = slice(at * LANES, (at + 1) * LANES)
            low, high = cuts(at)
            mid = mid_keys(scale, levels, level, kv, qg, mid_in, mid_rows, at, head, heads)
            queries, cots = stack(far_in, low), stack(far_in, high)
            rows = slice(at * far_count, (at + 1) * far_count)
            soft = jnp.exp(raw_scores[rows, :] - far_rows[pl.ds(head, 1), :])
            slopes = soft * (raw_grads[rows, :] - far_rows[pl.ds(head + heads, 1), :])
            far = [mm(slopes.astype(BF16), queries), mm(soft.astype(BF16), cots)]
            far = jnp.concatenate(far, axis=1)
            one, two = 2 * at, 2 * at + 1
            work[one], work[two] = dk[:, cut], dv[:, cut]
            for where, first in ((one, 0), (two, LANES)):
                put_rows(work, where, mid_off[head], mid[:, first : first + LANES])
                put_rows(work, where, far_off[head], far[:, first : first + LANES])
            out_k[:, cut] = (work[one] * scale).astype(BF16)
            out_v[:, cut] = work[two].astype(BF16)

    @pl.when(step == 0)
    def _():
        finish(0, second_in, dk_a, dv_a)

    @pl.when(step == 1)
    def _():
        finish(1, first_in, dk_b, dv_b)


def join_kernel(*refs):
    out, first = refs[-1], 0
    for ref in refs[:-2]:
        out[first : first + ref.shape[0], :] = ref[...]
        first += ref.shape[0]


def join(pieces, after):
    rows = sum(piece.shape[0] for piece in pieces)
    out = jax.ShapeDtypeStruct((rows, pieces[0].shape[1]), BF16)
    ins = [(fixed(piece.shape), piece) for piece in pieces + [after]]
    return call(join_kernel, 1, ins, [(fixed(out.shape), out)], [])[0]


def pack_kernel(*refs):
    out, first = refs[-1], 0
    for ref in refs[:-1]:
        out[:, first : first + ref.shape[1]] = ref[...]
        first += ref.shape[1]


def pack(pieces):
    width = sum(piece.shape[1] for piece in pieces)
    out = jax.ShapeDtypeStruct((pieces[0].shape[0], width), F32)
    ins = [(fixed(piece.shape), piece) for piece in pieces]
    return call(pack_kernel, 1, ins, [(fixed(out.shape), out)], [])[0]


def swap(array, axis, size, step):
    return lax.ppermute(array, axis, [(i, i ^ step) for i in range(size)])


def call(kernel, steps, ins, outs, scratch, limit=LIMIT, flops=0):
    specs, arrays = zip(*ins)
    out_specs, out_shapes = zip(*outs)
    return pl.pallas_call(
        kernel,
        grid=(steps,),
        in_specs=list(specs),
        out_specs=list(out_specs),
        out_shape=list(out_shapes),
        scratch_shapes=scratch,
        compiler_params=params(limit),
        cost_estimate=pl.CostEstimate(flops=flops, bytes_accessed=0, transcendentals=0),
    )(*arrays)


def local(queries, keys, values, grad_out, mid_offset, far_offset):
    rows, flat = queries.shape
    heads = mid_offset.shape[0]
    per = heads // 2
    width = flat // heads
    scale = width ** (-0.5)
    levels, rings = lax.axis_size("lvl"), lax.axis_size("seq")
    mid_count, far_count = rows // levels, rows // (levels * rings)
    block = far_count * levels
    shape = jax.ShapeDtypeStruct
    if width != LANES:
        raise ValueError("head width")
    parts = 2
    steps = heads // per
    tile = columns(rows, per * width)
    mid_spec = columns(mid_count, per * 2 * width)
    far_spec = pl.BlockSpec((2, far_count, per * 2 * width), lambda h: (0, 0, h))
    sources = [(tile, queries), (tile, keys), (tile, values), (tile, grad_out)]
    scalars = [(smem(), mid_offset), (smem(), far_offset)]
    mid_shape = shape((mid_count, 2 * flat), BF16)

    half_shape, half_spec = shape((mid_count, flat), BF16), fixed((mid_count, flat))
    mids = levels - 1

    kv, qg, far, *pays = call(
        select_kernel,
        steps,
        scalars + [(spec, pltpu.with_memory_space_constraint(x, pltpu.HBM)) for spec, x in sources],
        [(mid_spec, mid_shape)] * 2
        + [(far_spec, shape((2, far_count, 2 * flat), BF16))]
        + [(half_spec, half_shape)] * (2 * mids),
        [pltpu.VMEM((4 * per, rows, LANES), F32)],
    )
    far_level = [far] + [swap(far, "lvl", levels, step) for step in range(1, levels)]
    first = list(pays[:mids])
    first_in = [None] * mids
    first_in[1] = swap(first[1], "lvl", levels, 2)
    for step in range(1, levels):
        if step != 2:
            first_in[step - 1] = swap(first[step - 1], "lvl", levels, step)

    half = shape((rows, flat // 2), F32)
    square = shape((per, rows, rows), BF16)

    def group_tile(group):
        return pl.BlockSpec((rows, per * width), lambda h: (0, group))

    def group_sources(group, arrays):
        return [(group_tile(group), array) for array in arrays]

    def whole(array):
        return (fixed(array.shape), array)

    def result(*dims):
        return (fixed(dims), shape(dims, F32))

    def near_call(group, arrays):
        return call(
            functools.partial(near_kernel, scale, parts),
            1,
            group_sources(group, arrays),
            [result(2 * per, rows)]
            + [(fixed(square.shape), square)] * 2
            + [result(rows, flat)],
            [pltpu.VMEM((rows, LANES), F32)],
        )

    inputs = (queries, keys, values, grad_out)
    near_a = near_call(0, inputs)
    inputs, near_a = lax.optimization_barrier((inputs, near_a))
    near_b = near_call(1, inputs)
    far_level, near_b = lax.optimization_barrier((far_level, near_b))
    ring_bits = rings.bit_length() - 1
    col_shape = shape((block, 2 * flat), BF16)
    col_kv, col_qg, *ring_pays = call(
        functools.partial(column_kernel, levels, ring_bits),
        1,
        [(fixed(piece.shape), piece) for piece in far_level],
        [(fixed(col_shape.shape), col_shape)] * (2 + ring_bits),
        [],
        flops=4000000000,
    )
    far_ring = [None] * rings
    for step in range(2, rings, 2):
        far_ring[step] = swap(ring_pays[step.bit_length() - 1], "seq", rings, step)
    pieces = [ring_pays[0]] + far_ring[2::2]
    here = first_in[0][:16, :LANES] + first_in[1][:16, :LANES] + first_in[2][:16, :LANES]
    across = swap(join(pieces, swap(here, "seq", rings, 1)), "seq", rings, 1)

    col_spec = columns(block, per * 2 * width)
    first_list = [(half_spec, piece) for piece in first_in]
    far_rest = [(col_spec, piece) for piece in far_ring[2::2]]
    across_spec = columns(across.shape[0], per * 2 * width)
    far_rest.append((across_spec, across))
    far_kv, far_qg = [(col_spec, col_kv)] + far_rest, [(col_spec, col_qg)] + far_rest
    fars = len(far_kv)
    mid_own = [(mid_spec, kv), (mid_spec, qg)]
    own = mid_own + [(far_spec, far)]
    mid_stat, far_stat = result(mid_count, LANES), result(far_count, LANES)
    mid_stats = call(
        functools.partial(mid_stats_kernel, scale, levels, mids),
        steps,
        mid_own + first_list,
        [mid_stat] * 2 + [result(2 * per, mid_count)] * mids,
        [],
    )
    backs = [swap(mid_stats[1 + step], "lvl", levels, step) for step in range(1, levels)]
    second = list(pays[mids:])
    early, first_in = lax.optimization_barrier((second[1][: mid_count // 2], first_in))
    early = swap(early, "lvl", levels, 2)
    second[1] = second[1][mid_count // 2 :]
    far_base, *far_stats = call(
        functools.partial(far_stats_kernel, scale, levels, rows, fars),
        steps,
        own[2:] + far_kv,
        [(columns(far_count, per * 2 * width), shape((far_count, 2 * flat), F32))]
        + [far_stat] * 2,
        [],
    )
    level_stats = [*mid_stats[:2], *far_stats]
    group_rows = pl.BlockSpec((per * far_count, rows), lambda h: (h, 0))
    half_a = pl.BlockSpec((mid_count, per * 2 * width), lambda h: (0, 0))
    (mid_base,) = call(
        functools.partial(mid_base_kernel, scale, levels, mids),
        1,
        [(half_a, kv), (half_a, qg)]
        + [whole(array) for array in mid_stats[:2]]
        + [whole(piece) for piece in first_in],
        [result(mid_count, flat)],
        [],
    )
    raw_scores, raw_grads = call(
        functools.partial(far_raw_kernel, scale, levels, rows, fars),
        steps,
        own[2:] + far_qg,
        [(group_rows, shape((heads * far_count, rows), F32))] * 2,
        [],
    )
    waited = (second, backs, far_base, early)
    second, backs, far_base, early = lax.optimization_barrier(waited)
    second_in = [swap(second[step - 1], "lvl", levels, step) for step in range(1, levels)]
    second_in.insert(1, early)
    second_list = [whole(piece) for piece in second_in]
    near_cols, mid_cols, far_cols, mid_sent, far_sent = call(
        functools.partial(merge_kernel, heads, mids),
        1,
        scalars + [whole(array) for array in [near_a[0], near_b[0], *level_stats, *backs]],
        [result(rows, LANES), mid_stat, far_stat]
        + [result(2 * heads, mid_count), result(2 * heads, far_count)],
        [],
    )
    near_sent = [far_sent] + [swap(far_sent, "seq", rings, step) for step in range(2, rings, 2)]

    def near_grads(group, near):
        far_spec = pl.BlockSpec((far_count, per * 2 * width), lambda h: (0, group))
        return call(
            functools.partial(near_grads_kernel, parts, group, heads),
            1,
            scalars
            + group_sources(group, (queries, grad_out))
            + [whole(array) for array in near[1:]]
            + [whole(array) for array in (near_cols, mid_cols, far_cols)]
            + [whole(mid_base), (far_spec, far_base)],
            [result(rows, flat // 2)] * 3,
            [pltpu.VMEM((per, rows, LANES), F32)],
        )

    grads_a = near_grads(0, near_a)
    near_sent, grads_a = lax.optimization_barrier((near_sent, grads_a))
    near_sent = pack(near_sent)
    other_sent = swap(near_sent, "seq", rings, 1)
    grads_b = near_grads(1, near_b)
    other_sent, grads_b = lax.optimization_barrier((other_sent, grads_b))
    sent = pack([mid_sent, near_sent, other_sent])
    sent_in = [sent] + [swap(sent, "lvl", levels, step) for step in range(1, levels)]
    out = shape((rows, flat), BF16)
    group_mid = pl.BlockSpec((mid_count, per * 2 * width), lambda h: (0, 1))
    (grad_query,) = call(
        functools.partial(queries_kernel, scale, heads, levels, len(second_in)),
        steps,
        scalars[:1]
        + [(group_mid, kv), (group_mid, qg)]
        + [whole(array) for array in (grads_a[0], grads_b[0], mid_cols)]
        + second_list,
        [(tile, out)],
        [pltpu.VMEM((per, rows, LANES), F32)],
    )
    sent_in, grad_query = lax.optimization_barrier((sent_in, grad_query))
    grad_key, grad_value = call(
        functools.partial(keys_kernel, scale, heads, levels, rings, mids, len(second_in), fars),
        steps,
        scalars
        + mid_own
        + [(group_rows, array) for array in (raw_scores, raw_grads)]
        + [whole(array) for array in (*grads_a[1:], *grads_b[1:])]
        + first_list
        + second_list
        + far_qg
        + [whole(piece) for piece in sent_in],
        [(tile, out)] * 2,
        [pltpu.VMEM((2 * heads, rows), F32)] * 2 + [pltpu.VMEM((2 * per, rows, LANES), F32)],
    )
    return grad_query, grad_key, grad_value


def solution(mesh):
    row_spec = P(("seq", "lvl"), None)
    return jax.shard_map(
        local,
        mesh=mesh,
        in_specs=(row_spec, row_spec, row_spec, row_spec, P(), P()),
        out_specs=(row_spec, row_spec, row_spec),
        check_vma=False,
    )
```

```python
import functools

import jax
import jax.numpy as jnp
from jax import lax
from jax.experimental import pallas as pl
from jax.experimental.pallas import tpu as pltpu
from jax.sharding import PartitionSpec as P

F32 = jnp.float32
BF16 = jnp.bfloat16
LANES = 128
LOW = -1e30
MIB = 1024 * 1024
LIMIT = 22


def mm(a, b):
    return lax.dot_general(a, b, (((1,), (0,)), ((), ())), preferred_element_type=F32)


def mm_t(a, b):
    return lax.dot_general(a, b, (((1,), (1,)), ((), ())), preferred_element_type=F32)


def iota(shape, axis):
    return lax.broadcasted_iota(jnp.int32, shape, axis)


def params(limit):
    return pltpu.CompilerParams(
        vmem_limit_bytes=limit * MIB, dimension_semantics=("arbitrary",)
    )


def smem():
    return pl.BlockSpec(memory_space=pltpu.SMEM)


def columns(rows, width):
    return pl.BlockSpec((rows, width), lambda h: (0, h))


def fixed(shape):
    return pl.BlockSpec(shape, lambda h: (0,) * len(shape))


def pick_lane(ref, head):
    block = ref[...]
    return jnp.sum(jnp.where(iota(block.shape, 1) == head, block, 0.0), axis=1, keepdims=True)


def put_lane(ref, rows, head, value):
    block = ref[rows, :]
    ref[rows, :] = jnp.where(iota(block.shape, 1) == head, value, block)


def select_kernel(mid_off, far_off, q, k, v, g, kv, qg, far, *refs):
    per = q.shape[1] // LANES
    pays, work = refs[:-1], refs[-1]
    level = lax.axis_index("lvl")
    rows = q.shape[0]
    mid_count, far_count = kv.shape[0], far.shape[1]
    for at in range(per):
        head = pl.program_id(0) * per + at
        cut = slice(at * LANES, (at + 1) * LANES)
        mid_rows = pl.ds(mid_off[head], mid_count, stride=rows // mid_count)
        far_rows = pl.ds(far_off[head], far_count, stride=rows // far_count)
        for place, source in enumerate((k, v, q, g)):
            side, slot = divmod(place, 2)
            spot = 4 * at + place
            work[spot] = source[:, cut].astype(F32)
            wide = slice((2 * at + slot) * LANES, (2 * at + slot + 1) * LANES)
            (kv, qg)[side][:, wide] = work[spot, mid_rows, :].astype(BF16)
            far[side, :, wide] = work[spot, far_rows, :].astype(BF16)
    firsts, seconds = pays[: len(pays) // 2], pays[len(pays) // 2 :]
    for step, (first, second) in enumerate(zip(firsts, seconds), 1):
        upward = (level ^ step) > level

        @pl.when(upward & (pl.program_id(0) == 0))
        def _():
            first[...] = kv[...]

        @pl.when(upward & (pl.program_id(0) == 1))
        def _():
            second[...] = kv[...]

        @pl.when(jnp.logical_not(upward) & (pl.program_id(0) == 0))
        def _():
            second[...] = qg[...]

        @pl.when(jnp.logical_not(upward) & (pl.program_id(0) == 1))
        def _():
            first[...] = qg[...]


def near_kernel(scale, parts, q, k, v, g, stats, soft_out, slope_out, base, work):
    per = q.shape[1] // LANES
    work[...] = jnp.zeros_like(work)
    size = q.shape[0] // parts
    for at in range(per):
        cut = slice(at * LANES, (at + 1) * LANES)
        low, high = cuts(at)
        for part in range(parts):
            rows = slice(part * size, (part + 1) * size)
            width = (part + 1) * size
            scores = mm_t(q[rows, cut], k[:width, cut]) * scale
            grads = mm_t(g[rows, cut], v[:width, cut])
            seen = iota((size, width), 1) <= iota((size, width), 0) + part * size
            scores = jnp.where(seen, scores, LOW)
            peak = jnp.max(scores, axis=1, keepdims=True)
            weights = jnp.exp(scores - peak)
            total = jnp.sum(weights, axis=1, keepdims=True)
            soft = weights / total
            dot_part = jnp.sum(soft * grads, axis=1, keepdims=True)
            slopes = (soft * (grads - dot_part)).astype(BF16)
            soft = soft.astype(BF16)
            base[rows, low] = mm(slopes, k[:width, cut])
            base[rows, high] = mm(soft, k[:width, cut])
            soft_out[at, :width, rows] = soft.T
            slope_out[at, :width, rows] = slopes.T
            put_lane(work, rows, at, peak + jnp.log(total))
            put_lane(work, rows, per + at, dot_part)
    stats[...] = work[...].T[: 2 * per, :]


def row_stats(scores, grads):
    peak = jnp.max(scores, axis=1, keepdims=True)
    weights = jnp.exp(scores - peak)
    total = jnp.sum(weights, axis=1, keepdims=True)
    return peak + jnp.log(total), jnp.sum(weights * grads, axis=1, keepdims=True) / total


def mid_places(count, total, level):
    col = iota((count, total), 1)
    other = ((col >> (count.bit_length() - 1)) ^ level) * count + (col & (count - 1))
    return other, level * count + iota((count, total), 0)


def far_places(count, total, levels, level, ring):
    col = iota((count, total), 1)
    bits, level_bits = count.bit_length() - 1, levels.bit_length() - 1
    slot, ring_slot = (col >> bits) & (levels - 1), col >> (bits + level_bits)
    evens = total >> (bits + level_bits + 1)
    ring_slot = (ring_slot & (evens - 1)) * 2 + (ring_slot >> (evens.bit_length() - 1))
    other = ((ring_slot ^ ring) * levels + (slot ^ level)) * count + (col & (count - 1))
    return other, (ring * levels + level) * count + iota((count, total), 0)


def bias(seen):
    return jnp.where(seen, 0.0, LOW)


def stack(refs, cut):
    return jnp.concatenate([ref[:, cut] for ref in refs], axis=0)


def repeat_table(rows, count):
    return (iota((rows, count), 0) // (rows // count) == iota((rows, count), 1)).astype(F32)


def gather_table(rows, count):
    return (iota((count, rows), 1) // (rows // count) == iota((count, rows), 0)).astype(F32)


def column_kernel(levels, bits, *refs):
    pieces = refs[:levels]
    col_kv, col_qg = refs[levels : 2 + levels]
    pays = refs[2 + levels :]
    ring = lax.axis_index("seq")
    col_kv[...] = jnp.concatenate([piece[0] for piece in pieces], axis=0)
    col_qg[...] = jnp.concatenate([piece[1] for piece in pieces], axis=0)
    for bit in range(bits):
        upward = ((ring >> bit) & 1) == 0

        @pl.when(upward)
        def _():
            pays[bit][...] = col_kv[...]

        @pl.when(jnp.logical_not(upward))
        def _():
            pays[bit][...] = col_qg[...]


def cuts(at):
    low = slice(2 * at * LANES, (2 * at + 1) * LANES)
    return low, slice((2 * at + 1) * LANES, (2 * at + 2) * LANES)


def column_stats(scores, grads):
    peak = jnp.max(scores, axis=0, keepdims=True)
    weights = jnp.exp(scores - peak)
    total = jnp.sum(weights, axis=0, keepdims=True)
    return peak + jnp.log(total), jnp.sum(weights * grads, axis=0, keepdims=True) / total


def mid_stats_kernel(scale, levels, mids, *refs):
    per = refs[0].shape[1] // (2 * LANES)
    kv, qg = refs[:2]
    mid_in = refs[2 : 2 + mids]
    mlog, mdot = refs[2 + mids : 4 + mids]
    backs = refs[4 + mids :]
    step = pl.program_id(0)
    level = lax.axis_index("lvl")
    mid_count = kv.shape[0]
    every = slice(None)

    @pl.when(step == 0)
    def _():
        for ref in (mlog, mdot):
            ref[...] = jnp.zeros_like(ref)
        other, own = mid_places(mid_count, mid_count * levels, level)
        hide = bias(other <= own)
        for at in range(per):
            low, high = cuts(at)
            scores = mm_t(qg[:, low], stack((kv,) + mid_in, low)) * scale + hide
            grads = mm_t(qg[:, high], stack((kv,) + mid_in, high))
            log_part, dot_part = row_stats(scores, grads)
            put_lane(mlog, every, at, log_part)
            put_lane(mdot, every, at, dot_part)

    @pl.when(step == 1)
    def _():
        other, own = mid_places(mid_count, mid_count, level)
        hide = bias(other <= own)
        for at in range(per):
            low, high = cuts(at)
            scores = mm_t(qg[:, low], kv[:, low]) * scale + hide
            log_part, dot_part = row_stats(scores, mm_t(qg[:, high], kv[:, high]))
            put_lane(mlog, every, per + at, log_part)
            put_lane(mdot, every, per + at, dot_part)
            scores = mm_t(kv[:, low], stack(mid_in, low)) * scale
            log_part, dot_part = column_stats(scores, mm_t(kv[:, high], stack(mid_in, high)))
            for slot, back in enumerate(backs):
                where = slice(slot * mid_count, (slot + 1) * mid_count)
                back[at : at + 1, :] = log_part[:, where]
                back[per + at : per + at + 1, :] = dot_part[:, where]


def parts_of(block):
    high = block.astype(BF16)
    rest = block - high.astype(F32)
    middle = rest.astype(BF16)
    return jnp.concatenate([high, middle, (rest - middle.astype(F32)).astype(BF16)], axis=0)


def move(block, table):
    moved = mm(parts_of(block), table.astype(BF16))
    count = block.shape[0]
    return moved[:count] + moved[count : 2 * count] + moved[2 * count :]


def head_column(offsets, heads):
    row = iota((heads, 1), 0)
    values = jnp.zeros((heads, 1), jnp.int32)
    for head in range(heads):
        values = jnp.where(row == head, offsets[head], values)
    return values


def as_columns(blocks):
    height = sum(block.shape[0] for block in blocks)
    width = blocks[0].shape[1]
    fill = jnp.zeros((LANES - height, width), F32)
    whole = jnp.concatenate(blocks + [fill], axis=0)
    if width < LANES:
        whole = jnp.concatenate([whole, jnp.zeros((LANES, LANES - width), F32)], axis=1)
    return whole.T[:width, :]


def merge_kernel(heads, mids, *refs):
    per = heads // 2
    mid_off, far_off, rows_a, rows_b, mlog, mdot, flog, fdot = refs[:8]
    backs = refs[8 : 8 + mids]
    near_cols, mid_cols, far_cols, mid_sent, far_sent = refs[8 + mids :]
    level = lax.axis_index("lvl")
    rows, mid_count, far_count = rows_a.shape[1], mlog.shape[0], flog.shape[0]

    logs, dots = [mlog[...].T[:heads, :]], [mdot[...].T[:heads, :]]
    empty = jnp.zeros((heads - per, mid_count), F32)
    for slot, back in enumerate(backs, 1):
        hidden = jnp.where((slot ^ level) < level, 0.0, LOW)
        logs.append(jnp.concatenate([empty + LOW, back[:per, :] + hidden], axis=0))
        dots.append(jnp.concatenate([empty, back[per:, :]], axis=0))
    peak = functools.reduce(jnp.maximum, logs)
    weights = [jnp.exp(part - peak) for part in logs]
    whole = functools.reduce(jnp.add, weights)
    mid_logs = peak + jnp.log(whole)
    mid_dots = functools.reduce(jnp.add, [w * d for w, d in zip(weights, dots)]) / whole
    far_logs, far_dots = flog[...].T[:heads, :], fdot[...].T[:heads, :]

    lane = iota((heads, rows), 1)
    mid_here = (lane & (rows // mid_count - 1)) == head_column(mid_off, heads)
    far_here = (lane & (rows // far_count - 1)) == head_column(far_off, heads)
    mid_wide = move(jnp.concatenate([mid_logs, mid_dots], axis=0), gather_table(rows, mid_count))
    far_wide = move(jnp.concatenate([far_logs, far_dots], axis=0), gather_table(rows, far_count))
    near = jnp.concatenate([rows_a[:per, :], rows_b[:per, :]], axis=0)
    near_dots = jnp.concatenate([rows_a[per:, :], rows_b[per:, :]], axis=0)
    mid = jnp.where(mid_here, mid_wide[:heads], LOW)
    far = jnp.where(far_here, far_wide[:heads], LOW)
    peak = jnp.maximum(near, jnp.maximum(mid, far))
    near_part = jnp.exp(near - peak)
    mid, far = jnp.exp(mid - peak), jnp.exp(far - peak)
    whole = near_part + mid + far
    logs = peak + jnp.log(whole)
    dots = (near_part * near_dots + mid * mid_wide[heads:] + far * far_wide[heads:]) / whole
    near_cols[...] = as_columns([jnp.exp(near - logs), dots - near_dots])
    both = []
    for here, count in ((mid_here, mid_count), (far_here, far_count)):
        chosen = [jnp.where(here, logs, 0.0), jnp.where(here, dots, 0.0)]
        both.append(move(jnp.concatenate(chosen, axis=0), repeat_table(rows, count)))
    mid_sent[...], far_sent[...] = both
    log_rows, dot_rows = both[0][:heads], both[0][heads:]
    mid_cols[...] = as_columns(
        [jnp.exp(mid_logs - log_rows), dot_rows - mid_dots, log_rows, dot_rows]
    )
    log_rows, dot_rows = both[1][:heads], both[1][heads:]
    far_cols[...] = as_columns([jnp.exp(far_logs - log_rows), dot_rows - far_dots])


def row_side(scale, queries, cots, keys, vals, hide, logs, dots):
    scores = mm_t(queries, keys) * scale + hide
    soft = jnp.exp(scores - logs)
    slopes = soft * (mm_t(cots, vals) - dots)
    return soft.astype(BF16), slopes.astype(BF16)


def mid_queries(scale, levels, level, kv, qg, mid_in, mid_cols, at, head, heads):
    other, own = mid_places(kv.shape[0], kv.shape[0] * levels, level)
    low, high = cuts(at)
    keys, vals = stack((kv,) + mid_in, low), stack((kv,) + mid_in, high)
    logs, dots = pick_lane(mid_cols, 2 * heads + head), pick_lane(mid_cols, 3 * heads + head)
    hide = bias(other <= own)
    _, slopes = row_side(scale, qg[:, low], qg[:, high], keys, vals, hide, logs, dots)
    return mm(slopes, keys)


def key_side(scale, keys, vals, queries, cots, hide, stats, head, heads):
    logs, dots = stats[pl.ds(head, 1), :], stats[pl.ds(head + heads, 1), :]
    soft, slopes = row_side(scale, keys, vals, queries, cots, hide, logs, dots)
    return jnp.concatenate([mm(slopes, queries), mm(soft, cots)], axis=1)


def mid_keys(scale, levels, level, kv, qg, mid_in, stats, at, head, heads):
    other, own = mid_places(kv.shape[0], kv.shape[0] * levels, level)
    low, high = cuts(at)
    queries, cots = stack((qg,) + mid_in, low), stack((qg,) + mid_in, high)
    return key_side(
        scale, kv[:, low], kv[:, high], queries, cots, bias(other >= own), stats, head, heads
    )


def far_stats_kernel(scale, levels, total, fars, far_own, *refs):
    per = far_own.shape[2] // (2 * LANES)
    far_in = refs[:fars]
    far_base, flog, fdot = refs[fars:]
    step = pl.program_id(0)
    ring, level = lax.axis_index("seq"), lax.axis_index("lvl")
    every = slice(None)

    @pl.when(step == 0)
    def _():
        for ref in (flog, fdot):
            ref[...] = jnp.zeros_like(ref)

    other, own = far_places(far_own.shape[1], total, levels, level, ring)
    hide = bias(other <= own)
    for at in range(per):
        head = step * per + at
        low, high = cuts(at)
        keys = stack(far_in, low)
        scores = mm_t(far_own[1, :, low], keys) * scale + hide
        grads = mm_t(far_own[1, :, high], stack(far_in, high))
        peak = jnp.max(scores, axis=1, keepdims=True)
        weights = jnp.exp(scores - peak)
        whole = jnp.sum(weights, axis=1, keepdims=True)
        soft = weights / whole
        dots = jnp.sum(soft * grads, axis=1, keepdims=True)
        put_lane(flog, every, head, peak + jnp.log(whole))
        put_lane(fdot, every, head, dots)
        far_base[:, low] = mm((soft * (grads - dots)).astype(BF16), keys)
        far_base[:, high] = mm(soft.astype(BF16), keys)


def mid_base_kernel(scale, levels, mids, kv, qg, mlog, mdot, *refs):
    per = kv.shape[1] // (2 * LANES)
    mid_in, mid_base = refs[:mids], refs[mids]
    level = lax.axis_index("lvl")
    other, own = mid_places(kv.shape[0], kv.shape[0] * levels, level)
    hide = bias(other <= own)
    for at in range(per):
        low, high = cuts(at)
        keys, vals = stack((kv,) + mid_in, low), stack((kv,) + mid_in, high)
        logs, dots = pick_lane(mlog, at), pick_lane(mdot, at)
        soft, slopes = row_side(scale, qg[:, low], qg[:, high], keys, vals, hide, logs, dots)
        mid_base[:, low] = mm(slopes, keys)
        mid_base[:, high] = mm(soft, keys)


def far_raw_kernel(scale, levels, total, fars, far_own, *refs):
    per = far_own.shape[2] // (2 * LANES)
    far_in = refs[:fars]
    raw_scores, raw_grads = refs[fars:]
    ring, level = lax.axis_index("seq"), lax.axis_index("lvl")
    far_count = far_own.shape[1]
    other, own = far_places(far_count, total, levels, level, ring)
    hide = bias(other >= own)
    for at in range(per):
        low, high = cuts(at)
        rows = slice(at * far_count, (at + 1) * far_count)
        raw_scores[rows, :] = mm_t(far_own[0, :, low], stack(far_in, low)) * scale + hide
        raw_grads[rows, :] = mm_t(far_own[0, :, high], stack(far_in, high))


def put_rows(ref, at, offset, piece):
    count = piece.shape[0]
    rows = pl.ds(offset, count, stride=ref.shape[1] // count)
    ref[at, rows, :] += piece


def rescaled(base, at, cols, head, heads):
    low, high = cuts(at)
    factor, shift = pick_lane(cols, head), pick_lane(cols, heads + head)
    return factor * (base[:, low] - shift * base[:, high])


def near_grads_kernel(parts, group, heads, mid_off, far_off, q, g, soft_in, slope_in, base, *refs):
    per = q.shape[1] // LANES
    near_cols, mid_cols, far_cols = refs[:3]
    mid_base, far_base, out_q, out_k, out_v, work = refs[3:]
    rows = q.shape[0]
    size = rows // parts
    for at in range(per):
        head = group * per + at
        cut = slice(at * LANES, (at + 1) * LANES)
        low, high = cuts(at)
        factor, shift = pick_lane(near_cols, head), pick_lane(near_cols, heads + head)
        far = rescaled(far_base, at, far_cols, head, heads)
        work[at] = factor * (base[:, low] - shift * base[:, high])
        put_rows(work, at, far_off[head], far)
        if group == 0:
            mid = rescaled(mid_base, at, mid_cols, head, heads)
            put_rows(work, at, mid_off[head], mid)
        out_q[:, cut] = work[at]
        queries = factor * q[:, cut].astype(F32)
        shifted = (shift * queries).astype(BF16)
        queries = queries.astype(BF16)
        both = jnp.concatenate([(factor * g[:, cut].astype(F32)).astype(BF16), shifted], axis=1)
        for part in range(parts):
            keys = slice(part * size, (part + 1) * size)
            first = part * size
            value = mm(soft_in[at, keys, first:], both[first:])
            out_v[keys, cut] = value[:, :LANES]
            out_k[keys, cut] = mm(slope_in[at, keys, first:], queries[first:]) - value[:, LANES:]


def queries_kernel(scale, heads, levels, mids, *refs):
    per = heads // 2
    mid_off, kv, qg, dq_a, dq_b, mid_cols = refs[:6]
    mid_in, out_q, work = refs[6 : 6 + mids], refs[6 + mids], refs[7 + mids]
    level = lax.axis_index("lvl")

    @pl.when(pl.program_id(0) == 0)
    def _():
        out_q[...] = (dq_a[...] * scale).astype(BF16)

    @pl.when(pl.program_id(0) == 1)
    def _():
        for at in range(per):
            head = per + at
            cut = slice(at * LANES, (at + 1) * LANES)
            part = mid_queries(scale, levels, level, kv, qg, mid_in, mid_cols, at, head, heads)
            work[at] = dq_b[:, cut]
            put_rows(work, at, mid_off[head], part)
            out_q[:, cut] = (work[at] * scale).astype(BF16)


def keys_kernel(scale, heads, levels, rings, mids, seconds, fars, *refs):
    per = heads // 2
    mid_off, far_off, kv, qg, raw_scores, raw_grads, dk_a, dv_a, dk_b, dv_b = refs[:10]
    first_in, refs = refs[10 : 10 + mids], refs[10 + mids :]
    second_in, refs = refs[:seconds], refs[seconds:]
    far_in, refs = refs[:fars], refs[fars:]
    stats, refs = refs[: mids + 1], refs[mids + 1 :]
    out_k, out_v, mid_rows, far_rows, work = refs
    step = pl.program_id(0)
    level = lax.axis_index("lvl")
    mid_count, far_count = kv.shape[0], raw_scores.shape[0] // per

    @pl.when(step == 0)
    def _():
        mid_rows[...] = jnp.concatenate([ref[:, :mid_count] for ref in stats], axis=1)
        for slot in range(rings):
            source = mid_count + slot * far_count
            for low, ref in enumerate(stats):
                place = (slot * levels + low) * far_count
                far_rows[:, place : place + far_count] = ref[:, source : source + far_count]

    def finish(group, mid_in, dk, dv):
        for at in range(per):
            head = group * per + at
            cut = slice(at * LANES, (at + 1) * LANES)
            low, high = cuts(at)
            mid = mid_keys(scale, levels, level, kv, qg, mid_in, mid_rows, at, head, heads)
            queries, cots = stack(far_in, low), stack(far_in, high)
            rows = slice(at * far_count, (at + 1) * far_count)
            soft = jnp.exp(raw_scores[rows, :] - far_rows[pl.ds(head, 1), :])
            slopes = soft * (raw_grads[rows, :] - far_rows[pl.ds(head + heads, 1), :])
            far = [mm(slopes.astype(BF16), queries), mm(soft.astype(BF16), cots)]
            far = jnp.concatenate(far, axis=1)
            one, two = 2 * at, 2 * at + 1
            work[one], work[two] = dk[:, cut], dv[:, cut]
            for where, first in ((one, 0), (two, LANES)):
                put_rows(work, where, mid_off[head], mid[:, first : first + LANES])
                put_rows(work, where, far_off[head], far[:, first : first + LANES])
            out_k[:, cut] = (work[one] * scale).astype(BF16)
            out_v[:, cut] = work[two].astype(BF16)

    @pl.when(step == 0)
    def _():
        finish(0, second_in, dk_a, dv_a)

    @pl.when(step == 1)
    def _():
        finish(1, first_in, dk_b, dv_b)


def join_kernel(*refs):
    out, first = refs[-1], 0
    for ref in refs[:-2]:
        out[first : first + ref.shape[0], :] = ref[...]
        first += ref.shape[0]


def join(pieces, after):
    rows = sum(piece.shape[0] for piece in pieces)
    out = jax.ShapeDtypeStruct((rows, pieces[0].shape[1]), BF16)
    ins = [(fixed(piece.shape), piece) for piece in pieces + [after]]
    return call(join_kernel, 1, ins, [(fixed(out.shape), out)], [])[0]


def pack_kernel(*refs):
    out, first = refs[-1], 0
    for ref in refs[:-1]:
        out[:, first : first + ref.shape[1]] = ref[...]
        first += ref.shape[1]


def pack(pieces):
    width = sum(piece.shape[1] for piece in pieces)
    out = jax.ShapeDtypeStruct((pieces[0].shape[0], width), F32)
    ins = [(fixed(piece.shape), piece) for piece in pieces]
    return call(pack_kernel, 1, ins, [(fixed(out.shape), out)], [])[0]


def swap(array, axis, size, step):
    return lax.ppermute(array, axis, [(i, i ^ step) for i in range(size)])


def call(kernel, steps, ins, outs, scratch, limit=LIMIT, flops=0):
    specs, arrays = zip(*ins)
    out_specs, out_shapes = zip(*outs)
    return pl.pallas_call(
        kernel,
        grid=(steps,),
        in_specs=list(specs),
        out_specs=list(out_specs),
        out_shape=list(out_shapes),
        scratch_shapes=scratch,
        compiler_params=params(limit),
        cost_estimate=pl.CostEstimate(flops=flops, bytes_accessed=0, transcendentals=0),
    )(*arrays)


def local(queries, keys, values, grad_out, mid_offset, far_offset):
    rows, flat = queries.shape
    heads = mid_offset.shape[0]
    per = heads // 2
    width = flat // heads
    scale = width ** (-0.5)
    levels, rings = lax.axis_size("lvl"), lax.axis_size("seq")
    mid_count, far_count = rows // levels, rows // (levels * rings)
    block = far_count * levels
    shape = jax.ShapeDtypeStruct
    if width != LANES:
        raise ValueError("head width")
    parts = 2
    steps = heads // per
    tile = columns(rows, per * width)
    mid_spec = columns(mid_count, per * 2 * width)
    far_spec = pl.BlockSpec((2, far_count, per * 2 * width), lambda h: (0, 0, h))
    sources = [(tile, queries), (tile, keys), (tile, values), (tile, grad_out)]
    scalars = [(smem(), mid_offset), (smem(), far_offset)]
    mid_shape = shape((mid_count, 2 * flat), BF16)

    half_shape, half_spec = shape((mid_count, flat), BF16), fixed((mid_count, flat))
    mids = levels - 1

    kv, qg, far, *pays = call(
        select_kernel,
        steps,
        scalars + [(spec, pltpu.with_memory_space_constraint(x, pltpu.HBM)) for spec, x in sources],
        [(mid_spec, mid_shape)] * 2
        + [(far_spec, shape((2, far_count, 2 * flat), BF16))]
        + [(half_spec, half_shape)] * (2 * mids),
        [pltpu.VMEM((4 * per, rows, LANES), F32)],
    )
    far_level = [far] + [swap(far, "lvl", levels, step) for step in range(1, levels)]
    first = list(pays[:mids])
    first_in = [None] * mids
    first_in[1] = swap(first[1], "lvl", levels, 2)
    for step in range(1, levels):
        if step != 2:
            first_in[step - 1] = swap(first[step - 1], "lvl", levels, step)

    half = shape((rows, flat // 2), F32)
    square = shape((per, rows, rows), BF16)

    def group_tile(group):
        return pl.BlockSpec((rows, per * width), lambda h: (0, group))

    def group_sources(group, arrays):
        return [(group_tile(group), array) for array in arrays]

    def whole(array):
        return (fixed(array.shape), array)

    def result(*dims):
        return (fixed(dims), shape(dims, F32))

    def near_call(group, arrays):
        return call(
            functools.partial(near_kernel, scale, parts),
            1,
            group_sources(group, arrays),
            [result(2 * per, rows)]
            + [(fixed(square.shape), square)] * 2
            + [result(rows, flat)],
            [pltpu.VMEM((rows, LANES), F32)],
        )

    inputs = (queries, keys, values, grad_out)
    near_a = near_call(0, inputs)
    inputs, near_a = lax.optimization_barrier((inputs, near_a))
    near_b = near_call(1, inputs)
    far_level, near_b = lax.optimization_barrier((far_level, near_b))
    ring_bits = rings.bit_length() - 1
    col_shape = shape((block, 2 * flat), BF16)
    col_kv, col_qg, *ring_pays = call(
        functools.partial(column_kernel, levels, ring_bits),
        1,
        [(fixed(piece.shape), piece) for piece in far_level],
        [(fixed(col_shape.shape), col_shape)] * (2 + ring_bits),
        [],
        flops=4000000000,
    )
    far_ring = [None] * rings
    for step in range(2, rings, 2):
        far_ring[step] = swap(ring_pays[step.bit_length() - 1], "seq", rings, step)
    pieces = [ring_pays[0]] + far_ring[2::2]
    here = first_in[0][:16, :LANES] + first_in[1][:16, :LANES] + first_in[2][:16, :LANES]
    across = swap(join(pieces, swap(here, "seq", rings, 1)), "seq", rings, 1)

    col_spec = columns(block, per * 2 * width)
    first_list = [(half_spec, piece) for piece in first_in]
    far_rest = [(col_spec, piece) for piece in far_ring[2::2]]
    across_spec = columns(across.shape[0], per * 2 * width)
    far_rest.append((across_spec, across))
    far_kv, far_qg = [(col_spec, col_kv)] + far_rest, [(col_spec, col_qg)] + far_rest
    fars = len(far_kv)
    mid_own = [(mid_spec, kv), (mid_spec, qg)]
    own = mid_own + [(far_spec, far)]
    mid_stat, far_stat = result(mid_count, LANES), result(far_count, LANES)
    mid_stats = call(
        functools.partial(mid_stats_kernel, scale, levels, mids),
        steps,
        mid_own + first_list,
        [mid_stat] * 2 + [result(2 * per, mid_count)] * mids,
        [],
    )
    backs = [swap(mid_stats[1 + step], "lvl", levels, step) for step in range(1, levels)]
    second = list(pays[mids:])
    early, first_in = lax.optimization_barrier((second[1][: mid_count * 3 // 4], first_in))
    early = swap(early, "lvl", levels, 2)
    second[0], first_in = lax.optimization_barrier((second[0], first_in))
    nearest = swap(second[0], "lvl", levels, 1)
    second[1] = second[1][mid_count * 3 // 4 :]
    far_base, *far_stats = call(
        functools.partial(far_stats_kernel, scale, levels, rows, fars),
        steps,
        own[2:] + far_kv,
        [(columns(far_count, per * 2 * width), shape((far_count, 2 * flat), F32))]
        + [far_stat] * 2,
        [],
    )
    level_stats = [*mid_stats[:2], *far_stats]
    group_rows = pl.BlockSpec((per * far_count, rows), lambda h: (h, 0))
    half_a = pl.BlockSpec((mid_count, per * 2 * width), lambda h: (0, 0))
    (mid_base,) = call(
        functools.partial(mid_base_kernel, scale, levels, mids),
        1,
        [(half_a, kv), (half_a, qg)]
        + [whole(array) for array in mid_stats[:2]]
        + [whole(piece) for piece in first_in],
        [result(mid_count, flat)],
        [],
    )
    raw_scores, raw_grads = call(
        functools.partial(far_raw_kernel, scale, levels, rows, fars),
        steps,
        own[2:] + far_qg,
        [(group_rows, shape((heads * far_count, rows), F32))] * 2,
        [],
    )
    waited = (second[1:], backs, far_base, early, nearest)
    rest, backs, far_base, early, nearest = lax.optimization_barrier(waited)
    second_in = [swap(rest[step - 2], "lvl", levels, step) for step in range(2, levels)]
    second_in = [nearest, early] + second_in
    second_list = [whole(piece) for piece in second_in]
    near_cols, mid_cols, far_cols, mid_sent, far_sent = call(
        functools.partial(merge_kernel, heads, mids),
        1,
        scalars + [whole(array) for array in [near_a[0], near_b[0], *level_stats, *backs]],
        [result(rows, LANES), mid_stat, far_stat]
        + [result(2 * heads, mid_count), result(2 * heads, far_count)],
        [],
    )
    near_sent = [far_sent] + [swap(far_sent, "seq", rings, step) for step in range(2, rings, 2)]

    def near_grads(group, near):
        far_spec = pl.BlockSpec((far_count, per * 2 * width), lambda h: (0, group))
        return call(
            functools.partial(near_grads_kernel, parts, group, heads),
            1,
            scalars
            + group_sources(group, (queries, grad_out))
            + [whole(array) for array in near[1:]]
            + [whole(array) for array in (near_cols, mid_cols, far_cols)]
            + [whole(mid_base), (far_spec, far_base)],
            [result(rows, flat // 2)] * 3,
            [pltpu.VMEM((per, rows, LANES), F32)],
        )

    grads_a = near_grads(0, near_a)
    near_sent, grads_a = lax.optimization_barrier((near_sent, grads_a))
    near_sent = pack(near_sent)
    other_sent = swap(near_sent, "seq", rings, 1)
    grads_b = near_grads(1, near_b)
    other_sent, grads_b = lax.optimization_barrier((other_sent, grads_b))
    sent = pack([mid_sent, near_sent, other_sent])
    sent_in = [sent] + [swap(sent, "lvl", levels, step) for step in range(1, levels)]
    out = shape((rows, flat), BF16)
    group_mid = pl.BlockSpec((mid_count, per * 2 * width), lambda h: (0, 1))
    (grad_query,) = call(
        functools.partial(queries_kernel, scale, heads, levels, len(second_in)),
        steps,
        scalars[:1]
        + [(group_mid, kv), (group_mid, qg)]
        + [whole(array) for array in (grads_a[0], grads_b[0], mid_cols)]
        + second_list,
        [(tile, out)],
        [pltpu.VMEM((per, rows, LANES), F32)],
    )
    sent_in, grad_query = lax.optimization_barrier((sent_in, grad_query))
    grad_key, grad_value = call(
        functools.partial(keys_kernel, scale, heads, levels, rings, mids, len(second_in), fars),
        steps,
        scalars
        + mid_own
        + [(group_rows, array) for array in (raw_scores, raw_grads)]
        + [whole(array) for array in (*grads_a[1:], *grads_b[1:])]
        + first_list
        + second_list
        + far_qg
        + [whole(piece) for piece in sent_in],
        [(tile, out)] * 2,
        [pltpu.VMEM((2 * heads, rows), F32)] * 2 + [pltpu.VMEM((2 * per, rows, LANES), F32)],
    )
    return grad_query, grad_key, grad_value


def solution(mesh):
    row_spec = P(("seq", "lvl"), None)
    return jax.shard_map(
        local,
        mesh=mesh,
        in_specs=(row_spec, row_spec, row_spec, row_spec, P(), P()),
        out_specs=(row_spec, row_spec, row_spec),
        check_vma=False,
    )
```

```python
import functools

import jax
import jax.numpy as jnp
from jax import lax
from jax.experimental import pallas as pl
from jax.experimental.pallas import tpu as pltpu
from jax.sharding import PartitionSpec as P

F32 = jnp.float32
BF16 = jnp.bfloat16
LANES = 128
LOW = -1e30
MIB = 1024 * 1024
LIMIT = 22


def mm(a, b):
    return lax.dot_general(a, b, (((1,), (0,)), ((), ())), preferred_element_type=F32)


def mm_t(a, b):
    return lax.dot_general(a, b, (((1,), (1,)), ((), ())), preferred_element_type=F32)


def iota(shape, axis):
    return lax.broadcasted_iota(jnp.int32, shape, axis)


def params(limit):
    return pltpu.CompilerParams(
        vmem_limit_bytes=limit * MIB, dimension_semantics=("arbitrary",)
    )


def smem():
    return pl.BlockSpec(memory_space=pltpu.SMEM)


def columns(rows, width):
    return pl.BlockSpec((rows, width), lambda h: (0, h))


def fixed(shape):
    return pl.BlockSpec(shape, lambda h: (0,) * len(shape))


def pick_lane(ref, head):
    block = ref[...]
    return jnp.sum(jnp.where(iota(block.shape, 1) == head, block, 0.0), axis=1, keepdims=True)


def put_lane(ref, rows, head, value):
    block = ref[rows, :]
    ref[rows, :] = jnp.where(iota(block.shape, 1) == head, value, block)


def select_kernel(mid_off, far_off, q, k, v, g, kv, qg, far, *refs):
    per = q.shape[1] // LANES
    pays, work = refs[:-1], refs[-1]
    level = lax.axis_index("lvl")
    rows = q.shape[0]
    mid_count, far_count = kv.shape[0], far.shape[1]
    for at in range(per):
        head = pl.program_id(0) * per + at
        cut = slice(at * LANES, (at + 1) * LANES)
        mid_rows = pl.ds(mid_off[head], mid_count, stride=rows // mid_count)
        far_rows = pl.ds(far_off[head], far_count, stride=rows // far_count)
        for place, source in enumerate((k, v, q, g)):
            side, slot = divmod(place, 2)
            spot = 4 * at + place
            work[spot] = source[:, cut].astype(F32)
            wide = slice((2 * at + slot) * LANES, (2 * at + slot + 1) * LANES)
            (kv, qg)[side][:, wide] = work[spot, mid_rows, :].astype(BF16)
            far[side, :, wide] = work[spot, far_rows, :].astype(BF16)
    firsts, seconds = pays[: len(pays) // 2], pays[len(pays) // 2 :]
    for step, (first, second) in enumerate(zip(firsts, seconds), 1):
        upward = (level ^ step) > level

        @pl.when(upward & (pl.program_id(0) == 0))
        def _():
            first[...] = kv[...]

        @pl.when(upward & (pl.program_id(0) == 1))
        def _():
            second[...] = kv[...]

        @pl.when(jnp.logical_not(upward) & (pl.program_id(0) == 0))
        def _():
            second[...] = qg[...]

        @pl.when(jnp.logical_not(upward) & (pl.program_id(0) == 1))
        def _():
            first[...] = qg[...]


def near_kernel(scale, parts, q, k, v, g, stats, soft_out, slope_out, base, work):
    per = q.shape[1] // LANES
    work[...] = jnp.zeros_like(work)
    size = q.shape[0] // parts
    for at in range(per):
        cut = slice(at * LANES, (at + 1) * LANES)
        low, high = cuts(at)
        for part in range(parts):
            rows = slice(part * size, (part + 1) * size)
            width = (part + 1) * size
            scores = mm_t(q[rows, cut], k[:width, cut]) * scale
            grads = mm_t(g[rows, cut], v[:width, cut])
            seen = iota((size, width), 1) <= iota((size, width), 0) + part * size
            scores = jnp.where(seen, scores, LOW)
            peak = jnp.max(scores, axis=1, keepdims=True)
            weights = jnp.exp(scores - peak)
            total = jnp.sum(weights, axis=1, keepdims=True)
            soft = weights / total
            dot_part = jnp.sum(soft * grads, axis=1, keepdims=True)
            slopes = (soft * (grads - dot_part)).astype(BF16)
            soft = soft.astype(BF16)
            base[rows, low] = mm(slopes, k[:width, cut])
            base[rows, high] = mm(soft, k[:width, cut])
            soft_out[at, :width, rows] = soft.T
            slope_out[at, :width, rows] = slopes.T
            put_lane(work, rows, at, peak + jnp.log(total))
            put_lane(work, rows, per + at, dot_part)
    stats[...] = work[...].T[: 2 * per, :]


def row_stats(scores, grads):
    peak = jnp.max(scores, axis=1, keepdims=True)
    weights = jnp.exp(scores - peak)
    total = jnp.sum(weights, axis=1, keepdims=True)
    return peak + jnp.log(total), jnp.sum(weights * grads, axis=1, keepdims=True) / total


def mid_places(count, total, level):
    col = iota((count, total), 1)
    other = ((col >> (count.bit_length() - 1)) ^ level) * count + (col & (count - 1))
    return other, level * count + iota((count, total), 0)


def far_places(count, total, levels, level, ring):
    col = iota((count, total), 1)
    bits, level_bits = count.bit_length() - 1, levels.bit_length() - 1
    slot, ring_slot = (col >> bits) & (levels - 1), col >> (bits + level_bits)
    evens = total >> (bits + level_bits + 1)
    ring_slot = (ring_slot & (evens - 1)) * 2 + (ring_slot >> (evens.bit_length() - 1))
    other = ((ring_slot ^ ring) * levels + (slot ^ level)) * count + (col & (count - 1))
    return other, (ring * levels + level) * count + iota((count, total), 0)


def bias(seen):
    return jnp.where(seen, 0.0, LOW)


def stack(refs, cut):
    return jnp.concatenate([ref[:, cut] for ref in refs], axis=0)


def repeat_table(rows, count):
    return (iota((rows, count), 0) // (rows // count) == iota((rows, count), 1)).astype(F32)


def gather_table(rows, count):
    return (iota((count, rows), 1) // (rows // count) == iota((count, rows), 0)).astype(F32)


def column_kernel(levels, bits, *refs):
    pieces = refs[:levels]
    col_kv, col_qg = refs[levels : 2 + levels]
    pays = refs[2 + levels :]
    ring = lax.axis_index("seq")
    col_kv[...] = jnp.concatenate([piece[0] for piece in pieces], axis=0)
    col_qg[...] = jnp.concatenate([piece[1] for piece in pieces], axis=0)
    for bit in range(bits):
        upward = ((ring >> bit) & 1) == 0

        @pl.when(upward)
        def _():
            pays[bit][...] = col_kv[...]

        @pl.when(jnp.logical_not(upward))
        def _():
            pays[bit][...] = col_qg[...]


def cuts(at):
    low = slice(2 * at * LANES, (2 * at + 1) * LANES)
    return low, slice((2 * at + 1) * LANES, (2 * at + 2) * LANES)


def column_stats(scores, grads):
    peak = jnp.max(scores, axis=0, keepdims=True)
    weights = jnp.exp(scores - peak)
    total = jnp.sum(weights, axis=0, keepdims=True)
    return peak + jnp.log(total), jnp.sum(weights * grads, axis=0, keepdims=True) / total


def mid_stats_kernel(scale, levels, mids, *refs):
    per = refs[0].shape[1] // (2 * LANES)
    kv, qg = refs[:2]
    mid_in = refs[2 : 2 + mids]
    mlog, mdot = refs[2 + mids : 4 + mids]
    backs = refs[4 + mids :]
    step = pl.program_id(0)
    level = lax.axis_index("lvl")
    mid_count = kv.shape[0]
    every = slice(None)

    @pl.when(step == 0)
    def _():
        for ref in (mlog, mdot):
            ref[...] = jnp.zeros_like(ref)
        other, own = mid_places(mid_count, mid_count * levels, level)
        hide = bias(other <= own)
        for at in range(per):
            low, high = cuts(at)
            scores = mm_t(qg[:, low], stack((kv,) + mid_in, low)) * scale + hide
            grads = mm_t(qg[:, high], stack((kv,) + mid_in, high))
            log_part, dot_part = row_stats(scores, grads)
            put_lane(mlog, every, at, log_part)
            put_lane(mdot, every, at, dot_part)

    @pl.when(step == 1)
    def _():
        other, own = mid_places(mid_count, mid_count, level)
        hide = bias(other <= own)
        for at in range(per):
            low, high = cuts(at)
            scores = mm_t(qg[:, low], kv[:, low]) * scale + hide
            log_part, dot_part = row_stats(scores, mm_t(qg[:, high], kv[:, high]))
            put_lane(mlog, every, per + at, log_part)
            put_lane(mdot, every, per + at, dot_part)
            scores = mm_t(kv[:, low], stack(mid_in, low)) * scale
            log_part, dot_part = column_stats(scores, mm_t(kv[:, high], stack(mid_in, high)))
            for slot, back in enumerate(backs):
                where = slice(slot * mid_count, (slot + 1) * mid_count)
                back[at : at + 1, :] = log_part[:, where]
                back[per + at : per + at + 1, :] = dot_part[:, where]


def parts_of(block):
    high = block.astype(BF16)
    rest = block - high.astype(F32)
    middle = rest.astype(BF16)
    return jnp.concatenate([high, middle, (rest - middle.astype(F32)).astype(BF16)], axis=0)


def move(block, table):
    moved = mm(parts_of(block), table.astype(BF16))
    count = block.shape[0]
    return moved[:count] + moved[count : 2 * count] + moved[2 * count :]


def head_column(offsets, heads):
    row = iota((heads, 1), 0)
    values = jnp.zeros((heads, 1), jnp.int32)
    for head in range(heads):
        values = jnp.where(row == head, offsets[head], values)
    return values


def as_columns(blocks):
    height = sum(block.shape[0] for block in blocks)
    width = blocks[0].shape[1]
    fill = jnp.zeros((LANES - height, width), F32)
    whole = jnp.concatenate(blocks + [fill], axis=0)
    if width < LANES:
        whole = jnp.concatenate([whole, jnp.zeros((LANES, LANES - width), F32)], axis=1)
    return whole.T[:width, :]


def merge_kernel(heads, mids, *refs):
    per = heads // 2
    mid_off, far_off, rows_a, rows_b, mlog, mdot, flog, fdot = refs[:8]
    backs = refs[8 : 8 + mids]
    near_cols, mid_cols, far_cols, mid_sent, far_sent = refs[8 + mids :]
    level = lax.axis_index("lvl")
    rows, mid_count, far_count = rows_a.shape[1], mlog.shape[0], flog.shape[0]

    logs, dots = [mlog[...].T[:heads, :]], [mdot[...].T[:heads, :]]
    empty = jnp.zeros((heads - per, mid_count), F32)
    for slot, back in enumerate(backs, 1):
        hidden = jnp.where((slot ^ level) < level, 0.0, LOW)
        logs.append(jnp.concatenate([empty + LOW, back[:per, :] + hidden], axis=0))
        dots.append(jnp.concatenate([empty, back[per:, :]], axis=0))
    peak = functools.reduce(jnp.maximum, logs)
    weights = [jnp.exp(part - peak) for part in logs]
    whole = functools.reduce(jnp.add, weights)
    mid_logs = peak + jnp.log(whole)
    mid_dots = functools.reduce(jnp.add, [w * d for w, d in zip(weights, dots)]) / whole
    far_logs, far_dots = flog[...].T[:heads, :], fdot[...].T[:heads, :]

    lane = iota((heads, rows), 1)
    mid_here = (lane & (rows // mid_count - 1)) == head_column(mid_off, heads)
    far_here = (lane & (rows // far_count - 1)) == head_column(far_off, heads)
    mid_wide = move(jnp.concatenate([mid_logs, mid_dots], axis=0), gather_table(rows, mid_count))
    far_wide = move(jnp.concatenate([far_logs, far_dots], axis=0), gather_table(rows, far_count))
    near = jnp.concatenate([rows_a[:per, :], rows_b[:per, :]], axis=0)
    near_dots = jnp.concatenate([rows_a[per:, :], rows_b[per:, :]], axis=0)
    mid = jnp.where(mid_here, mid_wide[:heads], LOW)
    far = jnp.where(far_here, far_wide[:heads], LOW)
    peak = jnp.maximum(near, jnp.maximum(mid, far))
    near_part = jnp.exp(near - peak)
    mid, far = jnp.exp(mid - peak), jnp.exp(far - peak)
    whole = near_part + mid + far
    logs = peak + jnp.log(whole)
    dots = (near_part * near_dots + mid * mid_wide[heads:] + far * far_wide[heads:]) / whole
    near_cols[...] = as_columns([jnp.exp(near - logs), dots - near_dots])
    both = []
    for here, count in ((mid_here, mid_count), (far_here, far_count)):
        chosen = [jnp.where(here, logs, 0.0), jnp.where(here, dots, 0.0)]
        both.append(move(jnp.concatenate(chosen, axis=0), repeat_table(rows, count)))
    mid_sent[...], far_sent[...] = both
    log_rows, dot_rows = both[0][:heads], both[0][heads:]
    mid_cols[...] = as_columns(
        [jnp.exp(mid_logs - log_rows), dot_rows - mid_dots, log_rows, dot_rows]
    )
    log_rows, dot_rows = both[1][:heads], both[1][heads:]
    far_cols[...] = as_columns([jnp.exp(far_logs - log_rows), dot_rows - far_dots])


def row_side(scale, queries, cots, keys, vals, hide, logs, dots):
    scores = mm_t(queries, keys) * scale + hide
    soft = jnp.exp(scores - logs)
    slopes = soft * (mm_t(cots, vals) - dots)
    return soft.astype(BF16), slopes.astype(BF16)


def mid_queries(scale, levels, level, kv, qg, mid_in, mid_cols, at, head, heads):
    other, own = mid_places(kv.shape[0], kv.shape[0] * levels, level)
    low, high = cuts(at)
    keys, vals = stack((kv,) + mid_in, low), stack((kv,) + mid_in, high)
    logs, dots = pick_lane(mid_cols, 2 * heads + head), pick_lane(mid_cols, 3 * heads + head)
    hide = bias(other <= own)
    _, slopes = row_side(scale, qg[:, low], qg[:, high], keys, vals, hide, logs, dots)
    return mm(slopes, keys)


def key_side(scale, keys, vals, queries, cots, hide, stats, head, heads):
    logs, dots = stats[pl.ds(head, 1), :], stats[pl.ds(head + heads, 1), :]
    soft, slopes = row_side(scale, keys, vals, queries, cots, hide, logs, dots)
    return jnp.concatenate([mm(slopes, queries), mm(soft, cots)], axis=1)


def mid_keys(scale, levels, level, kv, qg, mid_in, stats, at, head, heads):
    other, own = mid_places(kv.shape[0], kv.shape[0] * levels, level)
    low, high = cuts(at)
    queries, cots = stack((qg,) + mid_in, low), stack((qg,) + mid_in, high)
    return key_side(
        scale, kv[:, low], kv[:, high], queries, cots, bias(other >= own), stats, head, heads
    )


def far_stats_kernel(scale, levels, total, fars, far_own, *refs):
    per = far_own.shape[2] // (2 * LANES)
    far_in = refs[:fars]
    far_base, flog, fdot = refs[fars:]
    step = pl.program_id(0)
    ring, level = lax.axis_index("seq"), lax.axis_index("lvl")
    every = slice(None)

    @pl.when(step == 0)
    def _():
        for ref in (flog, fdot):
            ref[...] = jnp.zeros_like(ref)

    other, own = far_places(far_own.shape[1], total, levels, level, ring)
    hide = bias(other <= own)
    for at in range(per):
        head = step * per + at
        low, high = cuts(at)
        keys = stack(far_in, low)
        scores = mm_t(far_own[1, :, low], keys) * scale + hide
        grads = mm_t(far_own[1, :, high], stack(far_in, high))
        peak = jnp.max(scores, axis=1, keepdims=True)
        weights = jnp.exp(scores - peak)
        whole = jnp.sum(weights, axis=1, keepdims=True)
        soft = weights / whole
        dots = jnp.sum(soft * grads, axis=1, keepdims=True)
        put_lane(flog, every, head, peak + jnp.log(whole))
        put_lane(fdot, every, head, dots)
        far_base[:, low] = mm((soft * (grads - dots)).astype(BF16), keys)
        far_base[:, high] = mm(soft.astype(BF16), keys)


def mid_base_kernel(scale, levels, mids, kv, qg, mlog, mdot, *refs):
    per = kv.shape[1] // (2 * LANES)
    mid_in, mid_base = refs[:mids], refs[mids]
    level = lax.axis_index("lvl")
    other, own = mid_places(kv.shape[0], kv.shape[0] * levels, level)
    hide = bias(other <= own)
    for at in range(per):
        low, high = cuts(at)
        keys, vals = stack((kv,) + mid_in, low), stack((kv,) + mid_in, high)
        logs, dots = pick_lane(mlog, at), pick_lane(mdot, at)
        soft, slopes = row_side(scale, qg[:, low], qg[:, high], keys, vals, hide, logs, dots)
        mid_base[:, low] = mm(slopes, keys)
        mid_base[:, high] = mm(soft, keys)


def far_raw_kernel(scale, levels, total, fars, far_own, *refs):
    per = far_own.shape[2] // (2 * LANES)
    far_in = refs[:fars]
    raw_scores, raw_grads = refs[fars:]
    ring, level = lax.axis_index("seq"), lax.axis_index("lvl")
    far_count = far_own.shape[1]
    other, own = far_places(far_count, total, levels, level, ring)
    hide = bias(other >= own)
    for at in range(per):
        low, high = cuts(at)
        rows = slice(at * far_count, (at + 1) * far_count)
        raw_scores[rows, :] = mm_t(far_own[0, :, low], stack(far_in, low)) * scale + hide
        raw_grads[rows, :] = mm_t(far_own[0, :, high], stack(far_in, high))


def put_rows(ref, at, offset, piece):
    count = piece.shape[0]
    rows = pl.ds(offset, count, stride=ref.shape[1] // count)
    ref[at, rows, :] += piece


def rescaled(base, at, cols, head, heads):
    low, high = cuts(at)
    factor, shift = pick_lane(cols, head), pick_lane(cols, heads + head)
    return factor * (base[:, low] - shift * base[:, high])


def near_grads_kernel(parts, group, heads, mid_off, far_off, q, g, soft_in, slope_in, base, *refs):
    per = q.shape[1] // LANES
    near_cols, mid_cols, far_cols = refs[:3]
    mid_base, far_base, out_q, out_k, out_v, work = refs[3:]
    rows = q.shape[0]
    size = rows // parts
    for at in range(per):
        head = group * per + at
        cut = slice(at * LANES, (at + 1) * LANES)
        low, high = cuts(at)
        factor, shift = pick_lane(near_cols, head), pick_lane(near_cols, heads + head)
        far = rescaled(far_base, at, far_cols, head, heads)
        work[at] = factor * (base[:, low] - shift * base[:, high])
        put_rows(work, at, far_off[head], far)
        if group == 0:
            mid = rescaled(mid_base, at, mid_cols, head, heads)
            put_rows(work, at, mid_off[head], mid)
        out_q[:, cut] = work[at]
        queries = factor * q[:, cut].astype(F32)
        shifted = (shift * queries).astype(BF16)
        queries = queries.astype(BF16)
        both = jnp.concatenate([(factor * g[:, cut].astype(F32)).astype(BF16), shifted], axis=1)
        for part in range(parts):
            keys = slice(part * size, (part + 1) * size)
            first = part * size
            value = mm(soft_in[at, keys, first:], both[first:])
            out_v[keys, cut] = value[:, :LANES]
            out_k[keys, cut] = mm(slope_in[at, keys, first:], queries[first:]) - value[:, LANES:]


def queries_kernel(scale, heads, levels, mids, *refs):
    per = heads // 2
    mid_off, kv, qg, dq_a, dq_b, mid_cols = refs[:6]
    mid_in, out_q, work = refs[6 : 6 + mids], refs[6 + mids], refs[7 + mids]
    level = lax.axis_index("lvl")

    @pl.when(pl.program_id(0) == 0)
    def _():
        out_q[...] = (dq_a[...] * scale).astype(BF16)

    @pl.when(pl.program_id(0) == 1)
    def _():
        for at in range(per):
            head = per + at
            cut = slice(at * LANES, (at + 1) * LANES)
            part = mid_queries(scale, levels, level, kv, qg, mid_in, mid_cols, at, head, heads)
            work[at] = dq_b[:, cut]
            put_rows(work, at, mid_off[head], part)
            out_q[:, cut] = (work[at] * scale).astype(BF16)


def keys_kernel(scale, heads, levels, rings, mids, seconds, fars, *refs):
    per = heads // 2
    mid_off, far_off, kv, qg, raw_scores, raw_grads, dk_a, dv_a, dk_b, dv_b = refs[:10]
    first_in, refs = refs[10 : 10 + mids], refs[10 + mids :]
    second_in, refs = refs[:seconds], refs[seconds:]
    far_in, refs = refs[:fars], refs[fars:]
    stats, refs = refs[: mids + 1], refs[mids + 1 :]
    out_k, out_v, mid_rows, far_rows, work = refs
    step = pl.program_id(0)
    level = lax.axis_index("lvl")
    mid_count, far_count = kv.shape[0], raw_scores.shape[0] // per

    @pl.when(step == 0)
    def _():
        mid_rows[...] = jnp.concatenate([ref[:, :mid_count] for ref in stats], axis=1)
        for slot in range(rings):
            source = mid_count + slot * far_count
            for low, ref in enumerate(stats):
                place = (slot * levels + low) * far_count
                far_rows[:, place : place + far_count] = ref[:, source : source + far_count]

    def finish(group, mid_in, dk, dv):
        for at in range(per):
            head = group * per + at
            cut = slice(at * LANES, (at + 1) * LANES)
            low, high = cuts(at)
            mid = mid_keys(scale, levels, level, kv, qg, mid_in, mid_rows, at, head, heads)
            queries, cots = stack(far_in, low), stack(far_in, high)
            rows = slice(at * far_count, (at + 1) * far_count)
            soft = jnp.exp(raw_scores[rows, :] - far_rows[pl.ds(head, 1), :])
            slopes = soft * (raw_grads[rows, :] - far_rows[pl.ds(head + heads, 1), :])
            far = [mm(slopes.astype(BF16), queries), mm(soft.astype(BF16), cots)]
            far = jnp.concatenate(far, axis=1)
            one, two = 2 * at, 2 * at + 1
            work[one], work[two] = dk[:, cut], dv[:, cut]
            for where, first in ((one, 0), (two, LANES)):
                put_rows(work, where, mid_off[head], mid[:, first : first + LANES])
                put_rows(work, where, far_off[head], far[:, first : first + LANES])
            out_k[:, cut] = (work[one] * scale).astype(BF16)
            out_v[:, cut] = work[two].astype(BF16)

    @pl.when(step == 0)
    def _():
        finish(0, second_in, dk_a, dv_a)

    @pl.when(step == 1)
    def _():
        finish(1, first_in, dk_b, dv_b)


def join_kernel(*refs):
    out, first = refs[-1], 0
    for ref in refs[:-2]:
        out[first : first + ref.shape[0], :] = ref[...]
        first += ref.shape[0]


def join(pieces, after):
    rows = sum(piece.shape[0] for piece in pieces)
    out = jax.ShapeDtypeStruct((rows, pieces[0].shape[1]), BF16)
    ins = [(fixed(piece.shape), piece) for piece in pieces + [after]]
    return call(join_kernel, 1, ins, [(fixed(out.shape), out)], [])[0]


def pack_kernel(*refs):
    out, first = refs[-1], 0
    for ref in refs[:-1]:
        out[:, first : first + ref.shape[1]] = ref[...]
        first += ref.shape[1]


def pack(pieces):
    width = sum(piece.shape[1] for piece in pieces)
    out = jax.ShapeDtypeStruct((pieces[0].shape[0], width), F32)
    ins = [(fixed(piece.shape), piece) for piece in pieces]
    return call(pack_kernel, 1, ins, [(fixed(out.shape), out)], [])[0]


def swap(array, axis, size, step):
    return lax.ppermute(array, axis, [(i, i ^ step) for i in range(size)])


def call(kernel, steps, ins, outs, scratch, limit=LIMIT, flops=0):
    specs, arrays = zip(*ins)
    out_specs, out_shapes = zip(*outs)
    return pl.pallas_call(
        kernel,
        grid=(steps,),
        in_specs=list(specs),
        out_specs=list(out_specs),
        out_shape=list(out_shapes),
        scratch_shapes=scratch,
        compiler_params=params(limit),
        cost_estimate=pl.CostEstimate(flops=flops, bytes_accessed=0, transcendentals=0),
    )(*arrays)


def local(queries, keys, values, grad_out, mid_offset, far_offset):
    rows, flat = queries.shape
    heads = mid_offset.shape[0]
    per = heads // 2
    width = flat // heads
    scale = width ** (-0.5)
    levels, rings = lax.axis_size("lvl"), lax.axis_size("seq")
    mid_count, far_count = rows // levels, rows // (levels * rings)
    block = far_count * levels
    shape = jax.ShapeDtypeStruct
    if width != LANES:
        raise ValueError("head width")
    parts = 2
    steps = heads // per
    tile = columns(rows, per * width)
    mid_spec = columns(mid_count, per * 2 * width)
    far_spec = pl.BlockSpec((2, far_count, per * 2 * width), lambda h: (0, 0, h))
    sources = [(tile, queries), (tile, keys), (tile, values), (tile, grad_out)]
    scalars = [(smem(), mid_offset), (smem(), far_offset)]
    mid_shape = shape((mid_count, 2 * flat), BF16)

    half_shape, half_spec = shape((mid_count, flat), BF16), fixed((mid_count, flat))
    mids = levels - 1

    kv, qg, far, *pays = call(
        select_kernel,
        steps,
        scalars + sources,
        [(mid_spec, mid_shape)] * 2
        + [(far_spec, shape((2, far_count, 2 * flat), BF16))]
        + [(half_spec, half_shape)] * (2 * mids),
        [pltpu.VMEM((4 * per, rows, LANES), F32)],
        60,
    )
    far_level = [far] + [swap(far, "lvl", levels, step) for step in range(1, levels)]
    first = list(pays[:mids])
    first_in = [None] * mids
    first_in[1] = swap(first[1], "lvl", levels, 2)
    for step in range(1, levels):
        if step != 2:
            first_in[step - 1] = swap(first[step - 1], "lvl", levels, step)

    half = shape((rows, flat // 2), F32)
    square = shape((per, rows, rows), BF16)

    def group_tile(group):
        return pl.BlockSpec((rows, per * width), lambda h: (0, group))

    def group_sources(group, arrays):
        return [(group_tile(group), array) for array in arrays]

    def whole(array):
        return (fixed(array.shape), array)

    def result(*dims):
        return (fixed(dims), shape(dims, F32))

    def near_call(group, arrays):
        return call(
            functools.partial(near_kernel, scale, parts),
            1,
            group_sources(group, arrays),
            [result(2 * per, rows)]
            + [(fixed(square.shape), square)] * 2
            + [result(rows, flat)],
            [pltpu.VMEM((rows, LANES), F32)],
        )

    inputs = (queries, keys, values, grad_out)
    near_a = near_call(0, inputs)
    inputs, near_a = lax.optimization_barrier((inputs, near_a))
    near_b = near_call(1, inputs)
    far_level, near_b = lax.optimization_barrier((far_level, near_b))
    ring_bits = rings.bit_length() - 1
    col_shape = shape((block, 2 * flat), BF16)
    col_kv, col_qg, *ring_pays = call(
        functools.partial(column_kernel, levels, ring_bits),
        1,
        [(fixed(piece.shape), piece) for piece in far_level],
        [(fixed(col_shape.shape), col_shape)] * (2 + ring_bits),
        [],
        flops=4000000000,
    )
    far_ring = [None] * rings
    for step in range(2, rings, 2):
        far_ring[step] = swap(ring_pays[step.bit_length() - 1], "seq", rings, step)
    pieces = [ring_pays[0]] + far_ring[2::2]
    here = first_in[0][:16, :LANES] + first_in[1][:16, :LANES] + first_in[2][:16, :LANES]
    across = swap(join(pieces, swap(here, "seq", rings, 1)), "seq", rings, 1)

    col_spec = columns(block, per * 2 * width)
    first_list = [(half_spec, piece) for piece in first_in]
    far_rest = [(col_spec, piece) for piece in far_ring[2::2]]
    across_spec = columns(across.shape[0], per * 2 * width)
    far_rest.append((across_spec, across))
    far_kv, far_qg = [(col_spec, col_kv)] + far_rest, [(col_spec, col_qg)] + far_rest
    fars = len(far_kv)
    mid_own = [(mid_spec, kv), (mid_spec, qg)]
    own = mid_own + [(far_spec, far)]
    mid_stat, far_stat = result(mid_count, LANES), result(far_count, LANES)
    mid_stats = call(
        functools.partial(mid_stats_kernel, scale, levels, mids),
        steps,
        mid_own + first_list,
        [mid_stat] * 2 + [result(2 * per, mid_count)] * mids,
        [],
    )
    backs = [swap(mid_stats[1 + step], "lvl", levels, step) for step in range(1, levels)]
    second = list(pays[mids:])
    early, first_in = lax.optimization_barrier((second[1][: mid_count * 3 // 4], first_in))
    early = swap(early, "lvl", levels, 2)
    second[0], first_in = lax.optimization_barrier((second[0], first_in))
    nearest = swap(second[0], "lvl", levels, 1)
    second[1] = second[1][mid_count * 3 // 4 :]
    far_base, *far_stats = call(
        functools.partial(far_stats_kernel, scale, levels, rows, fars),
        steps,
        own[2:] + far_kv,
        [(columns(far_count, per * 2 * width), shape((far_count, 2 * flat), F32))]
        + [far_stat] * 2,
        [],
    )
    level_stats = [*mid_stats[:2], *far_stats]
    group_rows = pl.BlockSpec((per * far_count, rows), lambda h: (h, 0))
    half_a = pl.BlockSpec((mid_count, per * 2 * width), lambda h: (0, 0))
    (mid_base,) = call(
        functools.partial(mid_base_kernel, scale, levels, mids),
        1,
        [(half_a, kv), (half_a, qg)]
        + [whole(array) for array in mid_stats[:2]]
        + [whole(piece) for piece in first_in],
        [result(mid_count, flat)],
        [],
    )
    raw_scores, raw_grads = call(
        functools.partial(far_raw_kernel, scale, levels, rows, fars),
        steps,
        own[2:] + far_qg,
        [(group_rows, shape((heads * far_count, rows), F32))] * 2,
        [],
    )
    waited = (second[1:], backs, far_base, early, nearest)
    rest, backs, far_base, early, nearest = lax.optimization_barrier(waited)
    second_in = [swap(rest[step - 2], "lvl", levels, step) for step in range(2, levels)]
    second_in = [nearest, early] + second_in
    second_list = [whole(piece) for piece in second_in]
    near_cols, mid_cols, far_cols, mid_sent, far_sent = call(
        functools.partial(merge_kernel, heads, mids),
        1,
        scalars + [whole(array) for array in [near_a[0], near_b[0], *level_stats, *backs]],
        [result(rows, LANES), mid_stat, far_stat]
        + [result(2 * heads, mid_count), result(2 * heads, far_count)],
        [],
    )
    near_sent = [far_sent] + [swap(far_sent, "seq", rings, step) for step in range(2, rings, 2)]

    def near_grads(group, near):
        far_spec = pl.BlockSpec((far_count, per * 2 * width), lambda h: (0, group))
        return call(
            functools.partial(near_grads_kernel, parts, group, heads),
            1,
            scalars
            + group_sources(group, (queries, grad_out))
            + [whole(array) for array in near[1:]]
            + [whole(array) for array in (near_cols, mid_cols, far_cols)]
            + [whole(mid_base), (far_spec, far_base)],
            [result(rows, flat // 2)] * 3,
            [pltpu.VMEM((per, rows, LANES), F32)],
        )

    grads_a = near_grads(0, near_a)
    near_sent, grads_a = lax.optimization_barrier((near_sent, grads_a))
    near_sent = pack(near_sent)
    other_sent = swap(near_sent, "seq", rings, 1)
    grads_b = near_grads(1, near_b)
    other_sent, grads_b = lax.optimization_barrier((other_sent, grads_b))
    sent = pack([mid_sent, near_sent, other_sent])
    sent_in = [sent] + [swap(sent, "lvl", levels, step) for step in range(1, levels)]
    out = shape((rows, flat), BF16)
    group_mid = pl.BlockSpec((mid_count, per * 2 * width), lambda h: (0, 1))
    (grad_query,) = call(
        functools.partial(queries_kernel, scale, heads, levels, len(second_in)),
        steps,
        scalars[:1]
        + [(group_mid, kv), (group_mid, qg)]
        + [whole(array) for array in (grads_a[0], grads_b[0], mid_cols)]
        + second_list,
        [(tile, out)],
        [pltpu.VMEM((per, rows, LANES), F32)],
    )
    sent_in, grad_query = lax.optimization_barrier((sent_in, grad_query))
    grad_key, grad_value = call(
        functools.partial(keys_kernel, scale, heads, levels, rings, mids, len(second_in), fars),
        steps,
        scalars
        + mid_own
        + [(group_rows, array) for array in (raw_scores, raw_grads)]
        + [whole(array) for array in (*grads_a[1:], *grads_b[1:])]
        + first_list
        + second_list
        + far_qg
        + [whole(piece) for piece in sent_in],
        [(tile, out)] * 2,
        [pltpu.VMEM((2 * heads, rows), F32)] * 2 + [pltpu.VMEM((2 * per, rows, LANES), F32)],
    )
    return grad_query, grad_key, grad_value


def solution(mesh):
    row_spec = P(("seq", "lvl"), None)
    return jax.shard_map(
        local,
        mesh=mesh,
        in_specs=(row_spec, row_spec, row_spec, row_spec, P(), P()),
        out_specs=(row_spec, row_spec, row_spec),
        check_vma=False,
    )
```
